128 devices in a mesh: row: 8 (over y, z_hi), col: 16 (over x, z_lo, core).
Axes of the slice: x: 4, y: 4, z: 4 (z_hi: 2, z_lo: 2; z = z_hi * 2 + z_lo), core: 2. Of those that a mesh axis runs over, the one named last changes fastest.
Arguments:
- parent_front: bfloat16 [28672, 28672], P('row', 'col'), may hold values from -6 to 6
- child_update: bfloat16 [2, 14336, 14336], P(None, 'row', 'col'), may hold values from -6 to 6
- parent_test: bfloat16 [28672, 448], P('col'), may hold values from -0.03125 to 0.03125
- child_test: bfloat16 [2, 14336, 448], P(None, 'col'), may hold values from -0.046875 to 0.046875
- child_map: int32 [2, 112], replicated, may hold values from 0 to 223, as said below
Outputs:
- leaf_basis: bfloat16 [224, 128, 448], P('row', 'col')
- couplings: float32 [32, 448, 448], P('row', 'col')
The draws below stay inside these ranges and needn't reach their ends.
Inputs may be any that keep to these rules, and one draw needn't show every extreme that they name: `child_map`: for each child the entries rise strictly along its blocks, and entry j is at least j.
All inputs are finite; a program needn't handle non-finite values.
Results may differ from the reference program's by a relative error of at most 0.006.
Values may be sent and summed in bfloat16 or wider, within the bound.
No kernel may reach another device: no remote copies, remote signals or barrier semaphores. Data moves between devices by JAX's collectives and lax.ppermute only.
A program may use at most 192 MiB of HBM per device.

```python
import math
import jax
import jax.numpy as jnp
from jax import lax

M = 14336
R = 448
LEAF = 896
BLOCK = 128
P_SIZE = 28672


def draw_child_map(key, part):
    blocks = M // BLOCK
    half = blocks // 2
    positions = jnp.arange(blocks, dtype=jnp.int32)
    first_key = jax.random.fold_in(key, 11)
    level = jax.random.randint(jax.random.fold_in(first_key, 1), (), 1, 4)
    draws = jax.random.randint(jax.random.fold_in(first_key, 2), (blocks,), 0, 4)
    steps_up = (draws < level).astype(jnp.int32)
    first = positions + jnp.cumsum(steps_up).astype(jnp.int32)
    second_key = jax.random.fold_in(key, 12)
    gaps = jax.random.randint(jax.random.fold_in(second_key, 2), (blocks,), 0, 2)
    gaps = jnp.where(positions < half, gaps, 0).astype(jnp.int32)
    later = jnp.cumsum(gaps[::-1])[::-1].astype(jnp.int32) - gaps
    second = positions + blocks - later
    return jnp.stack([first, second]).astype(jnp.int32)


def level_of(own_key, dims, split, low, high):
    factor_of = 1.0
    for axis_at, blocks in split:
        heights = jax.random.uniform(jax.random.fold_in(jax.random.fold_in(own_key, 6), axis_at), (blocks,), jnp.float32, low / len(split), high / len(split))
        factor_of = factor_of * jnp.repeat(jnp.exp(heights), dims[axis_at] // blocks).reshape((-1,) + (1,) * (len(dims) - 1 - axis_at))
    return factor_of


def scatter_about(key, extent, spread, most, pieces=(), kind=jnp.bfloat16):
    drawn = jax.random.normal(key, extent, jnp.float32) * spread
    if len(pieces) > 0:
        drawn = level_of(key, extent, pieces, -0.22, 0.18) * drawn
    return jnp.clip(drawn, min=-most, max=most).astype(kind)


def setup_inputs(seed: int = 0) -> dict:
    keys = jax.random.split(jax.random.key(seed), 6)
    parent_front = scatter_about(keys[0], (P_SIZE, P_SIZE), 1.0, 6.0, ((0, 8), (1, 16)))
    child_update = scatter_about(keys[1], (2, M, M), 1.0, 6.0, ((1, 8), (2, 16)))
    parent_test = scatter_about(keys[2], (P_SIZE, R), P_SIZE ** -0.5, 0.03125, ((0, 16),))
    child_test = scatter_about(keys[3], (2, M, R), M ** -0.5, 0.046875, ((1, 16),))
    child_map = draw_child_map(jax.random.fold_in(keys[5], 71), 0)
    return {"parent_front": parent_front, "child_update": child_update, "parent_test": parent_test, "child_test": child_test, "child_map": child_map}


HIGH = lax.Precision.HIGHEST

def orthonormal(leaves):
    gram_matrix = jnp.einsum('lkr,lks->lrs', leaves, leaves, precision=HIGH)
    factor = jnp.linalg.cholesky(gram_matrix)
    solved = lax.linalg.triangular_solve(factor, leaves, left_side=False, lower=True, transpose_a=True)
    return (solved * math.sqrt(LEAF)).astype(jnp.bfloat16)

def reference(parent_front, child_update, parent_test, child_test, child_map):
    sample = jnp.dot(parent_front.astype(jnp.float32), parent_test.astype(jnp.float32), preferred_element_type=jnp.float32)
    sample = sample.reshape(2 * M // BLOCK, BLOCK, R)
    for which in range(2):
        probed = jnp.dot(child_update[which].astype(jnp.float32), child_test[which].astype(jnp.float32), preferred_element_type=jnp.float32)
        sample = sample.at[child_map[which]].add(probed.reshape(M // BLOCK, BLOCK, R))
    leaves = sample.reshape(2 * M // LEAF, LEAF, R)
    bases = orthonormal(leaves)
    shrink = 1.0 / math.sqrt(LEAF)

    def coupling(leaf_index):
        sibling = jnp.bitwise_xor(leaf_index, 1)
        front_tile = lax.dynamic_slice(parent_front, (leaf_index * LEAF, sibling * LEAF), (LEAF, LEAF))
        product = (jnp.dot(front_tile.astype(jnp.float32), bases[sibling].astype(jnp.float32), preferred_element_type=jnp.float32) * shrink).astype(jnp.bfloat16)
        return jnp.dot(bases[leaf_index].T.astype(jnp.float32), product.astype(jnp.float32), preferred_element_type=jnp.float32) * shrink
    couplings = lax.map(coupling, jnp.arange(2 * M // LEAF, dtype=jnp.int32))
    return (bases.reshape(2 * M // BLOCK, BLOCK, R), couplings)
```

```python
import functools
import math

import jax
import jax.numpy as jnp
from jax import lax
from jax.experimental import pallas as pl
from jax.experimental.pallas import tpu as pltpu
from jax.sharding import Mesh
from jax.sharding import PartitionSpec as P

LEAF = 896
BLOCK = 128
ROW = ("y", "zh")
CHIP = ("x", "zl")
COL = ("x", "zl", "core")
F32 = jnp.float32
BF = jnp.bfloat16
HIGH = lax.Precision.HIGHEST
VMEM = pl.BlockSpec(memory_space=pltpu.VMEM)
STEP = 64


def params(mib):
    return pltpu.CompilerParams(vmem_limit_bytes=mib << 20)


def cost(flops, nbytes):
    return pl.CostEstimate(flops=int(flops), bytes_accessed=int(nbytes), transcendentals=0)


def send_kernel(a_ref, b_ref, o_ref):
    o_ref[...] = jnp.dot(a_ref[0], b_ref[0], preferred_element_type=F32)[None]


def keep_kernel(a_ref, b_ref, r_ref, o_ref):
    total = jnp.dot(a_ref[0], b_ref[0], preferred_element_type=F32) + r_ref[0]
    chips, blocks, rows, _ = o_ref.shape
    for block in range(blocks):
        for chip in range(chips):
            start = (block * chips + chip) * rows
            o_ref[chip, block] = total[start : start + rows].astype(BF)


def probe_send(a, b):
    count, rows, depth = a.shape
    half = b.shape[2]
    per = rows // LEAF
    return pl.pallas_call(
        send_kernel,
        grid=(count, per),
        out_shape=jax.ShapeDtypeStruct((count, rows, half), F32),
        in_specs=[
            pl.BlockSpec((1, LEAF, depth), lambda k, i: (k, i, 0)),
            pl.BlockSpec((1, depth, half), lambda k, i: (k, 0, 0)),
        ],
        out_specs=pl.BlockSpec((1, LEAF, half), lambda k, i: (k, i, 0)),
        compiler_params=params(40),
        cost_estimate=cost(2 * count * rows * depth * half, 2 * a.size + 4 * count * rows * half),
    )(a, b)


def probe_keep(a, b, received, chips):
    count, rows, depth = a.shape
    half = b.shape[2]
    per = rows // LEAF
    blocks = LEAF // BLOCK
    slab = BLOCK // chips
    return pl.pallas_call(
        keep_kernel,
        grid=(count, per),
        out_shape=jax.ShapeDtypeStruct((chips, count * rows // BLOCK, slab, half), BF),
        in_specs=[
            pl.BlockSpec((1, LEAF, depth), lambda k, i: (k, i, 0)),
            pl.BlockSpec((1, depth, half), lambda k, i: (k, 0, 0)),
            pl.BlockSpec((1, LEAF, half), lambda k, i: (k, i, 0)),
        ],
        out_specs=pl.BlockSpec((chips, blocks, slab, half), lambda k, i: (0, k * per + i, 0, 0)),
        compiler_params=params(40),
        cost_estimate=cost(2 * count * rows * depth * half, 2 * a.size + 6 * count * rows * half),
    )(a, b, received)


def shift(value, axis, by):
    size = lax.axis_size(axis)
    return lax.ppermute(value, axis, [(i, (i + by) % size) for i in range(size)])


def ring_gather(value, axis):
    size = lax.axis_size(axis)
    return jnp.stack([value] + [shift(value, axis, by) for by in range(1, size)])


def two_way_gather(first, second, big, small):
    first_ring = ring_gather(first, big)
    second_pair = ring_gather(second, small)
    return ring_gather(first_ring, small), ring_gather(second_pair, big)


def sum_kernel(k_ref, o_ref):
    total = k_ref[0].astype(F32)
    for chip in range(1, k_ref.shape[0]):
        total += k_ref[chip].astype(F32)
    o_ref[...] = total.astype(o_ref.dtype)


def sum_shares(shares, dtype):
    return pl.pallas_call(
        sum_kernel,
        out_shape=jax.ShapeDtypeStruct(shares.shape[1:], dtype),
        in_specs=[VMEM],
        out_specs=VMEM,
        compiler_params=params(24),
        cost_estimate=cost(shares.size, 2 * shares.size),
    )(shares)


def extend_kernel(at_ref, p_ref, first_ref, second_ref, o_ref):
    for block in range(p_ref.shape[1]):
        total = p_ref[0, block].astype(F32)
        for chip in range(1, p_ref.shape[0]):
            total += p_ref[chip, block].astype(F32)
        for kid, ref in enumerate((first_ref, second_ref)):
            near, far, place = (at_ref[kid, part, block] for part in range(3))
            there = at_ref[kid, 3, block]
            share = ref[near, far, place].astype(F32)
            total += jnp.where(there > 0, share, 0.0)
        o_ref[block] = total.astype(BF)


def extend_add(at, parent, first, second):
    return pl.pallas_call(
        extend_kernel,
        out_shape=jax.ShapeDtypeStruct(parent.shape[1:], BF),
        in_specs=[pl.BlockSpec(memory_space=pltpu.SMEM), VMEM, VMEM, VMEM],
        out_specs=VMEM,
        compiler_params=params(32),
        cost_estimate=cost(parent.size, 6 * parent.size),
    )(at, parent, first, second)


def halves(x):
    hi = x.astype(BF)
    return hi, (x - hi.astype(F32)).astype(BF)


def contract(a, b, left, right):
    return lax.dot_general(a, b, (((left,), (right,)), ((), ())), preferred_element_type=F32)


def gram_kernel(at_ref, f_ref, a0_ref, b0_ref, a1_ref, b1_ref, gram_ref, cross_ref, y_ref):
    x, zl, core, col = (at_ref[i] for i in range(4))
    step = pl.program_id(0)
    half = a0_ref.shape[-1]
    count = a0_ref.shape[2]
    per = LEAF // BLOCK
    leaves, order, _ = gram_ref.shape

    @pl.when(step == 0)
    def _():
        for first_ref, second_ref, owner in ((a0_ref, b0_ref, core), (a1_ref, b1_ref, 1 - core)):
            lanes = pl.ds(pl.multiple_of(owner * half, half), half)
            for i in range(4):
                for j in range(2):
                    chip = lax.rem(x + 4 - i, 4) * 2 + lax.rem(zl + j, 2)
                    rows = pl.ds(pl.multiple_of(chip * 16, 16), 16)
                    y_ref[:count, rows, lanes] = first_ref[j, i]
                    y_ref[count:, rows, lanes] = second_ref[i, j]
        for leaf in range(leaves):
            y = y_ref[leaf * per : (leaf + 1) * per].reshape(LEAF, 2 * half)
            gram_ref[leaf] = contract(y, y, 0, 0)[:order, :order]

    leaf = lax.rem(col, 2) * 2 + step
    sibling = lax.rem(col, 2) * 2 + 1 - step
    there = y_ref[pl.ds(sibling * per, per)].reshape(LEAF, 2 * half)
    here = y_ref[pl.ds(leaf * per, per)].reshape(LEAF, 2 * half)
    hi, lo = halves(jnp.dot(f_ref[...], there, preferred_element_type=F32))
    cross = contract(here, hi, 0, 0) + contract(here, lo, 0, 0)
    cross_ref[:, 0] = cross.reshape(cross_ref.shape[0], cross_ref.shape[2], 2 * half)


def grams(at, front, mine, other, order):
    a0, b0 = mine
    half = a0.shape[-1]
    wide = 2 * half
    leaves = 2 * a0.shape[2] * BLOCK // LEAF
    whole = pl.BlockSpec(memory_space=pltpu.VMEM)
    return pl.pallas_call(
        gram_kernel,
        grid_spec=pltpu.PrefetchScalarGridSpec(
            num_scalar_prefetch=1,
            grid=(2,),
            in_specs=[
                pl.BlockSpec((LEAF, LEAF), lambda i, at: (lax.rem(at[3], 2) * 2 + i, 1 - i)),
                whole,
                whole,
                whole,
                whole,
            ],
            out_specs=[
                pl.BlockSpec((leaves, order, order), lambda i, at: (0, 0, 0)),
                pl.BlockSpec((16, 1, wide // 16, wide), lambda i, at: (0, i, 0, 0)),
            ],
            scratch_shapes=[pltpu.VMEM((leaves * LEAF // BLOCK, BLOCK, wide), BF)],
        ),
        out_shape=[
            jax.ShapeDtypeStruct((leaves, order, order), F32),
            jax.ShapeDtypeStruct((16, 2, wide // 16, wide), F32),
        ],
        compiler_params=params(52),
        cost_estimate=cost(2 * 10 * LEAF * wide * wide, 4 * LEAF * LEAF + 4 * leaves * LEAF * wide),
    )(at, front, a0, b0, *other)


def product3(a, b):
    ah, al = halves(a)
    bh, bl = halves(b)
    return contract(ah, bh, 1, 0) + (contract(ah, bl, 1, 0) + contract(al, bh, 1, 0))


def eliminate(s, size):
    groups = size // 8
    sub = lax.broadcasted_iota(jnp.int32, (8, 1), 0)
    for j in range(size):
        g, r = divmod(j, 8)
        for rows in s:
            row = rows[g][r : r + 1, :]
            scaled = row * (1.0 / row[:, j : j + 1])
            for i in range(g, groups):
                c = rows[i][:, j : j + 1]
                if i == g:
                    if r == 7:
                        continue
                    c = jnp.where(sub > r, c, 0.0)
                rows[i] = rows[i] - c * scaled


def inverse_kernel(a_ref, w_ref):
    leaves, order, wide = w_ref.shape
    w_ref[:, :, order - order % 128 :] = jnp.zeros((leaves, order, wide - order + order % 128), F32)
    w_ref[:, :, :order] = a_ref[...]
    lane = lax.broadcasted_iota(jnp.int32, (STEP, 128), 1)
    sub = lax.broadcasted_iota(jnp.int32, (STEP, 128), 0)
    col = lax.broadcasted_iota(jnp.int32, (STEP, wide), 1)
    row = lax.broadcasted_iota(jnp.int32, (STEP, wide), 0)

    @pl.loop(0, order // STEP)
    def _(k):
        base = pl.multiple_of(k * STEP, STEP)
        tile = pl.multiple_of(lax.div(base, 128) * 128, 128)
        odd = base - tile > 0
        s = []
        for leaf in range(leaves):
            d = w_ref[leaf, pl.ds(base, STEP), pl.ds(tile, 128)]
            d = jnp.where(odd, pltpu.roll(d, 128 - STEP, 1), d)
            d = jnp.where(lane < STEP, d, (lane - STEP == sub).astype(F32))
            s.append([d[8 * i : 8 * i + 8] for i in range(STEP // 8)])
        eliminate(s, STEP)
        inside = (col >= base) & (col < base + STEP)
        unit = (col - base == row).astype(F32)
        later = col >= base + STEP
        for leaf in range(leaves):
            d = jnp.concatenate(s[leaf], axis=0)
            diagonal = jnp.sum(jnp.where(lane == sub, d, 0.0), axis=1, keepdims=True)
            x = (d * lax.rsqrt(diagonal))[:, STEP:]
            solved = product3(x, jnp.where(inside, unit, w_ref[leaf, pl.ds(base, STEP), :]))
            w_ref[leaf, pl.ds(base, STEP), :] = solved
            hi, lo = halves(solved)
            none = jnp.zeros_like(hi)
            left_hi, left_lo = jnp.where(later, hi, none), jnp.where(later, lo, none)
            left = jnp.concatenate([left_hi, left_hi, left_lo], axis=0)
            update = contract(left, jnp.concatenate([hi, lo, hi], axis=0), 0, 0)
            for i in range(order // STEP):
                rows = slice(i * STEP, (i + 1) * STEP)

                @pl.when(i > k)
                def _(rows=rows):
                    w_ref[leaf, rows, :] = jnp.where(inside, 0.0, w_ref[leaf, rows, :]) - update[rows]

    for leaf in range(leaves):
        for i in range(order // STEP):
            rows = slice(i * STEP, (i + 1) * STEP)
            w_ref[leaf, rows, :] = jnp.where(col <= row + i * STEP, w_ref[leaf, rows, :], 0.0)


def factor_inverse(gram):
    leaves, order, _ = gram.shape
    wide = -(-order // 128) * 128
    return pl.pallas_call(
        inverse_kernel,
        out_shape=jax.ShapeDtypeStruct((leaves, order, wide), F32),
        in_specs=[VMEM],
        out_specs=VMEM,
        compiler_params=params(40),
        cost_estimate=cost(40e9, 8 * gram.size),
    )(gram)


def local(parent_front, child_update, parent_test, child_test, child_map):
    y, zh = lax.axis_index("y"), lax.axis_index("zh")
    x, zl, core = lax.axis_index("x"), lax.axis_index("zl"), lax.axis_index("core")
    row_index, col_index = lax.axis_index(ROW), lax.axis_index(COL)
    probes = parent_test.shape[1]
    half = 256
    chips = lax.axis_size(CHIP)
    own_blocks = parent_front.shape[0] // BLOCK
    kid_blocks = child_update.shape[1] // BLOCK
    leaf_count = own_blocks * BLOCK // LEAF
    swap = [(0, 1), (1, 0)]

    def half_of(test, which):
        padded = jnp.pad(test, ((0, 0), (0, 0), (0, 2 * half - probes)))
        return lax.dynamic_slice_in_dim(padded, which * half, half, 2)

    front, whole_test = parent_front[None], parent_test[None]
    kid_sent = lax.ppermute(
        probe_send(child_update, half_of(child_test, 1 - core)), "core", swap
    )
    own_sent = lax.ppermute(probe_send(front, half_of(whole_test, 1 - core)), "core", swap)
    kid_part = probe_keep(child_update, half_of(child_test, core), kid_sent, chips)
    kid_share = lax.all_to_all(kid_part, CHIP, 0, 0, tiled=True)
    own_part = probe_keep(front, half_of(whole_test, core), own_sent, chips)
    own_share = lax.all_to_all(own_part, CHIP, 0, 0, tiled=True)

    kids = sum_shares(kid_share, BF)
    first, second = two_way_gather(kids[:kid_blocks], kids[kid_blocks:], "y", "zh")

    targets = row_index * own_blocks + jnp.arange(own_blocks, dtype=jnp.int32)
    hit = child_map[:, None, :] == targets[None, :, None]
    there = jnp.any(hit, axis=2).astype(jnp.int32)
    source = jnp.sum(jnp.where(hit, jnp.arange(child_map.shape[1], dtype=jnp.int32), 0), axis=2)
    owner, place = source // kid_blocks, source % kid_blocks
    ring = (y - owner // 2) % 4
    pair = (zh - owner % 2) % 2
    at = jnp.stack(
        [
            jnp.stack([pair[0], ring[0], place[0], there[0]]),
            jnp.stack([ring[1], pair[1], place[1], there[1]]),
        ]
    ).astype(jnp.int32)
    share = extend_add(at, own_share, first, second)

    cut = own_blocks // 2
    mine = two_way_gather(share[:cut], share[cut:], "x", "zl")
    other = tuple(lax.ppermute(part, "core", swap) for part in mine)
    place_of = jnp.stack([x, zl, core, col_index]).astype(jnp.int32)
    gram, cross = grams(place_of, parent_front, mine, other, probes)

    cross = lax.all_to_all(cross, COL, 0, 0, tiled=True)
    cross = lax.dynamic_slice_in_dim(cross, 2 * row_index, 2, 0)
    cross = cross.reshape(leaf_count, cross.shape[2], 2 * half)
    cross = lax.all_gather(cross, COL)
    inverse = factor_inverse(gram)[:, :, :probes]

    own_rows = jnp.where(
        core == 0,
        jnp.concatenate([share, jnp.concatenate([other[0][0, 0], other[1][0, 0]], 0)], axis=2),
        jnp.concatenate([jnp.concatenate([other[0][0, 0], other[1][0, 0]], 0), share], axis=2),
    )
    own_rows = lax.dynamic_slice_in_dim(own_rows, core * 8, 8, 1)[:, :, :probes]
    leaves = own_rows.reshape(leaf_count, -1, probes).astype(F32)
    basis = jnp.einsum("lkr,lsr->lks", leaves, inverse, precision=HIGH) * math.sqrt(LEAF)
    leaf_basis = basis.astype(BF).reshape(own_blocks, 8, probes)

    rows = probes // lax.axis_size(COL)
    left = lax.dynamic_slice_in_dim(inverse, col_index * rows, rows, 1)
    cross = jnp.moveaxis(cross, 0, 1).reshape(leaf_count, 2 * half, 2 * half)[:, :probes, :probes]
    siblings = inverse.reshape(-1, 2, probes, probes)[:, ::-1].reshape(inverse.shape)
    couplings = jnp.einsum("lir,lrs->lis", left, cross, precision=HIGH)
    couplings = jnp.einsum("lis,lts->lit", couplings, siblings, precision=HIGH)
    return (leaf_basis, couplings)


def solution(mesh):
    split = Mesh(mesh.devices.reshape(4, 2, 4, 2, 2), ("y", "zh", "x", "zl", "core"))
    placed = (P(ROW, COL), P(None, ROW, COL), P(COL, None), P(None, COL, None), P())
    return jax.shard_map(
        local,
        mesh=split,
        in_specs=placed,
        out_specs=(P(ROW, COL, None), P(ROW, COL, None)),
        check_vma=False,
    )
```

```python
import functools
import math

import jax
import jax.numpy as jnp
from jax import lax
from jax.experimental import pallas as pl
from jax.experimental.pallas import tpu as pltpu
from jax.sharding import Mesh
from jax.sharding import PartitionSpec as P

LEAF = 896
BLOCK = 128
ROW = ("y", "zh")
CHIP = ("x", "zl")
COL = ("x", "zl", "core")
F32 = jnp.float32
BF = jnp.bfloat16
VMEM = pl.BlockSpec(memory_space=pltpu.VMEM)
SMEM = pl.BlockSpec(memory_space=pltpu.SMEM)
STEP = 64


def params(mib):
    return pltpu.CompilerParams(vmem_limit_bytes=mib << 20)


def cost(flops, nbytes):
    return pl.CostEstimate(flops=int(flops), bytes_accessed=int(nbytes), transcendentals=0)


def probe_kernel(at_ref, a_ref, b_ref, sent_ref, kept_ref):
    total = contract(a_ref[0], b_ref[0], 1, 1)
    half = sent_ref.shape[2]
    low = total[:, :half]
    pad = jnp.zeros((total.shape[0], 2 * half - total.shape[1]), F32)
    high = jnp.concatenate([total[:, half:], pad], axis=1)
    first = at_ref[2] == 0
    kept_ref[0] = jnp.where(first, low, high)
    sent_ref[0] = jnp.where(first, high, low)


def probe(at, a, b, half):
    count, rows, depth = a.shape
    probes = b.shape[1]
    part = jax.ShapeDtypeStruct((count, rows, half), F32)
    return pl.pallas_call(
        probe_kernel,
        grid=(count, rows // LEAF),
        out_shape=[part, part],
        in_specs=[
            SMEM,
            pl.BlockSpec((1, LEAF, depth), lambda k, i: (k, i, 0)),
            pl.BlockSpec((1, probes, depth), lambda k, i: (k, 0, 0)),
        ],
        out_specs=[pl.BlockSpec((1, LEAF, half), lambda k, i: (k, i, 0))] * 2,
        compiler_params=params(40),
        cost_estimate=cost(4 * count * rows * depth * half, 2 * a.size + 8 * count * rows * half),
    )(at, a, b)


def pack_kernel(at_ref, a_ref, b_ref, o_ref, own_ref, sum_ref):
    total = a_ref[0] + b_ref[0]
    sum_ref[...] = total
    chips, blocks, rows, _ = o_ref.shape
    chip_here = at_ref[0] * 2 + at_ref[1]
    for block in range(blocks):
        for chip in range(chips):
            start = (block * chips + chip) * rows
            o_ref[chip, block] = total[start : start + rows].astype(BF)
        own = pl.multiple_of((block * chips + chip_here) * rows, rows)
        own_ref[block] = sum_ref[pl.ds(own, rows), :]


def pack(at, kept, received, chips):
    count, rows, half = kept.shape
    per = rows // LEAF
    blocks = LEAF // BLOCK
    slab = BLOCK // chips
    whole = count * rows // BLOCK
    return pl.pallas_call(
        pack_kernel,
        grid=(count, per),
        out_shape=[
            jax.ShapeDtypeStruct((chips, whole, slab, half), BF),
            jax.ShapeDtypeStruct((whole, slab, half), F32),
        ],
        in_specs=[
            SMEM,
            pl.BlockSpec((1, LEAF, half), lambda k, i: (k, i, 0)),
            pl.BlockSpec((1, LEAF, half), lambda k, i: (k, i, 0)),
        ],
        out_specs=[
            pl.BlockSpec((chips, blocks, slab, half), lambda k, i: (0, k * per + i, 0, 0)),
            pl.BlockSpec((blocks, slab, half), lambda k, i: (k * per + i, 0, 0)),
        ],
        scratch_shapes=[pltpu.VMEM((LEAF, half), F32)],
        compiler_params=params(24),
        cost_estimate=cost(kept.size, 10 * kept.size),
    )(at, kept, received)


def shift(value, axis, by):
    size = lax.axis_size(axis)
    return lax.ppermute(value, axis, [(i, (i + by) % size) for i in range(size)])


def ring_gather(value, axis):
    size = lax.axis_size(axis)
    return jnp.stack([value] + [shift(value, axis, by) for by in range(1, size)])


def two_way_gather(first, second, big, small):
    first_ring = ring_gather(first, big)
    second_pair = ring_gather(second, small)
    return ring_gather(first_ring, small), ring_gather(second_pair, big)


def sum_of(shares_ref, own, here, at):
    for chip in range(shares_ref.shape[0]):
        own += jnp.where(here != chip, shares_ref[(chip, *at)].astype(F32), 0.0)
    return own


def sum_kernel(at_ref, k_ref, own_ref, o_ref):
    here = at_ref[0] * 2 + at_ref[1]
    for block in range(o_ref.shape[0]):
        o_ref[block] = sum_of(k_ref, own_ref[block], here, (block,)).astype(o_ref.dtype)


def sum_shares(at, shares, own, dtype):
    return pl.pallas_call(
        sum_kernel,
        out_shape=jax.ShapeDtypeStruct(shares.shape[1:], dtype),
        in_specs=[SMEM, VMEM, VMEM],
        out_specs=VMEM,
        compiler_params=params(24),
        cost_estimate=cost(shares.size, 2 * shares.size),
    )(at, shares, own)


def extend_kernel(at_ref, from_ref, p_ref, own_ref, first_ref, second_ref, o_ref):
    here = at_ref[0] * 2 + at_ref[1]
    for block in range(p_ref.shape[1]):
        total = sum_of(p_ref, own_ref[block], here, (block,))
        for kid, ref in enumerate((first_ref, second_ref)):
            near, far, place = (from_ref[kid, part, block] for part in range(3))
            there = from_ref[kid, 3, block]
            total += jnp.where(there > 0, ref[near, far, place].astype(F32), 0.0)
        o_ref[block] = total.astype(BF)


def extend_add(at, source, parent, own, first, second):
    return pl.pallas_call(
        extend_kernel,
        out_shape=jax.ShapeDtypeStruct(parent.shape[1:], BF),
        in_specs=[SMEM, SMEM, VMEM, VMEM, VMEM, VMEM],
        out_specs=VMEM,
        compiler_params=params(32),
        cost_estimate=cost(parent.size, 6 * parent.size),
    )(at, source, parent, own, first, second)


def halves(x):
    hi = x.astype(BF)
    return hi, (x - hi.astype(F32)).astype(BF)


def contract(a, b, left, right):
    return lax.dot_general(a, b, (((left,), (right,)), ((), ())), preferred_element_type=F32)


def gram_kernel(at_ref, f_ref, a0_ref, b0_ref, a1_ref, b1_ref, gram_ref, cross_ref, y_ref):
    x, zl, core, col = (at_ref[i] for i in range(4))
    step = pl.program_id(0)
    half = a0_ref.shape[-1]
    count = a0_ref.shape[2]
    per = LEAF // BLOCK
    leaves, order, _ = gram_ref.shape

    @pl.when(step == 0)
    def _():
        for first_ref, second_ref, owner in ((a0_ref, b0_ref, core), (a1_ref, b1_ref, 1 - core)):
            lanes = pl.ds(pl.multiple_of(owner * half, half), half)
            for i in range(4):
                for j in range(2):
                    chip = lax.rem(x + 4 - i, 4) * 2 + lax.rem(zl + j, 2)
                    rows = pl.ds(pl.multiple_of(chip * 16, 16), 16)
                    y_ref[:count, rows, lanes] = first_ref[j, i]
                    y_ref[count:, rows, lanes] = second_ref[i, j]
        for leaf in range(leaves):
            y = y_ref[leaf * per : (leaf + 1) * per].reshape(LEAF, 2 * half)
            gram_ref[leaf] = contract(y, y, 0, 0)[:order]

    leaf = lax.rem(col, 2) * 2 + step
    sibling = lax.rem(col, 2) * 2 + 1 - step
    there = y_ref[pl.ds(sibling * per, per)].reshape(LEAF, 2 * half)
    here = y_ref[pl.ds(leaf * per, per)].reshape(LEAF, 2 * half)
    hi, lo = halves(jnp.dot(f_ref[...], there, preferred_element_type=F32))
    cross = contract(here, hi, 0, 0) + contract(here, lo, 0, 0)
    cross_ref[:, 0] = cross.reshape(cross_ref.shape[0], cross_ref.shape[2], 2 * half)


def grams(at, front, mine, other, order):
    a0, b0 = mine
    half = a0.shape[-1]
    wide = 2 * half
    leaves = 2 * a0.shape[2] * BLOCK // LEAF
    whole = pl.BlockSpec(memory_space=pltpu.VMEM)
    return pl.pallas_call(
        gram_kernel,
        grid_spec=pltpu.PrefetchScalarGridSpec(
            num_scalar_prefetch=1,
            grid=(2,),
            in_specs=[
                pl.BlockSpec((LEAF, LEAF), lambda i, at: (lax.rem(at[3], 2) * 2 + i, 1 - i)),
                whole,
                whole,
                whole,
                whole,
            ],
            out_specs=[
                pl.BlockSpec((leaves, order, wide), lambda i, at: (0, 0, 0)),
                pl.BlockSpec((16, 1, wide // 16, wide), lambda i, at: (0, i, 0, 0)),
            ],
            scratch_shapes=[pltpu.VMEM((leaves * LEAF // BLOCK, BLOCK, wide), BF)],
        ),
        out_shape=[
            jax.ShapeDtypeStruct((leaves, order, wide), F32),
            jax.ShapeDtypeStruct((16, 2, wide // 16, wide), F32),
        ],
        compiler_params=params(52),
        cost_estimate=cost(2 * 10 * LEAF * wide * wide, 4 * LEAF * LEAF + 4 * leaves * LEAF * wide),
    )(at, front, a0, b0, *other)


def product3(a, b):
    ah, al = halves(a)
    bh, bl = halves(b)
    return contract(ah, bh, 1, 0) + (contract(ah, bl, 1, 0) + contract(al, bh, 1, 0))


def eliminate(s, size):
    groups = size // 8
    sub = lax.broadcasted_iota(jnp.int32, (8, 1), 0)
    for j in range(size):
        g, r = divmod(j, 8)
        for rows in s:
            row = rows[g][r : r + 1, :]
            scaled = row * (1.0 / row[:, j : j + 1])
            for i in range(g, groups):
                c = rows[i][:, j : j + 1]
                if i == g:
                    if r == 7:
                        continue
                    c = jnp.where(sub > r, c, 0.0)
                rows[i] = rows[i] - c * scaled


def inverse_kernel(a_ref, w_ref, *, first, last):
    leaves, order, wide = w_ref.shape
    w_ref[...] = a_ref[...]
    lane = lax.broadcasted_iota(jnp.int32, (STEP, 128), 1)
    sub = lax.broadcasted_iota(jnp.int32, (STEP, 128), 0)
    col = lax.broadcasted_iota(jnp.int32, (STEP, wide), 1)
    row = lax.broadcasted_iota(jnp.int32, (STEP, wide), 0)

    @pl.loop(first, last)
    def _(k):
        base = pl.multiple_of(k * STEP, STEP)
        tile = pl.multiple_of(lax.div(base, 128) * 128, 128)
        odd = base - tile > 0
        s = []
        for leaf in range(leaves):
            d = w_ref[leaf, pl.ds(base, STEP), pl.ds(tile, 128)]
            d = jnp.where(odd, pltpu.roll(d, 128 - STEP, 1), d)
            d = jnp.where(lane < STEP, d, (lane - STEP == sub).astype(F32))
            s.append([d[8 * i : 8 * i + 8] for i in range(STEP // 8)])
        eliminate(s, STEP)
        inside = (col >= base) & (col < base + STEP)
        unit = (col - base == row).astype(F32)
        later = col >= base + STEP
        for leaf in range(leaves):
            d = jnp.concatenate(s[leaf], axis=0)
            diagonal = jnp.sum(jnp.where(lane == sub, d, 0.0), axis=1, keepdims=True)
            x = (d * lax.rsqrt(diagonal))[:, STEP:]
            solved = product3(x, jnp.where(inside, unit, w_ref[leaf, pl.ds(base, STEP), :]))
            w_ref[leaf, pl.ds(base, STEP), :] = solved
            hi, lo = halves(solved)
            none = jnp.zeros_like(hi)
            left_hi, left_lo = jnp.where(later, hi, none), jnp.where(later, lo, none)
            left = jnp.concatenate([left_hi, left_hi, left_lo], axis=0)
            update = contract(left, jnp.concatenate([hi, lo, hi], axis=0), 0, 0)
            for i in range(order // STEP):
                rows = slice(i * STEP, (i + 1) * STEP)

                @pl.when(i > k)
                def _(rows=rows):
                    w_ref[leaf, rows, :] = jnp.where(inside, 0.0, w_ref[leaf, rows, :]) - update[rows]

    if last < order // STEP:
        return
    for leaf in range(leaves):
        for i in range(order // STEP):
            rows = slice(i * STEP, (i + 1) * STEP)
            w_ref[leaf, rows, :] = jnp.where(col <= row + i * STEP, w_ref[leaf, rows, :], 0.0)


def factor_inverse(work, first, last):
    return pl.pallas_call(
        functools.partial(inverse_kernel, first=first, last=last),
        out_shape=jax.ShapeDtypeStruct(work.shape, F32),
        in_specs=[VMEM],
        out_specs=VMEM,
        compiler_params=params(40),
        cost_estimate=cost((last - first) * 10e9, 8 * work.size),
    )(work)


def finish_kernel(at_ref, w_ref, own_ref, cross_ref, basis_ref, core_ref):
    leaves, order, wide = w_ref.shape
    rows = core_ref.shape[1]
    base = at_ref[3] * rows
    odd = lax.rem(base, 8)
    base = pl.multiple_of(base - odd, 8)
    tall = rows + 4
    for leaf in range(leaves):
        hi, lo = halves(w_ref[leaf])
        own = own_ref[leaf].astype(BF)
        basis_ref[leaf] = (contract(own, hi, 1, 1) + contract(own, lo, 1, 1)) * math.sqrt(LEAF)
        left = w_ref[leaf, pl.ds(base, tall), :]
        left = jnp.where(odd > 0, jnp.concatenate([left[4:], left[:4]], axis=0), left)
        cross = cross_ref[:, leaf].reshape(wide, wide)
        half_way, rest = halves(product3(left, cross))
        hi, lo = halves(w_ref[leaf ^ 1])
        core = contract(half_way, hi, 1, 1) + (contract(half_way, lo, 1, 1) + contract(rest, hi, 1, 1))
        core_ref[leaf] = core[:rows]


def finish(at, inverse, own, cross, rows):
    leaves, order, _ = inverse.shape
    return pl.pallas_call(
        finish_kernel,
        out_shape=[
            jax.ShapeDtypeStruct((leaves, own.shape[1], order), F32),
            jax.ShapeDtypeStruct((leaves, rows, order), F32),
        ],
        in_specs=[SMEM, VMEM, VMEM, VMEM],
        out_specs=[VMEM, VMEM],
        compiler_params=params(40),
        cost_estimate=cost(4e9, 4 * (inverse.size + cross.size)),
    )(at, inverse, own, cross)


def local(parent_front, child_update, parent_test, child_test, child_map):
    y, zh = lax.axis_index("y"), lax.axis_index("zh")
    x, zl, core = lax.axis_index("x"), lax.axis_index("zl"), lax.axis_index("core")
    row_index, col_index = lax.axis_index(ROW), lax.axis_index(COL)
    probes = parent_test.shape[1]
    half = 256
    chips = lax.axis_size(CHIP)
    own_blocks = parent_front.shape[0] // BLOCK
    kid_blocks = child_update.shape[1] // BLOCK
    leaf_count = own_blocks * BLOCK // LEAF
    swap = [(0, 1), (1, 0)]

    at = jnp.stack([x, zl, core, col_index]).astype(jnp.int32)
    kid_sent, kid_kept = probe(at, child_update, jnp.swapaxes(child_test, 1, 2), half)
    kid_sent = lax.ppermute(kid_sent, "core", swap)
    own_sent, own_kept = probe(at, parent_front[None], parent_test.T[None], half)
    own_sent = lax.ppermute(own_sent, "core", swap)
    kid_part, kid_rest = pack(at, kid_kept, kid_sent, chips)
    kid_share = lax.all_to_all(kid_part, CHIP, 0, 0, tiled=True)
    own_part, own_rest = pack(at, own_kept, own_sent, chips)
    own_share = lax.all_to_all(own_part, CHIP, 0, 0, tiled=True)

    kids = sum_shares(at, kid_share, kid_rest, BF)
    first, second = two_way_gather(kids[:kid_blocks], kids[kid_blocks:], "y", "zh")

    targets = row_index * own_blocks + jnp.arange(own_blocks, dtype=jnp.int32)
    hit = child_map[:, None, :] == targets[None, :, None]
    there = jnp.any(hit, axis=2).astype(jnp.int32)
    source = jnp.sum(jnp.where(hit, jnp.arange(child_map.shape[1], dtype=jnp.int32), 0), axis=2)
    owner, place = source // kid_blocks, source % kid_blocks
    ring = (y - owner // 2) % 4
    pair = (zh - owner % 2) % 2
    origin = jnp.stack(
        [
            jnp.stack([pair[0], ring[0], place[0], there[0]]),
            jnp.stack([ring[1], pair[1], place[1], there[1]]),
        ]
    ).astype(jnp.int32)
    share = extend_add(at, origin, own_share, own_rest, first, second)

    cut = own_blocks // 2
    mine = two_way_gather(share[:cut], share[cut:], "x", "zl")
    other = tuple(lax.ppermute(part, "core", swap) for part in mine)
    gram, cross = grams(at, parent_front, mine, other, probes)

    own_rows = jnp.where(
        core == 0,
        jnp.concatenate([share, jnp.concatenate([other[0][0, 0], other[1][0, 0]], 0)], axis=2),
        jnp.concatenate([jnp.concatenate([other[0][0, 0], other[1][0, 0]], 0), share], axis=2),
    )
    own_rows = lax.dynamic_slice_in_dim(own_rows, core * 8, 8, 1).astype(F32)
    own_rows = own_rows.reshape(leaf_count, -1, 2 * half)

    cross = lax.all_to_all(cross, COL, 0, 0, tiled=True)
    cross = lax.dynamic_slice_in_dim(cross, 2 * row_index, 2, 0)
    cross = cross.reshape(leaf_count, cross.shape[2], 2 * half)
    work = factor_inverse(gram, 0, 3)
    work, cross = lax.optimization_barrier((work, cross))
    cross = lax.all_gather(cross, COL)
    inverse = factor_inverse(work, 3, probes // STEP)
    basis, couplings = finish(at, inverse, own_rows, cross, probes // lax.axis_size(COL))
    return (basis.astype(BF).reshape(own_blocks, 8, probes), couplings)


def solution(mesh):
    split = Mesh(mesh.devices.reshape(4, 2, 4, 2, 2), ("y", "zh", "x", "zl", "core"))
    placed = (P(ROW, COL), P(None, ROW, COL), P(COL, None), P(None, COL, None), P())
    return jax.shard_map(
        local,
        mesh=split,
        in_specs=placed,
        out_specs=(P(ROW, COL, None), P(ROW, COL, None)),
        check_vma=False,
    )
```

```python
import functools
import math

import jax
import jax.numpy as jnp
from jax import lax
from jax.experimental import pallas as pl
from jax.experimental.pallas import tpu as pltpu
from jax.sharding import Mesh
from jax.sharding import PartitionSpec as P

LEAF = 896
BLOCK = 128
ROW = ("y", "zh")
CHIP = ("x", "zl")
COL = ("x", "zl", "core")
F32 = jnp.float32
BF = jnp.bfloat16
VMEM = pl.BlockSpec(memory_space=pltpu.VMEM)
SMEM = pl.BlockSpec(memory_space=pltpu.SMEM)
STEP = 64


def params(mib):
    return pltpu.CompilerParams(vmem_limit_bytes=mib << 20)


def cost(flops, nbytes):
    return pl.CostEstimate(flops=int(flops), bytes_accessed=int(nbytes), transcendentals=0)


def probe_kernel(at_ref, a_ref, b_ref, sent_ref, kept_ref):
    total = contract(a_ref[0], b_ref[0], 1, 1)
    half = sent_ref.shape[2]
    low = total[:, :half]
    pad = jnp.zeros((total.shape[0], 2 * half - total.shape[1]), F32)
    high = jnp.concatenate([total[:, half:], pad], axis=1)
    first = at_ref[2] == 0
    kept_ref[0] = jnp.where(first, low, high)
    sent_ref[0] = jnp.where(first, high, low)


def probe(at, a, b, half):
    count, rows, depth = a.shape
    probes = b.shape[1]
    part = jax.ShapeDtypeStruct((count, rows, half), F32)
    return pl.pallas_call(
        probe_kernel,
        grid=(count, rows // LEAF),
        out_shape=[part, part],
        in_specs=[
            SMEM,
            pl.BlockSpec((1, LEAF, depth), lambda k, i: (k, i, 0)),
            pl.BlockSpec((1, probes, depth), lambda k, i: (k, 0, 0)),
        ],
        out_specs=[pl.BlockSpec((1, LEAF, half), lambda k, i: (k, i, 0))] * 2,
        compiler_params=params(40),
        cost_estimate=cost(4 * count * rows * depth * half, 2 * a.size + 8 * count * rows * half),
    )(at, a, b)


def pack_kernel(at_ref, a_ref, b_ref, o_ref, own_ref, sum_ref):
    total = a_ref[0] + b_ref[0]
    sum_ref[...] = total
    chips, blocks, rows, _ = o_ref.shape
    chip_here = at_ref[0] * 2 + at_ref[1]
    for block in range(blocks):
        for chip in range(chips):
            start = (block * chips + chip) * rows
            o_ref[chip, block] = total[start : start + rows].astype(BF)
        own = pl.multiple_of((block * chips + chip_here) * rows, rows)
        own_ref[block] = sum_ref[pl.ds(own, rows), :]


def pack(at, kept, received, chips):
    count, rows, half = kept.shape
    per = rows // LEAF
    blocks = LEAF // BLOCK
    slab = BLOCK // chips
    whole = count * rows // BLOCK
    return pl.pallas_call(
        pack_kernel,
        grid=(count, per),
        out_shape=[
            jax.ShapeDtypeStruct((chips, whole, slab, half), BF),
            jax.ShapeDtypeStruct((whole, slab, half), F32),
        ],
        in_specs=[
            SMEM,
            pl.BlockSpec((1, LEAF, half), lambda k, i: (k, i, 0)),
            pl.BlockSpec((1, LEAF, half), lambda k, i: (k, i, 0)),
        ],
        out_specs=[
            pl.BlockSpec((chips, blocks, slab, half), lambda k, i: (0, k * per + i, 0, 0)),
            pl.BlockSpec((blocks, slab, half), lambda k, i: (k * per + i, 0, 0)),
        ],
        scratch_shapes=[pltpu.VMEM((LEAF, half), F32)],
        compiler_params=params(24),
        cost_estimate=cost(kept.size, 10 * kept.size),
    )(at, kept, received)


def shift(value, axis, by):
    size = lax.axis_size(axis)
    return lax.ppermute(value, axis, [(i, (i + by) % size) for i in range(size)])


def ring_gather(value, axis):
    size = lax.axis_size(axis)
    return jnp.stack([value] + [shift(value, axis, by) for by in range(1, size)])


def two_way_gather(first, second, big, small):
    first_ring = ring_gather(first, big)
    second_pair = ring_gather(second, small)
    return ring_gather(first_ring, small), ring_gather(second_pair, big)


def sum_of(shares_ref, own, here, at):
    for chip in range(shares_ref.shape[0]):
        own += jnp.where(here != chip, shares_ref[(chip, *at)].astype(F32), 0.0)
    return own


def sum_kernel(at_ref, k_ref, own_ref, o_ref):
    here = at_ref[0] * 2 + at_ref[1]
    for block in range(o_ref.shape[0]):
        o_ref[block] = sum_of(k_ref, own_ref[block], here, (block,)).astype(o_ref.dtype)


def sum_shares(at, shares, own, dtype):
    return pl.pallas_call(
        sum_kernel,
        out_shape=jax.ShapeDtypeStruct(shares.shape[1:], dtype),
        in_specs=[SMEM, VMEM, VMEM],
        out_specs=VMEM,
        compiler_params=params(24),
        cost_estimate=cost(shares.size, 2 * shares.size),
    )(at, shares, own)


def extend_kernel(at_ref, from_ref, p_ref, own_ref, first_ref, second_ref, keep_ref, send_ref, all_ref):
    here = at_ref[0] * 2 + at_ref[1]
    core = at_ref[2]
    for block in range(p_ref.shape[1]):
        total = sum_of(p_ref, own_ref[block], here, (block,))
        for kid, ref in enumerate((first_ref, second_ref)):
            near, far, place = (from_ref[kid, part, block] for part in range(3))
            there = from_ref[kid, 3, block]
            total += jnp.where(there > 0, ref[near, far, place].astype(F32), 0.0)
        all_ref[block] = total.astype(BF)
    count = keep_ref.shape[0]
    keep_ref[...] = all_ref[pl.ds(core * count, count)]
    send_ref[...] = all_ref[pl.ds((1 - core) * count, count)]


def extend_add(at, source, parent, own, first, second):
    blocks, slab, half = parent.shape[1:]
    pair = jax.ShapeDtypeStruct((blocks // 2, slab, half), BF)
    return pl.pallas_call(
        extend_kernel,
        out_shape=[pair, pair],
        in_specs=[SMEM, SMEM, VMEM, VMEM, VMEM, VMEM],
        out_specs=[VMEM, VMEM],
        scratch_shapes=[pltpu.VMEM(parent.shape[1:], BF)],
        compiler_params=params(16),
        cost_estimate=cost(parent.size, 6 * parent.size),
    )(at, source, parent, own, first, second)


def halves(x):
    hi = x.astype(BF)
    return hi, (x - hi.astype(F32)).astype(BF)


def contract(a, b, left, right):
    return lax.dot_general(a, b, (((left,), (right,)), ((), ())), preferred_element_type=F32)


def product3(a, b):
    ah, al = halves(a)
    bh, bl = halves(b)
    return contract(ah, bh, 1, 0) + (contract(ah, bl, 1, 0) + contract(al, bh, 1, 0))


LEVEL = 8.0


def gram_kernel(at_ref, f_ref, a_ref, b_ref, gram_ref, root_ref, cross_ref, y_ref):
    x, zl, core = (at_ref[i] for i in range(3))
    step = pl.program_id(0)
    half = a_ref.shape[-1]
    per = LEAF // BLOCK
    leaves, order, wide = gram_ref.shape
    row = lax.broadcasted_iota(jnp.int32, (order, wide), 0)
    col = lax.broadcasted_iota(jnp.int32, (order, wide), 1)
    lane = lax.broadcasted_iota(jnp.int32, (1, wide), 1)

    @pl.when(step == 0)
    def _():
        for side, owner in ((0, core), (1, 1 - core)):
            lanes = pl.ds(pl.multiple_of(owner * half, half), half)
            for i in range(4):
                for j in range(2):
                    chip = lax.rem(x + 4 - i, 4) * 2 + lax.rem(zl + j, 2)
                    rows = pl.ds(pl.multiple_of(chip * 16, 16), 16)
                    y_ref[:per, rows, lanes] = a_ref[j, i, side]
                    y_ref[per:, rows, lanes] = b_ref[i, j, side]
        for leaf in range(leaves):
            y = y_ref[leaf * per : (leaf + 1) * per].reshape(LEAF, wide)
            gram = contract(y, y, 0, 0)[:order]
            gram_ref[leaf] = gram
            square = jnp.sum(jnp.where(row == col, gram, 0.0), axis=0, keepdims=True)
            root_ref[leaf] = jnp.sqrt(jnp.where(lane < order, square, 1.0))

    here = y_ref[pl.ds(step * per, per)].reshape(LEAF, wide)
    there = y_ref[pl.ds((1 - step) * per, per)].reshape(LEAF, wide)
    hi, lo = halves(jnp.dot(f_ref[...], there, preferred_element_type=F32) / root_ref[1 - step])
    cross = (contract(here, hi, 0, 0) + contract(here, lo, 0, 0))[:order]
    square = jnp.sum(jnp.where(row == col, gram_ref[step], 0.0), axis=1, keepdims=True)
    cross = cross * lax.rsqrt(square)
    most = jnp.max(jnp.max(jnp.abs(cross), axis=0, keepdims=True), axis=1, keepdims=True)
    power = jnp.ceil(jnp.log2(jnp.maximum(most, 1e-30)))
    cross = jnp.where(col < order, cross * jnp.exp2(LEVEL - power), power)
    cross_ref[:, 0] = cross.reshape(cross_ref.shape[0], cross_ref.shape[2], wide)


def grams(at, front, mine, order, chips):
    half = mine[0].shape[-1]
    wide = 2 * half
    whole = pl.BlockSpec(memory_space=pltpu.VMEM)
    return pl.pallas_call(
        gram_kernel,
        grid_spec=pltpu.PrefetchScalarGridSpec(
            num_scalar_prefetch=1,
            grid=(2,),
            in_specs=[
                pl.BlockSpec((LEAF, LEAF), lambda i, at: (at[2] * 2 + i, 1 - i)),
                whole,
                whole,
            ],
            out_specs=[
                pl.BlockSpec((2, order, wide), lambda i, at: (0, 0, 0)),
                pl.BlockSpec((2, 1, wide), lambda i, at: (0, 0, 0)),
                pl.BlockSpec((chips, 1, order // chips, wide), lambda i, at: (0, i, 0, 0)),
            ],
            scratch_shapes=[pltpu.VMEM((2 * LEAF // BLOCK, BLOCK, wide), BF)],
        ),
        out_shape=[
            jax.ShapeDtypeStruct((2, order, wide), F32),
            jax.ShapeDtypeStruct((2, 1, wide), F32),
            jax.ShapeDtypeStruct((chips, 2, order // chips, wide), F32),
        ],
        compiler_params=params(52),
        cost_estimate=cost(2 * 8 * LEAF * wide * wide, 4 * LEAF * LEAF + 2 * leaves_bytes(wide)),
    )(at, front, *mine)


def leaves_bytes(wide):
    return 2 * LEAF * wide * 2


def eliminate(s, size):
    groups = size // 8
    shape = (8, 128)
    sub = lax.broadcasted_iota(jnp.int32, shape, 0)
    for g in range(groups):
        for rows in s:
            c = {
                (i, k): jnp.broadcast_to(rows[i][:, 8 * g + k : 8 * g + k + 1], shape)
                for i in range(g, groups)
                for k in range(8)
            }
            pivot = [jnp.broadcast_to(rows[g][k : k + 1, :], shape) for k in range(8)]
            d = {
                (i, k): jnp.broadcast_to(c[g, k][i : i + 1, :], shape)
                for i in range(8)
                for k in range(i, 8)
            }
            low = {}
            scaled = []
            for k in range(8):
                inverse = pl.reciprocal(d[k, k], approx=True)
                inverse = inverse * (2.0 - d[k, k] * inverse)
                scaled.append(pivot[k] * inverse)
                for i in range(k + 1, 8):
                    low[i, k] = d[k, i] * inverse
                    pivot[i] = pivot[i] - low[i, k] * pivot[k]
                    for m in range(i, 8):
                        d[i, m] = d[i, m] - low[i, k] * d[k, m]
            for m in reversed(range(8)):
                for k in range(m + 1, 8):
                    scaled[m] = scaled[m] - low[k, m] * scaled[k]
            for i in range(g + 1, groups):
                new = rows[i]
                for k in range(8):
                    new = new - c[i, k] * scaled[k]
                rows[i] = new
            new = pivot[0]
            for k in range(1, 8):
                new = jnp.where(sub == k, pivot[k], new)
            rows[g] = new


def inverse_kernel(a_ref, w_ref, x_ref, d_ref, *, first, last):
    leaves, order, wide = w_ref.shape
    blocks = order // STEP
    w_ref[...] = a_ref[...]
    lane = lax.broadcasted_iota(jnp.int32, (STEP, 128), 1)
    sub = lax.broadcasted_iota(jnp.int32, (STEP, 128), 0)
    col = lax.broadcasted_iota(jnp.int32, (STEP, wide), 1)
    row = lax.broadcasted_iota(jnp.int32, (STEP, wide), 0)
    unit = (lane - STEP == sub).astype(F32)

    def spread(k, live):
        base = pl.multiple_of(k * STEP, STEP)
        inside = (col >= base) & (col < base + STEP)
        own = (col - base == row).astype(F32)
        rest = (col >= base + STEP) & live
        for leaf in range(leaves):
            w = w_ref[leaf, pl.ds(base, STEP), :]
            r = product3(x_ref[leaf], jnp.where(inside, own, w))
            w_ref[leaf, pl.ds(base, STEP), :] = jnp.where(live, r, w)
            hi, lo = halves(r)
            none = jnp.zeros_like(hi)
            left_hi, left_lo = jnp.where(rest, hi, none), jnp.where(rest, lo, none)
            left = jnp.concatenate([left_hi, left_hi, left_lo], axis=0)
            update = contract(left, jnp.concatenate([hi, lo, hi], axis=0), 0, 0)
            for i in range(1, blocks):
                rows = slice(i * STEP, (i + 1) * STEP)
                old = jnp.where(inside & live & (i > k), 0.0, w_ref[leaf, rows, :])
                w_ref[leaf, rows, :] = old - update[rows]

    start, tile = first * STEP, first * STEP // 128 * 128
    for leaf in range(leaves):
        d = w_ref[leaf, start : start + STEP, tile : tile + 128]
        d_ref[leaf] = pltpu.roll(d, 128 - STEP, 1) if start > tile else d
        x_ref[leaf] = jnp.zeros((STEP, STEP), F32)

    @pl.loop(first, last)
    def _(k):
        s = []
        for leaf in range(leaves):
            d = jnp.where(lane < STEP, d_ref[leaf], unit)
            s.append([d[8 * i : 8 * i + 8] for i in range(STEP // 8)])
        spread(jnp.maximum(k - 1, 0), k > first)
        eliminate(s, STEP)
        base = pl.multiple_of(k * STEP, STEP)
        after = pl.multiple_of(jnp.minimum(k + 1, blocks - 1) * STEP, STEP)
        tile = pl.multiple_of(lax.div(after, 128) * 128, 128)
        odd = after - tile > 0
        for leaf in range(leaves):
            d = jnp.concatenate(s[leaf], axis=0)
            diagonal = jnp.sum(jnp.where(lane == sub, d, 0.0), axis=1, keepdims=True)
            x = (d * lax.rsqrt(diagonal))[:, STEP:]
            x_ref[leaf] = x
            hi, lo = halves(product3(x, w_ref[leaf, pl.ds(base, STEP), pl.ds(tile, 128)]))
            left = jnp.concatenate([hi, hi, lo], axis=0)
            update = contract(left, jnp.concatenate([hi, lo, hi], axis=0), 0, 0)
            update = jnp.where(odd, update[STEP:], update[:STEP])
            d = w_ref[leaf, pl.ds(after, STEP), pl.ds(tile, 128)] - update
            d_ref[leaf] = jnp.where(odd, pltpu.roll(d, 128 - STEP, 1), d)

    spread(last - 1, True)
    if last < blocks:
        return
    for leaf in range(leaves):
        for i in range(blocks):
            rows = slice(i * STEP, (i + 1) * STEP)
            w_ref[leaf, rows, :] = jnp.where(col <= row + i * STEP, w_ref[leaf, rows, :], 0.0)


def factor_inverse(work, first, last):
    leaves = work.shape[0]
    return pl.pallas_call(
        functools.partial(inverse_kernel, first=first, last=last),
        out_shape=jax.ShapeDtypeStruct(work.shape, F32),
        in_specs=[VMEM],
        out_specs=VMEM,
        scratch_shapes=[
            pltpu.VMEM((leaves, STEP, STEP), F32),
            pltpu.VMEM((leaves, STEP, 128), F32),
        ],
        compiler_params=params(24),
        cost_estimate=cost((last - first) * 5.5e9, 8 * work.size),
    )(work)


def finish_kernel(at_ref, w_ref, root_ref, own_ref, cross_ref, keep_ref, send_ref):
    leaves, order, wide = w_ref.shape
    slabs = LEAF // BLOCK
    rows = order // cross_ref.shape[0]
    base = pl.multiple_of((at_ref[0] * 2 + at_ref[1]) * rows, 8)
    first = at_ref[2] == 0
    tall = own_ref.shape[1] // 2
    for leaf in range(leaves):
        hi, lo = halves(w_ref[leaf])
        own = own_ref[leaf]
        basis = (contract(own, hi, 1, 1) + contract(own, lo, 1, 1)) * math.sqrt(LEAF)
        parts = basis.reshape(slabs, 2, tall // slabs, order)
        low, high = parts[:, 0].reshape(tall, order), parts[:, 1].reshape(tall, order)
        keep_ref[leaf, :tall] = jnp.where(first, low, high)
        send_ref[leaf, :tall] = jnp.where(first, high, low)
        left = w_ref[leaf, pl.ds(base, rows), :] * root_ref[leaf]
        cross = cross_ref[:, leaf].reshape(order, wide)
        level = jnp.exp2(cross[:1, order : order + 1] - LEVEL)
        half_way, rest = halves(product3(left[:, :order], cross))
        hi, lo = halves(w_ref[1 - leaf] * root_ref[1 - leaf])
        core = contract(half_way, hi, 1, 1) + (contract(half_way, lo, 1, 1) + contract(rest, hi, 1, 1))
        core = core * level
        low, high = core[: rows // 2], core[rows // 2 :]
        keep_ref[leaf, tall:] = jnp.where(first, low, high)
        send_ref[leaf, tall:] = jnp.where(first, high, low)


def finish(at, inverse, root, own, cross):
    leaves, order, _ = inverse.shape
    rows = (own.shape[1] + order // cross.shape[0]) // 2
    part = jax.ShapeDtypeStruct((leaves, rows, order), F32)
    return pl.pallas_call(
        finish_kernel,
        out_shape=[part, part],
        in_specs=[SMEM, VMEM, VMEM, VMEM, VMEM],
        out_specs=[VMEM, VMEM],
        compiler_params=params(24),
        cost_estimate=cost(2e9, 4 * (inverse.size + cross.size)),
    )(at, inverse, root, own, cross)


def local(parent_front, child_update, parent_test, child_test, child_map):
    y, zh = lax.axis_index("y"), lax.axis_index("zh")
    x, zl, core = lax.axis_index("x"), lax.axis_index("zl"), lax.axis_index("core")
    row_index = lax.axis_index(ROW)
    probes = parent_test.shape[1]
    half = 256
    chips = lax.axis_size(CHIP)
    own_blocks = parent_front.shape[0] // BLOCK
    kid_blocks = child_update.shape[1] // BLOCK
    swap = [(0, 1), (1, 0)]

    at = jnp.stack([x, zl, core]).astype(jnp.int32)
    kid_sent, kid_kept = probe(at, child_update, jnp.swapaxes(child_test, 1, 2), half)
    kid_sent = lax.ppermute(kid_sent, "core", swap)
    own_sent, own_kept = probe(at, parent_front[None], parent_test.T[None], half)
    own_sent = lax.ppermute(own_sent, "core", swap)
    kid_part, kid_rest = pack(at, kid_kept, kid_sent, chips)
    kid_share = lax.all_to_all(kid_part, CHIP, 0, 0, tiled=True)
    own_part, own_rest = pack(at, own_kept, own_sent, chips)
    own_share = lax.all_to_all(own_part, CHIP, 0, 0, tiled=True)

    kids = sum_shares(at, kid_share, kid_rest, BF)
    first, second = two_way_gather(kids[:kid_blocks], kids[kid_blocks:], "y", "zh")

    targets = row_index * own_blocks + jnp.arange(own_blocks, dtype=jnp.int32)
    hit = child_map[:, None, :] == targets[None, :, None]
    there = jnp.any(hit, axis=2).astype(jnp.int32)
    source = jnp.sum(jnp.where(hit, jnp.arange(child_map.shape[1], dtype=jnp.int32), 0), axis=2)
    owner, place = source // kid_blocks, source % kid_blocks
    ring = (y - owner // 2) % 4
    pair = (zh - owner % 2) % 2
    origin = jnp.stack(
        [
            jnp.stack([pair[0], ring[0], place[0], there[0]]),
            jnp.stack([ring[1], pair[1], place[1], there[1]]),
        ]
    ).astype(jnp.int32)
    keep, send = extend_add(at, origin, own_share, own_rest, first, second)
    came = lax.ppermute(send, "core", swap)

    per = LEAF // BLOCK
    first = jnp.stack([keep[:per], came[:per]])
    second = jnp.stack([keep[per:], came[per:]])
    mine = two_way_gather(first, second, "x", "zl")
    gram, root, cross = grams(at, parent_front, mine, probes, chips)

    own_rows = jnp.where(
        core == 0,
        jnp.concatenate([keep, came], axis=2),
        jnp.concatenate([came, keep], axis=2),
    ).reshape(2, -1, 2 * half)

    cross = lax.all_to_all(cross.astype(jnp.float16), CHIP, 0, 0, tiled=True)
    cross = lax.dynamic_slice_in_dim(cross, row_index, 1, 0)
    work = factor_inverse(gram, 0, 3)
    work, cross = lax.optimization_barrier((work, cross))
    cross = lax.all_to_all(jnp.broadcast_to(cross, (chips, *cross.shape[1:])), CHIP, 0, 0, tiled=True)
    inverse = factor_inverse(work, 3, probes // STEP)
    inverse, cross = lax.optimization_barrier((inverse, cross))
    keep, send = finish(at, inverse, root, own_rows, cross.astype(F32))
    came = lax.ppermute(send, "core", swap)
    both = jnp.where(core == 0, jnp.concatenate([keep, came]), jnp.concatenate([came, keep]))
    tall = own_rows.shape[1] // 2
    leaf_basis = both[:, :tall].astype(BF).reshape(own_blocks, -1, probes)
    return (leaf_basis, both[:, tall:])


def solution(mesh):
    split = Mesh(mesh.devices.reshape(4, 2, 4, 2, 2), ("y", "zh", "x", "zl", "core"))
    placed = (P(ROW, COL), P(None, ROW, COL), P(COL, None), P(None, COL, None), P())
    return jax.shard_map(
        local,
        mesh=split,
        in_specs=placed,
        out_specs=(P(ROW, COL, None), P(ROW, COL, None)),
        check_vma=False,
    )
```

```python
import functools
import math

import jax
import jax.numpy as jnp
from jax import lax
from jax.experimental import pallas as pl
from jax.experimental.pallas import tpu as pltpu
from jax.sharding import Mesh
from jax.sharding import PartitionSpec as P

LEAF = 896
BLOCK = 128
ROW = ("y", "zh")
CHIP = ("x", "zl")
COL = ("x", "zl", "core")
F32 = jnp.float32
BF = jnp.bfloat16
SMEM = pl.BlockSpec(memory_space=pltpu.SMEM)
STEP = 64


def whole(array):
    return pl.BlockSpec(array.shape, lambda *_: (0,) * len(array.shape))


def params(mib):
    return pltpu.CompilerParams(vmem_limit_bytes=mib << 20)


def cost(flops, nbytes):
    return pl.CostEstimate(flops=int(flops), bytes_accessed=int(nbytes), transcendentals=0)


def probe_kernel(at_ref, a_ref, b_ref, sent_ref, kept_ref):
    total = contract(a_ref[0], b_ref[0], 1, 1)
    half = sent_ref.shape[2]
    low = total[:, :half]
    pad = jnp.zeros((total.shape[0], 2 * half - total.shape[1]), F32)
    high = jnp.concatenate([total[:, half:], pad], axis=1)
    first = at_ref[2] == 0
    kept_ref[0] = jnp.where(first, low, high)
    sent_ref[0] = jnp.where(first, high, low)


def probe(at, a, b, half):
    count, rows, depth = a.shape
    probes = b.shape[1]
    part = jax.ShapeDtypeStruct((count, rows, half), F32)
    return pl.pallas_call(
        probe_kernel,
        grid=(count, rows // LEAF),
        out_shape=[part, part],
        in_specs=[
            SMEM,
            pl.BlockSpec((1, LEAF, depth), lambda k, i: (k, i, 0)),
            pl.BlockSpec((1, probes, depth), lambda k, i: (k, 0, 0)),
        ],
        out_specs=[pl.BlockSpec((1, LEAF, half), lambda k, i: (k, i, 0))] * 2,
        compiler_params=params(40),
        cost_estimate=cost(4 * count * rows * depth * half, 2 * a.size + 8 * count * rows * half),
    )(at, a, b)


def pack_kernel(at_ref, a_ref, b_ref, o_ref, own_ref, sum_ref):
    total = a_ref[0] + b_ref[0]
    sum_ref[...] = total
    chips, blocks, rows, _ = o_ref.shape
    chip_here = at_ref[0] * 2 + at_ref[1]
    for block in range(blocks):
        for chip in range(chips):
            start = (block * chips + chip) * rows
            o_ref[chip, block] = total[start : start + rows].astype(BF)
        own = pl.multiple_of((block * chips + chip_here) * rows, rows)
        own_ref[block] = sum_ref[pl.ds(own, rows), :]


def pack(at, kept, received, chips):
    count, rows, half = kept.shape
    per = rows // LEAF
    blocks = LEAF // BLOCK
    slab = BLOCK // chips
    whole = count * rows // BLOCK
    return pl.pallas_call(
        pack_kernel,
        grid=(count, per),
        out_shape=[
            jax.ShapeDtypeStruct((chips, whole, slab, half), BF),
            jax.ShapeDtypeStruct((whole, slab, half), F32),
        ],
        in_specs=[
            SMEM,
            pl.BlockSpec((1, LEAF, half), lambda k, i: (k, i, 0)),
            pl.BlockSpec((1, LEAF, half), lambda k, i: (k, i, 0)),
        ],
        out_specs=[
            pl.BlockSpec((chips, blocks, slab, half), lambda k, i: (0, k * per + i, 0, 0)),
            pl.BlockSpec((blocks, slab, half), lambda k, i: (k * per + i, 0, 0)),
        ],
        scratch_shapes=[pltpu.VMEM((LEAF, half), F32)],
        compiler_params=params(24),
        cost_estimate=cost(kept.size, 10 * kept.size),
    )(at, kept, received)


def shift(value, axis, by):
    size = lax.axis_size(axis)
    return lax.ppermute(value, axis, [(i, (i + by) % size) for i in range(size)])


def ring_pieces(value, axis):
    return [value] + [shift(value, axis, by) for by in range(1, lax.axis_size(axis))]


def two_way_pieces(first, second, big, small):
    first_ring = jnp.stack(ring_pieces(first, big))
    second_pair = jnp.stack(ring_pieces(second, small))
    return ring_pieces(first_ring, small), ring_pieces(second_pair, big)


def sum_of(shares_ref, own, here, at):
    for chip in range(shares_ref.shape[0]):
        own += jnp.where(here != chip, shares_ref[(chip, *at)].astype(F32), 0.0)
    return own


def sum_kernel(at_ref, k_ref, own_ref, o_ref):
    here = at_ref[0] * 2 + at_ref[1]
    for block in range(o_ref.shape[0]):
        o_ref[block] = sum_of(k_ref, own_ref[block], here, (block,)).astype(o_ref.dtype)


def sum_shares(at, shares, own, dtype):
    chips, blocks, slab, half = shares.shape
    step = LEAF // BLOCK
    return pl.pallas_call(
        sum_kernel,
        grid=(blocks // step,),
        out_shape=jax.ShapeDtypeStruct(shares.shape[1:], dtype),
        in_specs=[
            SMEM,
            pl.BlockSpec((chips, step, slab, half), lambda i: (0, i, 0, 0)),
            pl.BlockSpec((step, slab, half), lambda i: (i, 0, 0)),
        ],
        out_specs=pl.BlockSpec((step, slab, half), lambda i: (i, 0, 0)),
        compiler_params=params(16),
        cost_estimate=cost(shares.size, 2 * shares.size),
    )(at, shares, own)


def extend_kernel(at_ref, from_ref, p_ref, own_ref, *refs):
    *kid_refs, keep_ref, send_ref, all_ref = refs
    here = at_ref[0] * 2 + at_ref[1]
    core = at_ref[2]
    step = pl.program_id(0)
    blocks = own_ref.shape[0]
    for block in range(blocks):
        total = sum_of(p_ref, own_ref[block], here, (block,))
        target = step * blocks + block
        for kid in range(2):
            ring, pair, place, there = (from_ref[kid, part, target] for part in range(4))
            for i, ref in enumerate(kid_refs):
                hit = (there > 0) & (ring == i)
                total += jnp.where(hit, ref[pair, kid, place].astype(F32), 0.0)
        all_ref[target] = total.astype(BF)

    @pl.when(step == pl.num_programs(0) - 1)
    def _():
        count = keep_ref.shape[0]
        keep_ref[...] = all_ref[pl.ds(core * count, count)]
        send_ref[...] = all_ref[pl.ds((1 - core) * count, count)]


def extend_add(at, source, parent, own, kids):
    chips, blocks, slab, half = parent.shape
    step = LEAF // BLOCK
    pair = jax.ShapeDtypeStruct((blocks // 2, slab, half), BF)
    return pl.pallas_call(
        extend_kernel,
        grid=(blocks // step,),
        out_shape=[pair, pair],
        in_specs=[
            SMEM,
            SMEM,
            pl.BlockSpec((chips, step, slab, half), lambda i: (0, i, 0, 0)),
            pl.BlockSpec((step, slab, half), lambda i: (i, 0, 0)),
        ]
        + [whole(piece) for piece in kids],
        out_specs=[whole(pair)] * 2,
        scratch_shapes=[pltpu.VMEM(parent.shape[1:], BF)],
        compiler_params=params(24),
        cost_estimate=cost(parent.size, 6 * parent.size),
    )(at, source, parent, own, *kids)


def halves(x):
    hi = x.astype(BF)
    return hi, (x - hi.astype(F32)).astype(BF)


def contract(a, b, left, right):
    return lax.dot_general(a, b, (((left,), (right,)), ((), ())), preferred_element_type=F32)


def product3(a, b):
    ah, al = halves(a)
    bh, bl = halves(b)
    return contract(ah, bh, 1, 0) + (contract(ah, bl, 1, 0) + contract(al, bh, 1, 0))


LEVEL = 8.0


def gram_kernel(at_ref, f_ref, *refs):
    a_refs, b_refs = refs[:2], refs[2:6]
    gram_ref, root_ref, cross_ref, y_ref, t_ref = refs[6:]
    x, zl, core = (at_ref[i] for i in range(3))
    step = pl.program_id(0)
    half = y_ref.shape[-1] // 2
    per = LEAF // BLOCK
    leaves, order, wide = gram_ref.shape
    row = lax.broadcasted_iota(jnp.int32, (order, wide), 0)
    col = lax.broadcasted_iota(jnp.int32, (order, wide), 1)
    lane = lax.broadcasted_iota(jnp.int32, (1, wide), 1)

    @pl.when(step == 0)
    def _():
        for side, owner in ((0, core), (1, 1 - core)):
            lanes = pl.ds(pl.multiple_of(owner * half, half), half)
            for i in range(4):
                for j in range(2):
                    chip = lax.rem(x + 4 - i, 4) * 2 + lax.rem(zl + j, 2)
                    rows = pl.ds(pl.multiple_of(chip * 16, 16), 16)
                    y_ref[:per, rows, lanes] = a_refs[j][i, side]
                    y_ref[per:, rows, lanes] = b_refs[i][j, side]
        for leaf in range(leaves):
            y = y_ref[leaf * per : (leaf + 1) * per].reshape(LEAF, wide)
            t_ref[leaf] = y.T[:order]
            gram = contract(t_ref[leaf], y, 1, 0)
            gram_ref[leaf] = gram
            square = jnp.sum(jnp.where(row == col, gram, 0.0), axis=0, keepdims=True)
            root_ref[leaf] = jnp.sqrt(jnp.where(lane < order, square, 1.0))

    here = t_ref[step]
    there = y_ref[pl.ds((1 - step) * per, per)].reshape(LEAF, wide)
    hi, lo = halves(jnp.dot(f_ref[...], there, preferred_element_type=F32) / root_ref[1 - step])
    cross = contract(here, hi, 1, 0) + contract(here, lo, 1, 0)
    square = jnp.sum(jnp.where(row == col, gram_ref[step], 0.0), axis=1, keepdims=True)
    cross = cross * lax.rsqrt(square)
    most = jnp.max(jnp.max(jnp.abs(cross), axis=0, keepdims=True), axis=1, keepdims=True)
    power = jnp.ceil(jnp.log2(jnp.maximum(most, 1e-30)))
    cross = jnp.where(col < order, cross * jnp.exp2(LEVEL - power), power)
    cross_ref[:, 0] = cross.reshape(cross_ref.shape[0], cross_ref.shape[2], wide)


def grams(at, front, mine, order, chips):
    half = mine[0].shape[-1]
    wide = 2 * half
    return pl.pallas_call(
        gram_kernel,
        grid_spec=pltpu.PrefetchScalarGridSpec(
            num_scalar_prefetch=1,
            grid=(2,),
            in_specs=[
                pl.BlockSpec((LEAF, LEAF), lambda i, at: (at[2] * 2 + i, 1 - i)),
            ]
            + [whole(piece) for piece in mine],
            out_specs=[
                pl.BlockSpec((2, order, wide), lambda i, at: (0, 0, 0)),
                pl.BlockSpec((2, 1, wide), lambda i, at: (0, 0, 0)),
                pl.BlockSpec((chips, 1, order // chips, wide), lambda i, at: (0, i, 0, 0)),
            ],
            scratch_shapes=[
                pltpu.VMEM((2 * LEAF // BLOCK, BLOCK, wide), BF),
                pltpu.VMEM((2, order, LEAF), BF),
            ],
        ),
        out_shape=[
            jax.ShapeDtypeStruct((2, order, wide), F32),
            jax.ShapeDtypeStruct((2, 1, wide), F32),
            jax.ShapeDtypeStruct((chips, 2, order // chips, wide), F32),
        ],
        compiler_params=params(52),
        cost_estimate=cost(2 * 8 * LEAF * wide * wide, 4 * LEAF * LEAF + 2 * leaves_bytes(wide)),
    )(at, front, *mine)


def leaves_bytes(wide):
    return 2 * LEAF * wide * 2


def eliminate(s, size):
    groups = size // 8
    shape = (8, 128)
    sub = lax.broadcasted_iota(jnp.int32, shape, 0)
    for g in range(groups):
        for rows in s:
            c = {
                (i, k): jnp.broadcast_to(rows[i][:, 8 * g + k : 8 * g + k + 1], shape)
                for i in range(g, groups)
                for k in range(8)
            }
            pivot = [jnp.broadcast_to(rows[g][k : k + 1, :], shape) for k in range(8)]
            d = {
                (i, k): jnp.broadcast_to(c[g, k][i : i + 1, :], shape)
                for i in range(8)
                for k in range(i, 8)
            }
            low = {}
            scaled = []
            for k in range(8):
                inverse = pl.reciprocal(d[k, k], approx=True)
                inverse = inverse * (2.0 - d[k, k] * inverse)
                scaled.append(pivot[k] * inverse)
                for i in range(k + 1, 8):
                    low[i, k] = d[k, i] * inverse
                    pivot[i] = pivot[i] - low[i, k] * pivot[k]
                    for m in range(i, 8):
                        d[i, m] = d[i, m] - low[i, k] * d[k, m]
            for m in reversed(range(8)):
                for k in range(m + 1, 8):
                    scaled[m] = scaled[m] - low[k, m] * scaled[k]
            for i in range(g + 1, groups):
                new = rows[i]
                for k in range(8):
                    new = new - c[i, k] * scaled[k]
                rows[i] = new
            new = pivot[0]
            for k in range(1, 8):
                new = jnp.where(sub == k, pivot[k], new)
            rows[g] = new


def inverse_kernel(a_ref, after_ref, w_ref, x_ref, d_ref, *, first, last):
    del after_ref
    leaves, order, wide = w_ref.shape
    blocks = order // STEP
    w_ref[...] = a_ref[...]
    lane = lax.broadcasted_iota(jnp.int32, (STEP, 128), 1)
    sub = lax.broadcasted_iota(jnp.int32, (STEP, 128), 0)
    col = lax.broadcasted_iota(jnp.int32, (STEP, wide), 1)
    row = lax.broadcasted_iota(jnp.int32, (STEP, wide), 0)
    unit = (lane - STEP == sub).astype(F32)

    def spread(k, live):
        base = pl.multiple_of(k * STEP, STEP)
        inside = (col >= base) & (col < base + STEP)
        own = (col - base == row).astype(F32)
        rest = (col >= base + STEP) & live
        for leaf in range(leaves):
            w = w_ref[leaf, pl.ds(base, STEP), :]
            r = product3(x_ref[leaf], jnp.where(inside, own, w))
            w_ref[leaf, pl.ds(base, STEP), :] = jnp.where(live, r, w)
            hi, lo = halves(r)
            none = jnp.zeros_like(hi)
            left_hi, left_lo = jnp.where(rest, hi, none), jnp.where(rest, lo, none)
            left = jnp.concatenate([left_hi, left_hi, left_lo], axis=0)
            update = contract(left, jnp.concatenate([hi, lo, hi], axis=0), 0, 0)
            for i in range(1, blocks):
                rows = slice(i * STEP, (i + 1) * STEP)
                old = jnp.where(inside & live & (i > k), 0.0, w_ref[leaf, rows, :])
                w_ref[leaf, rows, :] = old - update[rows]

    start, tile = first * STEP, first * STEP // 128 * 128
    for leaf in range(leaves):
        d = w_ref[leaf, start : start + STEP, tile : tile + 128]
        d_ref[leaf] = pltpu.roll(d, 128 - STEP, 1) if start > tile else d
        x_ref[leaf] = jnp.zeros((STEP, STEP), F32)

    @pl.loop(first, last)
    def _(k):
        s = []
        for leaf in range(leaves):
            d = jnp.where(lane < STEP, d_ref[leaf], unit)
            s.append([d[8 * i : 8 * i + 8] for i in range(STEP // 8)])
        spread(jnp.maximum(k - 1, 0), k > first)
        eliminate(s, STEP)
        base = pl.multiple_of(k * STEP, STEP)
        after = pl.multiple_of(jnp.minimum(k + 1, blocks - 1) * STEP, STEP)
        tile = pl.multiple_of(lax.div(after, 128) * 128, 128)
        odd = after - tile > 0
        for leaf in range(leaves):
            d = jnp.concatenate(s[leaf], axis=0)
            diagonal = jnp.sum(jnp.where(lane == sub, d, 0.0), axis=1, keepdims=True)
            x = (d * lax.rsqrt(diagonal))[:, STEP:]
            x_ref[leaf] = x
            hi, lo = halves(product3(x, w_ref[leaf, pl.ds(base, STEP), pl.ds(tile, 128)]))
            left = jnp.concatenate([hi, hi, lo], axis=0)
            update = contract(left, jnp.concatenate([hi, lo, hi], axis=0), 0, 0)
            update = jnp.where(odd, update[STEP:], update[:STEP])
            d = w_ref[leaf, pl.ds(after, STEP), pl.ds(tile, 128)] - update
            d_ref[leaf] = jnp.where(odd, pltpu.roll(d, 128 - STEP, 1), d)

    spread(last - 1, True)
    if last < blocks:
        return
    for leaf in range(leaves):
        for i in range(blocks):
            rows = slice(i * STEP, (i + 1) * STEP)
            w_ref[leaf, rows, :] = jnp.where(col <= row + i * STEP, w_ref[leaf, rows, :], 0.0)


def factor_inverse(work, after, first, last):
    leaves = work.shape[0]
    return pl.pallas_call(
        functools.partial(inverse_kernel, first=first, last=last),
        grid=(1,),
        out_shape=jax.ShapeDtypeStruct(work.shape, F32),
        in_specs=[whole(work), pl.BlockSpec(memory_space=pl.ANY)],
        out_specs=whole(work),
        scratch_shapes=[
            pltpu.VMEM((leaves, STEP, STEP), F32),
            pltpu.VMEM((leaves, STEP, 128), F32),
        ],
        compiler_params=params(24),
        cost_estimate=cost((last - first) * 5.5e9, 8 * work.size),
    )(work, after)


def finish_kernel(at_ref, w_ref, root_ref, own_ref, cross_ref, keep_ref, send_ref):
    leaves, order, wide = w_ref.shape
    slabs = LEAF // BLOCK
    rows = order // cross_ref.shape[0]
    base = pl.multiple_of((at_ref[0] * 2 + at_ref[1]) * rows, 8)
    first = at_ref[2] == 0
    tall = own_ref.shape[1] // 2
    for leaf in range(leaves):
        hi, lo = halves(w_ref[leaf])
        own = own_ref[leaf]
        basis = (contract(own, hi, 1, 1) + contract(own, lo, 1, 1)) * math.sqrt(LEAF)
        parts = basis.reshape(slabs, 2, tall // slabs, order)
        low, high = parts[:, 0].reshape(tall, order), parts[:, 1].reshape(tall, order)
        keep_ref[leaf, :tall] = jnp.where(first, low, high)
        send_ref[leaf, :tall] = jnp.where(first, high, low)
        left = w_ref[leaf, pl.ds(base, rows), :] * root_ref[leaf]
        cross = cross_ref[:, leaf].reshape(order, wide)
        level = jnp.exp2(cross[:1, order : order + 1] - LEVEL)
        half_way, rest = halves(product3(left[:, :order], cross))
        hi, lo = halves(w_ref[1 - leaf] * root_ref[1 - leaf])
        core = contract(half_way, hi, 1, 1) + (contract(half_way, lo, 1, 1) + contract(rest, hi, 1, 1))
        core = core * level
        low, high = core[: rows // 2], core[rows // 2 :]
        keep_ref[leaf, tall:] = jnp.where(first, low, high)
        send_ref[leaf, tall:] = jnp.where(first, high, low)


def finish(at, inverse, root, own, cross):
    leaves, order, _ = inverse.shape
    rows = (own.shape[1] + order // cross.shape[0]) // 2
    part = jax.ShapeDtypeStruct((leaves, rows, order), F32)
    return pl.pallas_call(
        finish_kernel,
        grid=(1,),
        out_shape=[part, part],
        in_specs=[SMEM, whole(inverse), whole(root), whole(own), whole(cross)],
        out_specs=[whole(part)] * 2,
        compiler_params=params(24),
        cost_estimate=cost(2e9, 4 * (inverse.size + cross.size)),
    )(at, inverse, root, own, cross)


def local(parent_front, child_update, parent_test, child_test, child_map):
    y, zh = lax.axis_index("y"), lax.axis_index("zh")
    x, zl, core = lax.axis_index("x"), lax.axis_index("zl"), lax.axis_index("core")
    row_index = lax.axis_index(ROW)
    probes = parent_test.shape[1]
    half = 256
    chips = lax.axis_size(CHIP)
    own_blocks = parent_front.shape[0] // BLOCK
    kid_blocks = child_update.shape[1] // BLOCK
    swap = [(0, 1), (1, 0)]

    at = jnp.stack([x, zl, core]).astype(jnp.int32)
    kid_sent, kid_kept = probe(at, child_update, jnp.swapaxes(child_test, 1, 2), half)
    kid_sent = lax.ppermute(kid_sent, "core", swap)
    own_sent, own_kept = probe(at, parent_front[None], parent_test.T[None], half)
    own_sent = lax.ppermute(own_sent, "core", swap)
    kid_part, kid_rest = pack(at, kid_kept, kid_sent, chips)
    kid_share = lax.all_to_all(kid_part, CHIP, 0, 0, tiled=True)
    own_part, own_rest = pack(at, own_kept, own_sent, chips)

    kids = sum_shares(at, kid_share, kid_rest, BF).reshape(2, kid_blocks, -1, half)
    pair = ring_pieces(kids, "zh")
    pair[1], own_part = lax.optimization_barrier((pair[1], own_part))
    pair = jnp.stack(pair)
    own_share = lax.all_to_all(own_part, CHIP, 0, 0, tiled=True)
    reach = [(0, 1), (0, 2), (1, 0), (1, 2), (2, 1), (2, 3), (3, 1), (3, 2)]
    kid_pieces = [pair] + [
        lax.ppermute(pair, "y", [(i, j) for i, j in reach if (j - i) % 4 == by])
        for by in range(1, 4)
    ]

    targets = row_index * own_blocks + jnp.arange(own_blocks, dtype=jnp.int32)
    hit = child_map[:, None, :] == targets[None, :, None]
    there = jnp.any(hit, axis=2).astype(jnp.int32)
    source = jnp.sum(jnp.where(hit, jnp.arange(child_map.shape[1], dtype=jnp.int32), 0), axis=2)
    owner, place = source // kid_blocks, source % kid_blocks
    ring = (y - owner // 2) % 4
    pair_of = (zh - owner % 2) % 2
    origin = jnp.stack([ring, pair_of, place, there], axis=1).astype(jnp.int32)
    keep, send = extend_add(at, origin, own_share, own_rest, kid_pieces)
    came = lax.ppermute(send, "core", swap)

    per = LEAF // BLOCK
    first = jnp.stack([keep[:per], came[:per]])
    second = jnp.stack([keep[per:], came[per:]])
    firsts, seconds = two_way_pieces(first, second, "x", "zl")
    gram, root, cross = grams(at, parent_front, firsts + seconds, probes, chips)

    own_rows = jnp.where(
        core == 0,
        jnp.concatenate([keep, came], axis=2),
        jnp.concatenate([came, keep], axis=2),
    ).reshape(2, -1, 2 * half)

    cross = lax.all_to_all(cross.astype(jnp.float16), CHIP, 0, 0, tiled=True)
    ready = lax.dynamic_slice_in_dim(cross, row_index, 1, 0)
    work = factor_inverse(gram, own_rows, 0, 3)
    cross = lax.all_to_all(jnp.broadcast_to(ready, (chips, *ready.shape[1:])), CHIP, 0, 0, tiled=True)
    inverse = factor_inverse(work, ready[0, 0, :8, :128].astype(F32), 3, probes // STEP)
    keep, send = finish(at, inverse, root, own_rows, cross.astype(F32))
    came = lax.ppermute(send, "core", swap)
    both = jnp.where(core == 0, jnp.concatenate([keep, came]), jnp.concatenate([came, keep]))
    tall = own_rows.shape[1] // 2
    leaf_basis = both[:, :tall].astype(BF).reshape(own_blocks, -1, probes)
    return (leaf_basis, both[:, tall:])


def solution(mesh):
    split = Mesh(mesh.devices.reshape(4, 2, 4, 2, 2), ("y", "zh", "x", "zl", "core"))
    placed = (P(ROW, COL), P(None, ROW, COL), P(COL, None), P(None, COL, None), P())
    return jax.shard_map(
        local,
        mesh=split,
        in_specs=placed,
        out_specs=(P(ROW, COL, None), P(ROW, COL, None)),
        check_vma=False,
    )
```

```python
import functools
import math

import jax
import jax.numpy as jnp
from jax import lax
from jax.experimental import pallas as pl
from jax.experimental.pallas import tpu as pltpu
from jax.sharding import Mesh
from jax.sharding import PartitionSpec as P

LEAF = 896
BLOCK = 128
ROW = ("y", "zh")
CHIP = ("x", "zl")
COL = ("x", "zl", "core")
F32 = jnp.float32
BF = jnp.bfloat16
SMEM = pl.BlockSpec(memory_space=pltpu.SMEM)
STEP = 64


def whole(array):
    return pl.BlockSpec(array.shape, lambda *_: (0,) * len(array.shape))


def params(mib):
    return pltpu.CompilerParams(vmem_limit_bytes=mib << 20)


def cost(flops, nbytes):
    return pl.CostEstimate(flops=int(flops), bytes_accessed=int(nbytes), transcendentals=0)


def probe_kernel(at_ref, a_ref, b_ref, sent_ref, kept_ref):
    total = contract(a_ref[0], b_ref[0], 1, 1)
    half = sent_ref.shape[2]
    low = total[:, :half]
    pad = jnp.zeros((total.shape[0], 2 * half - total.shape[1]), F32)
    high = jnp.concatenate([total[:, half:], pad], axis=1)
    first = at_ref[2] == 0
    kept_ref[0] = jnp.where(first, low, high)
    sent_ref[0] = jnp.where(first, high, low)


def probe(at, a, b, half, tall):
    count, rows, depth = a.shape
    probes = b.shape[1]
    part = jax.ShapeDtypeStruct((count, rows, half), F32)
    return pl.pallas_call(
        probe_kernel,
        grid=(count, rows // tall),
        out_shape=[part, part],
        in_specs=[
            SMEM,
            pl.BlockSpec((1, tall, depth), lambda k, i: (k, i, 0)),
            pl.BlockSpec((1, probes, depth), lambda k, i: (k, 0, 0)),
        ],
        out_specs=[pl.BlockSpec((1, tall, half), lambda k, i: (k, i, 0))] * 2,
        compiler_params=params(56),
        cost_estimate=cost(4 * count * rows * depth * half, 2 * a.size + 8 * count * rows * half),
    )(at, a, b)


def pack_kernel(at_ref, a_ref, b_ref, o_ref, own_ref, sum_ref):
    total = a_ref[0] + b_ref[0]
    sum_ref[...] = total
    chips, blocks, rows, _ = o_ref.shape
    chip_here = at_ref[0] * 2 + at_ref[1]
    for block in range(blocks):
        for chip in range(chips):
            start = (block * chips + chip) * rows
            o_ref[chip, block] = total[start : start + rows].astype(BF)
        own = pl.multiple_of((block * chips + chip_here) * rows, rows)
        own_ref[block] = sum_ref[pl.ds(own, rows), :]


def pack(at, kept, received, chips):
    count, rows, half = kept.shape
    per = rows // LEAF
    blocks = LEAF // BLOCK
    slab = BLOCK // chips
    whole = count * rows // BLOCK
    return pl.pallas_call(
        pack_kernel,
        grid=(count, per),
        out_shape=[
            jax.ShapeDtypeStruct((chips, whole, slab, half), BF),
            jax.ShapeDtypeStruct((whole, slab, half), F32),
        ],
        in_specs=[
            SMEM,
            pl.BlockSpec((1, LEAF, half), lambda k, i: (k, i, 0)),
            pl.BlockSpec((1, LEAF, half), lambda k, i: (k, i, 0)),
        ],
        out_specs=[
            pl.BlockSpec((chips, blocks, slab, half), lambda k, i: (0, k * per + i, 0, 0)),
            pl.BlockSpec((blocks, slab, half), lambda k, i: (k * per + i, 0, 0)),
        ],
        scratch_shapes=[pltpu.VMEM((LEAF, half), F32)],
        compiler_params=params(56),
        cost_estimate=cost(kept.size, 10 * kept.size),
    )(at, kept, received)


def shift(value, axis, by):
    size = lax.axis_size(axis)
    return lax.ppermute(value, axis, [(i, (i + by) % size) for i in range(size)])


def ring_pieces(value, axis):
    return [value] + [shift(value, axis, by) for by in range(1, lax.axis_size(axis))]


def two_way_pieces(first, second, big, small):
    first_ring = jnp.stack(ring_pieces(first, big))
    second_pair = jnp.stack(ring_pieces(second, small))
    return ring_pieces(first_ring, small), ring_pieces(second_pair, big)


def sum_of(shares_ref, own, here, at):
    for chip in range(shares_ref.shape[0]):
        own += jnp.where(here != chip, shares_ref[(chip, *at)].astype(F32), 0.0)
    return own


def sum_kernel(at_ref, k_ref, own_ref, o_ref):
    here = at_ref[0] * 2 + at_ref[1]
    for block in range(o_ref.shape[0]):
        o_ref[block] = sum_of(k_ref, own_ref[block], here, (block,)).astype(o_ref.dtype)


def sum_shares(at, shares, own, dtype):
    chips, blocks, slab, half = shares.shape
    step = LEAF // BLOCK
    return pl.pallas_call(
        sum_kernel,
        grid=(blocks // step,),
        out_shape=jax.ShapeDtypeStruct(shares.shape[1:], dtype),
        in_specs=[
            SMEM,
            pl.BlockSpec((chips, step, slab, half), lambda i: (0, i, 0, 0)),
            pl.BlockSpec((step, slab, half), lambda i: (i, 0, 0)),
        ],
        out_specs=pl.BlockSpec((step, slab, half), lambda i: (i, 0, 0)),
        compiler_params=params(56),
        cost_estimate=cost(shares.size, 2 * shares.size),
    )(at, shares, own)


def extend_kernel(at_ref, from_ref, p_ref, own_ref, *refs):
    *kid_refs, keep_ref, send_ref, all_ref = refs
    here = at_ref[0] * 2 + at_ref[1]
    core = at_ref[2]
    step = pl.program_id(0)
    blocks = own_ref.shape[0]
    for block in range(blocks):
        total = sum_of(p_ref, own_ref[block], here, (block,))
        target = step * blocks + block
        for kid in range(2):
            ring, pair, place, there = (from_ref[kid, part, target] for part in range(4))
            for i, ref in enumerate(kid_refs):
                hit = (there > 0) & (ring == i)
                total += jnp.where(hit, ref[pair, kid, place].astype(F32), 0.0)
        all_ref[target] = total.astype(BF)

    @pl.when(step == pl.num_programs(0) - 1)
    def _():
        count = keep_ref.shape[0]
        keep_ref[...] = all_ref[pl.ds(core * count, count)]
        send_ref[...] = all_ref[pl.ds((1 - core) * count, count)]


def extend_add(at, source, parent, own, kids):
    chips, blocks, slab, half = parent.shape
    step = LEAF // BLOCK
    pair = jax.ShapeDtypeStruct((blocks // 2, slab, half), BF)
    return pl.pallas_call(
        extend_kernel,
        grid=(blocks // step,),
        out_shape=[pair, pair],
        in_specs=[
            SMEM,
            SMEM,
            pl.BlockSpec((chips, step, slab, half), lambda i: (0, i, 0, 0)),
            pl.BlockSpec((step, slab, half), lambda i: (i, 0, 0)),
        ]
        + [whole(piece) for piece in kids],
        out_specs=[whole(pair)] * 2,
        scratch_shapes=[pltpu.VMEM(parent.shape[1:], BF)],
        compiler_params=params(24),
        cost_estimate=cost(parent.size, 6 * parent.size),
    )(at, source, parent, own, *kids)


def halves(x):
    hi = x.astype(BF)
    return hi, (x - hi.astype(F32)).astype(BF)


def contract(a, b, left, right):
    return lax.dot_general(a, b, (((left,), (right,)), ((), ())), preferred_element_type=F32)


def product3(a, b):
    ah, al = halves(a)
    bh, bl = halves(b)
    return contract(ah, bh, 1, 0) + (contract(ah, bl, 1, 0) + contract(al, bh, 1, 0))


LEVEL = 8.0


def gram_kernel(at_ref, f_ref, *refs):
    a_refs, b_refs = refs[:2], refs[2:6]
    gram_ref, root_ref, cross_ref, y_ref, t_ref = refs[6:]
    x, zl, core = (at_ref[i] for i in range(3))
    step = pl.program_id(0)
    half = y_ref.shape[-1] // 2
    per = LEAF // BLOCK
    leaves, order, wide = gram_ref.shape
    row = lax.broadcasted_iota(jnp.int32, (order, wide), 0)
    col = lax.broadcasted_iota(jnp.int32, (order, wide), 1)
    lane = lax.broadcasted_iota(jnp.int32, (1, wide), 1)

    @pl.when(step == 0)
    def _():
        for side, owner in ((0, core), (1, 1 - core)):
            lanes = pl.ds(pl.multiple_of(owner * half, half), half)
            for i in range(4):
                for j in range(2):
                    chip = lax.rem(x + 4 - i, 4) * 2 + lax.rem(zl + j, 2)
                    rows = pl.ds(pl.multiple_of(chip * 16, 16), 16)
                    y_ref[:per, rows, lanes] = a_refs[j][i, side]
                    y_ref[per:, rows, lanes] = b_refs[i][j, side]
        for leaf in range(leaves):
            y = y_ref[leaf * per : (leaf + 1) * per].reshape(LEAF, wide)
            t_ref[leaf] = y.T[:order]
            gram = contract(t_ref[leaf], y, 1, 0)
            gram_ref[leaf] = gram
            square = jnp.sum(jnp.where(row == col, gram, 0.0), axis=0, keepdims=True)
            root_ref[leaf] = jnp.sqrt(jnp.where(lane < order, square, 1.0))

    here = t_ref[step]
    there = y_ref[pl.ds((1 - step) * per, per)].reshape(LEAF, wide)
    hi, lo = halves(jnp.dot(f_ref[...], there, preferred_element_type=F32) * (1.0 / root_ref[1 - step]))
    cross = contract(here, hi, 1, 0) + contract(here, lo, 1, 0)
    square = jnp.sum(jnp.where(row == col, gram_ref[step], 0.0), axis=1, keepdims=True)
    cross = cross * lax.rsqrt(square)
    most = jnp.max(jnp.max(jnp.abs(cross), axis=0, keepdims=True), axis=1, keepdims=True)
    power = jnp.ceil(jnp.log2(jnp.maximum(most, 1e-30)))
    cross = jnp.where(col < order, cross * jnp.exp2(LEVEL - power), power)
    cross_ref[:, 0] = cross.reshape(cross_ref.shape[0], cross_ref.shape[2], wide)


def grams(at, front, mine, order, chips):
    half = mine[0].shape[-1]
    wide = 2 * half
    return pl.pallas_call(
        gram_kernel,
        grid_spec=pltpu.PrefetchScalarGridSpec(
            num_scalar_prefetch=1,
            grid=(2,),
            in_specs=[
                pl.BlockSpec((LEAF, LEAF), lambda i, at: (at[2] * 2 + i, 1 - i)),
            ]
            + [whole(piece) for piece in mine],
            out_specs=[
                pl.BlockSpec((2, order, wide), lambda i, at: (0, 0, 0)),
                pl.BlockSpec((2, 1, wide), lambda i, at: (0, 0, 0)),
                pl.BlockSpec((chips, 1, order // chips, wide), lambda i, at: (0, i, 0, 0)),
            ],
            scratch_shapes=[
                pltpu.VMEM((2 * LEAF // BLOCK, BLOCK, wide), BF),
                pltpu.VMEM((2, order, LEAF), BF),
            ],
        ),
        out_shape=[
            jax.ShapeDtypeStruct((2, order, wide), F32),
            jax.ShapeDtypeStruct((2, 1, wide), F32),
            jax.ShapeDtypeStruct((chips, 2, order // chips, wide), F32),
        ],
        compiler_params=params(52),
        cost_estimate=cost(2 * 8 * LEAF * wide * wide, 4 * LEAF * LEAF + 2 * leaves_bytes(wide)),
    )(at, front, *mine)


def leaves_bytes(wide):
    return 2 * LEAF * wide * 2


def eliminate(s, size):
    groups = size // 8
    shape = (8, 128)
    sub = lax.broadcasted_iota(jnp.int32, shape, 0)
    for g in range(groups):
        for rows in s:
            c = {
                (i, k): jnp.broadcast_to(rows[i][:, 8 * g + k : 8 * g + k + 1], shape)
                for i in range(g, groups)
                for k in range(8)
            }
            pivot = [jnp.broadcast_to(rows[g][k : k + 1, :], shape) for k in range(8)]
            d = {
                (i, k): jnp.broadcast_to(c[g, k][i : i + 1, :], shape)
                for i in range(8)
                for k in range(i, 8)
            }
            low = {}
            scaled = []
            for k in range(8):
                inverse = pl.reciprocal(d[k, k], approx=True)
                inverse = inverse * (2.0 - d[k, k] * inverse)
                scaled.append(pivot[k] * inverse)
                for i in range(k + 1, 8):
                    low[i, k] = d[k, i] * inverse
                    pivot[i] = pivot[i] - low[i, k] * pivot[k]
                    for m in range(i, 8):
                        d[i, m] = d[i, m] - low[i, k] * d[k, m]
            for m in reversed(range(8)):
                for k in range(m + 1, 8):
                    scaled[m] = scaled[m] - low[k, m] * scaled[k]
            for i in range(g + 1, groups):
                terms = [c[i, k] * scaled[k] for k in range(8)]
                while len(terms) > 1:
                    terms = [a + b for a, b in zip(terms[::2], terms[1::2])]
                rows[i] = rows[i] - terms[0]
            new = pivot[0]
            for k in range(1, 8):
                new = jnp.where(sub == k, pivot[k], new)
            rows[g] = new


def inverse_kernel(a_ref, after_ref, w_ref, x_ref, d_ref, *, first, last):
    del after_ref
    leaves, order, wide = w_ref.shape
    blocks = order // STEP
    w_ref[...] = a_ref[...]
    lane = lax.broadcasted_iota(jnp.int32, (STEP, 128), 1)
    sub = lax.broadcasted_iota(jnp.int32, (STEP, 128), 0)
    col = lax.broadcasted_iota(jnp.int32, (STEP, wide), 1)
    row = lax.broadcasted_iota(jnp.int32, (STEP, wide), 0)
    unit = (lane - STEP == sub).astype(F32)

    def spread(k, live):
        base = pl.multiple_of(k * STEP, STEP)
        inside = (col >= base) & (col < base + STEP)
        own = (col - base == row).astype(F32)
        rest = (col >= base + STEP) & live
        for leaf in range(leaves):
            w = w_ref[leaf, pl.ds(base, STEP), :]
            r = product3(x_ref[leaf], jnp.where(inside, own, w))
            w_ref[leaf, pl.ds(base, STEP), :] = jnp.where(live, r, w)
            hi, lo = halves(r)
            none = jnp.zeros_like(hi)
            left_hi, left_lo = jnp.where(rest, hi, none), jnp.where(rest, lo, none)
            left = jnp.concatenate([left_hi, left_hi, left_lo], axis=0)
            update = contract(left, jnp.concatenate([hi, lo, hi], axis=0), 0, 0)
            for i in range(1, blocks):
                rows = slice(i * STEP, (i + 1) * STEP)
                old = jnp.where(inside & live & (i > k), 0.0, w_ref[leaf, rows, :])
                w_ref[leaf, rows, :] = old - update[rows]

    start, tile = first * STEP, first * STEP // 128 * 128
    for leaf in range(leaves):
        d = w_ref[leaf, start : start + STEP, tile : tile + 128]
        d_ref[leaf] = pltpu.roll(d, 128 - STEP, 1) if start > tile else d
        x_ref[leaf] = jnp.zeros((STEP, STEP), F32)

    @pl.loop(first, last)
    def _(k):
        s = []
        for leaf in range(leaves):
            d = jnp.where(lane < STEP, d_ref[leaf], unit)
            s.append([d[8 * i : 8 * i + 8] for i in range(STEP // 8)])
        spread(jnp.maximum(k - 1, 0), k > first)
        eliminate(s, STEP)
        base = pl.multiple_of(k * STEP, STEP)
        after = pl.multiple_of(jnp.minimum(k + 1, blocks - 1) * STEP, STEP)
        tile = pl.multiple_of(lax.div(after, 128) * 128, 128)
        odd = after - tile > 0
        for leaf in range(leaves):
            d = jnp.concatenate(s[leaf], axis=0)
            diagonal = jnp.sum(jnp.where(lane == sub, d, 0.0), axis=1, keepdims=True)
            x = (d * lax.rsqrt(diagonal))[:, STEP:]
            x_ref[leaf] = x
            hi, lo = halves(product3(x, w_ref[leaf, pl.ds(base, STEP), pl.ds(tile, 128)]))
            left = jnp.concatenate([hi, hi, lo], axis=0)
            update = contract(left, jnp.concatenate([hi, lo, hi], axis=0), 0, 0)
            update = jnp.where(odd, update[STEP:], update[:STEP])
            d = w_ref[leaf, pl.ds(after, STEP), pl.ds(tile, 128)] - update
            d_ref[leaf] = jnp.where(odd, pltpu.roll(d, 128 - STEP, 1), d)

    spread(last - 1, True)
    if last < blocks:
        return
    for leaf in range(leaves):
        for i in range(blocks):
            rows = slice(i * STEP, (i + 1) * STEP)
            w_ref[leaf, rows, :] = jnp.where(col <= row + i * STEP, w_ref[leaf, rows, :], 0.0)


def factor_inverse(work, after, first, last):
    leaves = work.shape[0]
    return pl.pallas_call(
        functools.partial(inverse_kernel, first=first, last=last),
        grid=(1,),
        out_shape=jax.ShapeDtypeStruct(work.shape, F32),
        in_specs=[whole(work), pl.BlockSpec(memory_space=pl.ANY)],
        out_specs=whole(work),
        scratch_shapes=[
            pltpu.VMEM((leaves, STEP, STEP), F32),
            pltpu.VMEM((leaves, STEP, 128), F32),
        ],
        compiler_params=params(56),
        cost_estimate=cost((last - first) * 5.5e9, 8 * work.size),
    )(work, after)


def finish_kernel(at_ref, w_ref, root_ref, own_ref, cross_ref, keep_ref, send_ref):
    leaves, order, wide = w_ref.shape
    slabs = LEAF // BLOCK
    rows = order // cross_ref.shape[0]
    base = pl.multiple_of((at_ref[0] * 2 + at_ref[1]) * rows, 8)
    first = at_ref[2] == 0
    tall = own_ref.shape[1] // 2
    for leaf in range(leaves):
        hi, lo = halves(w_ref[leaf])
        own = own_ref[leaf]
        basis = (contract(own, hi, 1, 1) + contract(own, lo, 1, 1)) * math.sqrt(LEAF)
        parts = basis.reshape(slabs, 2, tall // slabs, order)
        low, high = parts[:, 0].reshape(tall, order), parts[:, 1].reshape(tall, order)
        keep_ref[leaf, :tall] = jnp.where(first, low, high)
        send_ref[leaf, :tall] = jnp.where(first, high, low)
        left = w_ref[leaf, pl.ds(base, rows), :] * root_ref[leaf]
        cross = cross_ref[:, leaf].reshape(order, wide)
        level = jnp.exp2(cross[:1, order : order + 1] - LEVEL)
        half_way, rest = halves(product3(left[:, :order], cross))
        hi, lo = halves(w_ref[1 - leaf] * root_ref[1 - leaf])
        core = contract(half_way, hi, 1, 1) + (contract(half_way, lo, 1, 1) + contract(rest, hi, 1, 1))
        core = core * level
        low, high = core[: rows // 2], core[rows // 2 :]
        keep_ref[leaf, tall:] = jnp.where(first, low, high)
        send_ref[leaf, tall:] = jnp.where(first, high, low)


def finish(at, inverse, root, own, cross):
    leaves, order, _ = inverse.shape
    rows = (own.shape[1] + order // cross.shape[0]) // 2
    part = jax.ShapeDtypeStruct((leaves, rows, order), F32)
    return pl.pallas_call(
        finish_kernel,
        grid=(1,),
        out_shape=[part, part],
        in_specs=[SMEM, whole(inverse), whole(root), whole(own), whole(cross)],
        out_specs=[whole(part)] * 2,
        compiler_params=params(24),
        cost_estimate=cost(2e9, 4 * (inverse.size + cross.size)),
    )(at, inverse, root, own, cross)


def local(parent_front, child_update, parent_test, child_test, child_map):
    y, zh = lax.axis_index("y"), lax.axis_index("zh")
    x, zl, core = lax.axis_index("x"), lax.axis_index("zl"), lax.axis_index("core")
    row_index = lax.axis_index(ROW)
    probes = parent_test.shape[1]
    half = 256
    chips = lax.axis_size(CHIP)
    own_blocks = parent_front.shape[0] // BLOCK
    kid_blocks = child_update.shape[1] // BLOCK
    swap = [(0, 1), (1, 0)]

    at = jnp.stack([x, zl, core]).astype(jnp.int32)
    kid_sent, kid_kept = probe(at, child_update, jnp.swapaxes(child_test, 1, 2), half, 2 * LEAF)
    kid_sent = lax.ppermute(kid_sent, "core", swap)
    own_sent, own_kept = probe(at, parent_front[None], parent_test.T[None], half, LEAF)
    own_sent = lax.ppermute(own_sent, "core", swap)
    kid_part, kid_rest = pack(at, kid_kept, kid_sent, chips)
    kid_share = lax.all_to_all(kid_part, CHIP, 0, 0, tiled=True)
    own_part, own_rest = pack(at, own_kept, own_sent, chips)

    kids = sum_shares(at, kid_share, kid_rest, BF).reshape(2, kid_blocks, -1, half)
    pair = ring_pieces(kids, "zh")
    pair = jnp.stack(pair)
    own_share = lax.all_to_all(own_part, CHIP, 0, 0, tiled=True)
    reach = [(0, 1), (0, 2), (1, 0), (1, 2), (2, 1), (2, 3), (3, 1), (3, 2)]
    kid_pieces = [pair] + [
        lax.ppermute(pair, "y", [(i, j) for i, j in reach if (j - i) % 4 == by])
        for by in range(1, 4)
    ]

    targets = row_index * own_blocks + jnp.arange(own_blocks, dtype=jnp.int32)
    hit = child_map[:, None, :] == targets[None, :, None]
    there = jnp.any(hit, axis=2).astype(jnp.int32)
    source = jnp.sum(jnp.where(hit, jnp.arange(child_map.shape[1], dtype=jnp.int32), 0), axis=2)
    owner, place = source // kid_blocks, source % kid_blocks
    ring = (y - owner // 2) % 4
    pair_of = (zh - owner % 2) % 2
    origin = jnp.stack([ring, pair_of, place, there], axis=1).astype(jnp.int32)
    keep, send = extend_add(at, origin, own_share, own_rest, kid_pieces)
    came = lax.ppermute(send, "core", swap)

    per = LEAF // BLOCK
    first = jnp.stack([keep[:per], came[:per]])
    second = jnp.stack([keep[per:], came[per:]])
    firsts, seconds = two_way_pieces(first, second, "x", "zl")
    gram, root, cross = grams(at, parent_front, firsts + seconds, probes, chips)

    own_rows = jnp.where(
        core == 0,
        jnp.concatenate([keep, came], axis=2),
        jnp.concatenate([came, keep], axis=2),
    ).reshape(2, -1, 2 * half)

    cross = lax.all_to_all(cross.astype(jnp.float16), CHIP, 0, 0, tiled=True)
    ready = lax.dynamic_slice_in_dim(cross, row_index, 1, 0)
    work = factor_inverse(gram, own_rows, 0, 3)
    cross = lax.all_to_all(jnp.broadcast_to(ready, (chips, *ready.shape[1:])), CHIP, 0, 0, tiled=True)
    inverse = factor_inverse(work, ready[0, 0, :8, :128].astype(F32), 3, probes // STEP)
    keep, send = finish(at, inverse, root, own_rows, cross.astype(F32))
    came = lax.ppermute(send, "core", swap)
    both = jnp.where(core == 0, jnp.concatenate([keep, came]), jnp.concatenate([came, keep]))
    tall = own_rows.shape[1] // 2
    leaf_basis = both[:, :tall].astype(BF).reshape(own_blocks, -1, probes)
    return (leaf_basis, both[:, tall:])


def solution(mesh):
    split = Mesh(mesh.devices.reshape(4, 2, 4, 2, 2), ("y", "zh", "x", "zl", "core"))
    placed = (P(ROW, COL), P(None, ROW, COL), P(COL, None), P(None, COL, None), P())
    return jax.shard_map(
        local,
        mesh=split,
        in_specs=placed,
        out_specs=(P(ROW, COL, None), P(ROW, COL, None)),
        check_vma=False,
    )
```

```python
import functools
import math

import jax
import jax.numpy as jnp
from jax import lax
from jax.experimental import pallas as pl
from jax.experimental.pallas import tpu as pltpu
from jax.sharding import Mesh
from jax.sharding import PartitionSpec as P

LEAF = 896
BLOCK = 128
ROW = ("y", "zh")
CHIP = ("x", "zl")
COL = ("x", "zl", "core")
F32 = jnp.float32
BF = jnp.bfloat16
SMEM = pl.BlockSpec(memory_space=pltpu.SMEM)
STEP = 64


def whole(array):
    return pl.BlockSpec(array.shape, lambda *_: (0,) * len(array.shape))


def params(mib):
    return pltpu.CompilerParams(vmem_limit_bytes=mib << 20)


def cost(flops, nbytes):
    return pl.CostEstimate(flops=int(flops), bytes_accessed=int(nbytes), transcendentals=0)


def probe_kernel(at_ref, a_ref, b_ref, sent_ref, kept_ref):
    total = contract(a_ref[0], b_ref[0], 1, 1)
    half = sent_ref.shape[2]
    low = total[:, :half]
    pad = jnp.zeros((total.shape[0], 2 * half - total.shape[1]), F32)
    high = jnp.concatenate([total[:, half:], pad], axis=1)
    first = at_ref[2] == 0
    kept_ref[0] = jnp.where(first, low, high)
    sent_ref[0] = jnp.where(first, high, low)


def probe(at, a, b, half):
    count, rows, depth = a.shape
    probes = b.shape[1]
    part = jax.ShapeDtypeStruct((count, rows, half), F32)
    return pl.pallas_call(
        probe_kernel,
        grid=(count, rows // LEAF),
        out_shape=[part, part],
        in_specs=[
            SMEM,
            pl.BlockSpec((1, LEAF, depth), lambda k, i: (k, i, 0)),
            pl.BlockSpec((1, probes, depth), lambda k, i: (k, 0, 0)),
        ],
        out_specs=[pl.BlockSpec((1, LEAF, half), lambda k, i: (k, i, 0))] * 2,
        compiler_params=params(40),
        cost_estimate=cost(4 * count * rows * depth * half, 2 * a.size + 8 * count * rows * half),
    )(at, a, b)


def pack_kernel(at_ref, a_ref, b_ref, o_ref, own_ref, sum_ref):
    total = a_ref[0] + b_ref[0]
    sum_ref[...] = total
    chips, blocks, rows, _ = o_ref.shape
    chip_here = at_ref[0] * 2 + at_ref[1]
    for block in range(blocks):
        for chip in range(chips):
            start = (block * chips + chip) * rows
            o_ref[chip, block] = total[start : start + rows].astype(BF)
        own = pl.multiple_of((block * chips + chip_here) * rows, rows)
        own_ref[block] = sum_ref[pl.ds(own, rows), :]


def pack(at, kept, received, chips):
    count, rows, half = kept.shape
    per = rows // LEAF
    blocks = LEAF // BLOCK
    slab = BLOCK // chips
    whole = count * rows // BLOCK
    return pl.pallas_call(
        pack_kernel,
        grid=(count, per),
        out_shape=[
            jax.ShapeDtypeStruct((chips, whole, slab, half), BF),
            jax.ShapeDtypeStruct((whole, slab, half), F32),
        ],
        in_specs=[
            SMEM,
            pl.BlockSpec((1, LEAF, half), lambda k, i: (k, i, 0)),
            pl.BlockSpec((1, LEAF, half), lambda k, i: (k, i, 0)),
        ],
        out_specs=[
            pl.BlockSpec((chips, blocks, slab, half), lambda k, i: (0, k * per + i, 0, 0)),
            pl.BlockSpec((blocks, slab, half), lambda k, i: (k * per + i, 0, 0)),
        ],
        scratch_shapes=[pltpu.VMEM((LEAF, half), F32)],
        compiler_params=params(24),
        cost_estimate=cost(kept.size, 10 * kept.size),
    )(at, kept, received)


def shift(value, axis, by):
    size = lax.axis_size(axis)
    return lax.ppermute(value, axis, [(i, (i + by) % size) for i in range(size)])


def ring_pieces(value, axis):
    return [value] + [shift(value, axis, by) for by in range(1, lax.axis_size(axis))]


def two_way_pieces(first, second, big, small):
    first_ring = jnp.stack(ring_pieces(first, big))
    second_pair = jnp.stack(ring_pieces(second, small))
    return ring_pieces(first_ring, small), ring_pieces(second_pair, big)


def sum_of(shares_ref, own, here, at):
    for chip in range(shares_ref.shape[0]):
        own += jnp.where(here != chip, shares_ref[(chip, *at)].astype(F32), 0.0)
    return own


def sum_kernel(at_ref, k_ref, own_ref, o_ref):
    here = at_ref[0] * 2 + at_ref[1]
    for block in range(o_ref.shape[0]):
        o_ref[block] = sum_of(k_ref, own_ref[block], here, (block,)).astype(o_ref.dtype)


def sum_shares(at, shares, own, dtype):
    chips, blocks, slab, half = shares.shape
    step = LEAF // BLOCK
    return pl.pallas_call(
        sum_kernel,
        grid=(blocks // step,),
        out_shape=jax.ShapeDtypeStruct(shares.shape[1:], dtype),
        in_specs=[
            SMEM,
            pl.BlockSpec((chips, step, slab, half), lambda i: (0, i, 0, 0)),
            pl.BlockSpec((step, slab, half), lambda i: (i, 0, 0)),
        ],
        out_specs=pl.BlockSpec((step, slab, half), lambda i: (i, 0, 0)),
        compiler_params=params(16),
        cost_estimate=cost(shares.size, 2 * shares.size),
    )(at, shares, own)


def extend_kernel(at_ref, from_ref, p_ref, own_ref, *refs):
    *kid_refs, keep_ref, send_ref, all_ref = refs
    here = at_ref[0] * 2 + at_ref[1]
    core = at_ref[2]
    step = pl.program_id(0)
    blocks = own_ref.shape[0]
    for block in range(blocks):
        total = sum_of(p_ref, own_ref[block], here, (block,))
        target = step * blocks + block
        for kid in range(2):
            ring, pair, place, there = (from_ref[kid, part, target] for part in range(4))
            for i, ref in enumerate(kid_refs):
                hit = (there > 0) & (ring == i)
                total += jnp.where(hit, ref[pair, kid, place].astype(F32), 0.0)
        all_ref[target] = total.astype(BF)

    @pl.when(step == pl.num_programs(0) - 1)
    def _():
        count = keep_ref.shape[0]
        keep_ref[...] = all_ref[pl.ds(core * count, count)]
        send_ref[...] = all_ref[pl.ds((1 - core) * count, count)]


def extend_add(at, source, parent, own, kids):
    chips, blocks, slab, half = parent.shape
    step = LEAF // BLOCK
    pair = jax.ShapeDtypeStruct((blocks // 2, slab, half), BF)
    return pl.pallas_call(
        extend_kernel,
        grid=(blocks // step,),
        out_shape=[pair, pair],
        in_specs=[
            SMEM,
            SMEM,
            pl.BlockSpec((chips, step, slab, half), lambda i: (0, i, 0, 0)),
            pl.BlockSpec((step, slab, half), lambda i: (i, 0, 0)),
        ]
        + [whole(piece) for piece in kids],
        out_specs=[whole(pair)] * 2,
        scratch_shapes=[pltpu.VMEM(parent.shape[1:], BF)],
        compiler_params=params(24),
        cost_estimate=cost(parent.size, 6 * parent.size),
    )(at, source, parent, own, *kids)


def halves(x):
    hi = x.astype(BF)
    return hi, (x - hi.astype(F32)).astype(BF)


def contract(a, b, left, right):
    return lax.dot_general(a, b, (((left,), (right,)), ((), ())), preferred_element_type=F32)


def product3(a, b):
    ah, al = halves(a)
    bh, bl = halves(b)
    return contract(ah, bh, 1, 0) + (contract(ah, bl, 1, 0) + contract(al, bh, 1, 0))


LEVEL = 14.0


def gram_kernel(at_ref, f_ref, *refs):
    a_refs, b_refs = refs[:2], refs[2:6]
    gram_ref, root_ref, cross_ref, y_ref, t_ref = refs[6:]
    x, zl, core = (at_ref[i] for i in range(3))
    step = pl.program_id(0)
    half = y_ref.shape[-1] // 2
    per = LEAF // BLOCK
    leaves, order, wide = gram_ref.shape
    row = lax.broadcasted_iota(jnp.int32, (order, wide), 0)
    col = lax.broadcasted_iota(jnp.int32, (order, wide), 1)
    lane = lax.broadcasted_iota(jnp.int32, (1, wide), 1)

    @pl.when(step == 0)
    def _():
        for side, owner in ((0, core), (1, 1 - core)):
            lanes = pl.ds(pl.multiple_of(owner * half, half), half)
            for i in range(4):
                for j in range(2):
                    chip = lax.rem(x + 4 - i, 4) * 2 + lax.rem(zl + j, 2)
                    rows = pl.ds(pl.multiple_of(chip * 16, 16), 16)
                    y_ref[:per, rows, lanes] = a_refs[j][i, side]
                    y_ref[per:, rows, lanes] = b_refs[i][j, side]
        for leaf in range(leaves):
            y = y_ref[leaf * per : (leaf + 1) * per].reshape(LEAF, wide)
            t_ref[leaf] = y.T[:order]
            gram = contract(t_ref[leaf], y, 1, 0)
            gram_ref[leaf] = gram
            square = jnp.sum(jnp.where(row == col, gram, 0.0), axis=0, keepdims=True)
            root_ref[leaf] = jnp.sqrt(jnp.where(lane < order, square, 1.0))

    here = t_ref[step]
    there = y_ref[pl.ds((1 - step) * per, per)].reshape(LEAF, wide)
    hi, lo = halves(jnp.dot(f_ref[...], there, preferred_element_type=F32) * (1.0 / root_ref[1 - step]))
    cross = contract(here, hi, 1, 0) + contract(here, lo, 1, 0)
    square = jnp.sum(jnp.where(row == col, gram_ref[step], 0.0), axis=1, keepdims=True)
    cross = cross * lax.rsqrt(square)
    most = jnp.max(jnp.max(jnp.abs(cross), axis=0, keepdims=True), axis=1, keepdims=True)
    power = jnp.ceil(jnp.log2(jnp.maximum(most, 1e-30)))
    cross = jnp.where(col < order, cross * jnp.exp2(LEVEL - power), power)
    cross = jnp.round(cross).astype(jnp.int32).astype(jnp.int16)
    cross_ref[:, 0] = cross.reshape(cross_ref.shape[0], cross_ref.shape[2], wide)


def grams(at, front, mine, order, chips):
    half = mine[0].shape[-1]
    wide = 2 * half
    return pl.pallas_call(
        gram_kernel,
        grid_spec=pltpu.PrefetchScalarGridSpec(
            num_scalar_prefetch=1,
            grid=(2,),
            in_specs=[
                pl.BlockSpec((LEAF, LEAF), lambda i, at: (at[2] * 2 + i, 1 - i)),
            ]
            + [whole(piece) for piece in mine],
            out_specs=[
                pl.BlockSpec((2, order, wide), lambda i, at: (0, 0, 0)),
                pl.BlockSpec((2, 1, wide), lambda i, at: (0, 0, 0)),
                pl.BlockSpec((chips, 1, order // chips, wide), lambda i, at: (0, i, 0, 0)),
            ],
            scratch_shapes=[
                pltpu.VMEM((2 * LEAF // BLOCK, BLOCK, wide), BF),
                pltpu.VMEM((2, order, LEAF), BF),
            ],
        ),
        out_shape=[
            jax.ShapeDtypeStruct((2, order, wide), F32),
            jax.ShapeDtypeStruct((2, 1, wide), F32),
            jax.ShapeDtypeStruct((chips, 2, order // chips, wide), jnp.int16),
        ],
        compiler_params=params(52),
        cost_estimate=cost(2 * 8 * LEAF * wide * wide, 4 * LEAF * LEAF + 2 * leaves_bytes(wide)),
    )(at, front, *mine)


def leaves_bytes(wide):
    return 2 * LEAF * wide * 2


def eliminate(s, size):
    groups = size // 8
    shape = (8, 128)
    sub = lax.broadcasted_iota(jnp.int32, shape, 0)
    for g in range(groups):
        for rows in s:
            c = {
                (i, k): jnp.broadcast_to(rows[i][:, 8 * g + k : 8 * g + k + 1], shape)
                for i in range(g, groups)
                for k in range(8)
            }
            pivot = [jnp.broadcast_to(rows[g][k : k + 1, :], shape) for k in range(8)]
            d = {
                (i, k): jnp.broadcast_to(c[g, k][i : i + 1, :], shape)
                for i in range(8)
                for k in range(i, 8)
            }
            low = {}
            scaled = []
            for k in range(8):
                inverse = pl.reciprocal(d[k, k], approx=True)
                inverse = inverse * (2.0 - d[k, k] * inverse)
                scaled.append(pivot[k] * inverse)
                for i in range(k + 1, 8):
                    low[i, k] = d[k, i] * inverse
                    pivot[i] = pivot[i] - low[i, k] * pivot[k]
                    for m in range(i, 8):
                        d[i, m] = d[i, m] - low[i, k] * d[k, m]
            for m in reversed(range(8)):
                for k in range(m + 1, 8):
                    scaled[m] = scaled[m] - low[k, m] * scaled[k]
            for i in range(g + 1, groups):
                terms = [c[i, k] * scaled[k] for k in range(8)]
                while len(terms) > 1:
                    terms = [a + b for a, b in zip(terms[::2], terms[1::2])]
                rows[i] = rows[i] - terms[0]
            new = pivot[0]
            for k in range(1, 8):
                new = jnp.where(sub == k, pivot[k], new)
            rows[g] = new


def inverse_kernel(a_ref, after_ref, w_ref, x_ref, d_ref, *, first, last):
    del after_ref
    leaves, order, wide = w_ref.shape
    blocks = order // STEP
    w_ref[...] = a_ref[...]
    lane = lax.broadcasted_iota(jnp.int32, (STEP, 128), 1)
    sub = lax.broadcasted_iota(jnp.int32, (STEP, 128), 0)
    col = lax.broadcasted_iota(jnp.int32, (STEP, wide), 1)
    row = lax.broadcasted_iota(jnp.int32, (STEP, wide), 0)
    unit = (lane - STEP == sub).astype(F32)

    def spread(k, live):
        base = pl.multiple_of(k * STEP, STEP)
        inside = (col >= base) & (col < base + STEP)
        own = (col - base == row).astype(F32)
        rest = (col >= base + STEP) & live
        for leaf in range(leaves):
            w = w_ref[leaf, pl.ds(base, STEP), :]
            r = product3(x_ref[leaf], jnp.where(inside, own, w))
            w_ref[leaf, pl.ds(base, STEP), :] = jnp.where(live, r, w)
            hi, lo = halves(r)
            none = jnp.zeros_like(hi)
            left_hi, left_lo = jnp.where(rest, hi, none), jnp.where(rest, lo, none)
            left = jnp.concatenate([left_hi, left_hi, left_lo], axis=0)
            update = contract(left, jnp.concatenate([hi, lo, hi], axis=0), 0, 0)
            for i in range(1, blocks):
                rows = slice(i * STEP, (i + 1) * STEP)
                old = jnp.where(inside & live & (i > k), 0.0, w_ref[leaf, rows, :])
                w_ref[leaf, rows, :] = old - update[rows]

    start, tile = first * STEP, first * STEP // 128 * 128
    for leaf in range(leaves):
        d = w_ref[leaf, start : start + STEP, tile : tile + 128]
        d_ref[leaf] = pltpu.roll(d, 128 - STEP, 1) if start > tile else d
        x_ref[leaf] = jnp.zeros((STEP, STEP), F32)

    @pl.loop(first, last)
    def _(k):
        s = []
        for leaf in range(leaves):
            d = jnp.where(lane < STEP, d_ref[leaf], unit)
            s.append([d[8 * i : 8 * i + 8] for i in range(STEP // 8)])
        spread(jnp.maximum(k - 1, 0), k > first)
        eliminate(s, STEP)
        base = pl.multiple_of(k * STEP, STEP)
        after = pl.multiple_of(jnp.minimum(k + 1, blocks - 1) * STEP, STEP)
        tile = pl.multiple_of(lax.div(after, 128) * 128, 128)
        odd = after - tile > 0
        for leaf in range(leaves):
            d = jnp.concatenate(s[leaf], axis=0)
            diagonal = jnp.sum(jnp.where(lane == sub, d, 0.0), axis=1, keepdims=True)
            x = (d * lax.rsqrt(diagonal))[:, STEP:]
            x_ref[leaf] = x
            hi, lo = halves(product3(x, w_ref[leaf, pl.ds(base, STEP), pl.ds(tile, 128)]))
            left = jnp.concatenate([hi, hi, lo], axis=0)
            update = contract(left, jnp.concatenate([hi, lo, hi], axis=0), 0, 0)
            update = jnp.where(odd, update[STEP:], update[:STEP])
            d = w_ref[leaf, pl.ds(after, STEP), pl.ds(tile, 128)] - update
            d_ref[leaf] = jnp.where(odd, pltpu.roll(d, 128 - STEP, 1), d)

    spread(last - 1, True)
    if last < blocks:
        return
    for leaf in range(leaves):
        for i in range(blocks):
            rows = slice(i * STEP, (i + 1) * STEP)
            w_ref[leaf, rows, :] = jnp.where(col <= row + i * STEP, w_ref[leaf, rows, :], 0.0)


def factor_inverse(work, after, first, last):
    leaves = work.shape[0]
    return pl.pallas_call(
        functools.partial(inverse_kernel, first=first, last=last),
        grid=(1,),
        out_shape=jax.ShapeDtypeStruct(work.shape, F32),
        in_specs=[whole(work), pl.BlockSpec(memory_space=pl.ANY)],
        out_specs=whole(work),
        scratch_shapes=[
            pltpu.VMEM((leaves, STEP, STEP), F32),
            pltpu.VMEM((leaves, STEP, 128), F32),
        ],
        compiler_params=params(24),
        cost_estimate=cost((last - first) * 5.5e9, 8 * work.size),
    )(work, after)


def finish_kernel(at_ref, w_ref, root_ref, own_ref, cross_ref, keep_ref, send_ref):
    leaves, order, wide = w_ref.shape
    slabs = LEAF // BLOCK
    rows = order // cross_ref.shape[0]
    base = pl.multiple_of((at_ref[0] * 2 + at_ref[1]) * rows, 8)
    first = at_ref[2] == 0
    tall = own_ref.shape[1] // 2
    for leaf in range(leaves):
        hi, lo = halves(w_ref[leaf])
        own = own_ref[leaf]
        basis = (contract(own, hi, 1, 1) + contract(own, lo, 1, 1)) * math.sqrt(LEAF)
        parts = basis.reshape(slabs, 2, tall // slabs, order)
        low, high = parts[:, 0].reshape(tall, order), parts[:, 1].reshape(tall, order)
        keep_ref[leaf, :tall] = jnp.where(first, low, high)
        send_ref[leaf, :tall] = jnp.where(first, high, low)
        left = w_ref[leaf, pl.ds(base, rows), :] * root_ref[leaf]
        cross = cross_ref[:, leaf].astype(jnp.int32).astype(F32).reshape(order, wide)
        level = jnp.exp2(cross[:1, order : order + 1] - LEVEL)
        half_way, rest = halves(product3(left[:, :order], cross))
        hi, lo = halves(w_ref[1 - leaf] * root_ref[1 - leaf])
        core = contract(half_way, hi, 1, 1) + (contract(half_way, lo, 1, 1) + contract(rest, hi, 1, 1))
        core = core * level
        low, high = core[: rows // 2], core[rows // 2 :]
        keep_ref[leaf, tall:] = jnp.where(first, low, high)
        send_ref[leaf, tall:] = jnp.where(first, high, low)


def finish(at, inverse, root, own, cross):
    leaves, order, _ = inverse.shape
    rows = (own.shape[1] + order // cross.shape[0]) // 2
    part = jax.ShapeDtypeStruct((leaves, rows, order), F32)
    return pl.pallas_call(
        finish_kernel,
        grid=(1,),
        out_shape=[part, part],
        in_specs=[SMEM, whole(inverse), whole(root), whole(own), whole(cross)],
        out_specs=[whole(part)] * 2,
        compiler_params=params(24),
        cost_estimate=cost(2e9, 4 * (inverse.size + cross.size)),
    )(at, inverse, root, own, cross)


def local(parent_front, child_update, parent_test, child_test, child_map):
    y, zh = lax.axis_index("y"), lax.axis_index("zh")
    x, zl, core = lax.axis_index("x"), lax.axis_index("zl"), lax.axis_index("core")
    row_index = lax.axis_index(ROW)
    probes = parent_test.shape[1]
    half = 256
    chips = lax.axis_size(CHIP)
    own_blocks = parent_front.shape[0] // BLOCK
    kid_blocks = child_update.shape[1] // BLOCK
    swap = [(0, 1), (1, 0)]

    at = jnp.stack([x, zl, core]).astype(jnp.int32)
    kid_sent, kid_kept = probe(at, child_update, jnp.swapaxes(child_test, 1, 2), half)
    kid_sent = lax.ppermute(kid_sent, "core", swap)
    own_sent, own_kept = probe(at, parent_front[None], parent_test.T[None], half)
    own_sent = lax.ppermute(own_sent, "core", swap)
    kid_part, kid_rest = pack(at, kid_kept, kid_sent, chips)
    kid_share = lax.all_to_all(kid_part, CHIP, 0, 0, tiled=True)
    own_part, own_rest = pack(at, own_kept, own_sent, chips)

    kids = sum_shares(at, kid_share, kid_rest, BF).reshape(2, kid_blocks, -1, half)
    pair = ring_pieces(kids, "zh")
    pair[1], own_part = lax.optimization_barrier((pair[1], own_part))
    pair = jnp.stack(pair)
    own_share = lax.all_to_all(own_part, CHIP, 0, 0, tiled=True)
    reach = [(0, 1), (0, 2), (1, 0), (1, 2), (2, 1), (2, 3), (3, 1), (3, 2)]
    kid_pieces = [pair] + [
        lax.ppermute(pair, "y", [(i, j) for i, j in reach if (j - i) % 4 == by])
        for by in range(1, 4)
    ]

    targets = row_index * own_blocks + jnp.arange(own_blocks, dtype=jnp.int32)
    hit = child_map[:, None, :] == targets[None, :, None]
    there = jnp.any(hit, axis=2).astype(jnp.int32)
    source = jnp.sum(jnp.where(hit, jnp.arange(child_map.shape[1], dtype=jnp.int32), 0), axis=2)
    owner, place = source // kid_blocks, source % kid_blocks
    ring = (y - owner // 2) % 4
    pair_of = (zh - owner % 2) % 2
    origin = jnp.stack([ring, pair_of, place, there], axis=1).astype(jnp.int32)
    keep, send = extend_add(at, origin, own_share, own_rest, kid_pieces)
    came = lax.ppermute(send, "core", swap)

    per = LEAF // BLOCK
    first = jnp.stack([keep[:per], came[:per]])
    second = jnp.stack([keep[per:], came[per:]])
    firsts, seconds = two_way_pieces(first, second, "x", "zl")
    gram, root, cross = grams(at, parent_front, firsts + seconds, probes, chips)

    own_rows = jnp.where(
        core == 0,
        jnp.concatenate([keep, came], axis=2),
        jnp.concatenate([came, keep], axis=2),
    ).reshape(2, -1, 2 * half)

    cross = lax.all_to_all(cross, CHIP, 0, 0, tiled=True)
    ready = lax.dynamic_slice_in_dim(cross, row_index, 1, 0)
    work = factor_inverse(gram, own_rows, 0, 3)
    cross = lax.all_to_all(jnp.broadcast_to(ready, (chips, *ready.shape[1:])), CHIP, 0, 0, tiled=True)
    inverse = factor_inverse(work, ready[0, 0, :8, :128].astype(F32), 3, probes // STEP)
    keep, send = finish(at, inverse, root, own_rows, cross)
    came = lax.ppermute(send, "core", swap)
    both = jnp.where(core == 0, jnp.concatenate([keep, came]), jnp.concatenate([came, keep]))
    tall = own_rows.shape[1] // 2
    leaf_basis = both[:, :tall].astype(BF).reshape(own_blocks, -1, probes)
    return (leaf_basis, both[:, tall:])


def solution(mesh):
    split = Mesh(mesh.devices.reshape(4, 2, 4, 2, 2), ("y", "zh", "x", "zl", "core"))
    placed = (P(ROW, COL), P(None, ROW, COL), P(COL, None), P(None, COL, None), P())
    return jax.shard_map(
        local,
        mesh=split,
        in_specs=placed,
        out_specs=(P(ROW, COL, None), P(ROW, COL, None)),
        check_vma=False,
    )
```

```python
import functools
import math

import jax
import jax.numpy as jnp
from jax import lax
from jax.experimental import pallas as pl
from jax.experimental.pallas import tpu as pltpu
from jax.sharding import Mesh
from jax.sharding import PartitionSpec as P

LEAF = 896
BLOCK = 128
ROW = ("y", "zh")
CHIP = ("x", "zl")
COL = ("x", "zl", "core")
F32 = jnp.float32
BF = jnp.bfloat16
SMEM = pl.BlockSpec(memory_space=pltpu.SMEM)
STEP = 64


def whole(array):
    return pl.BlockSpec(array.shape, lambda *_: (0,) * len(array.shape))


def params(mib):
    return pltpu.CompilerParams(vmem_limit_bytes=mib << 20)


def cost(flops, nbytes):
    return pl.CostEstimate(flops=int(flops), bytes_accessed=int(nbytes), transcendentals=0)


def probe_kernel(at_ref, a_ref, b_ref, sent_ref, kept_ref):
    total = contract(a_ref[0], b_ref[0], 1, 1)
    half = sent_ref.shape[2]
    low = total[:, :half]
    pad = jnp.zeros((total.shape[0], 2 * half - total.shape[1]), F32)
    high = jnp.concatenate([total[:, half:], pad], axis=1)
    first = at_ref[2] == 0
    kept_ref[0] = jnp.where(first, low, high)
    sent_ref[0] = jnp.where(first, high, low)


def probe(at, a, b, half, tall):
    count, rows, depth = a.shape
    probes = b.shape[1]
    part = jax.ShapeDtypeStruct((count, rows, half), F32)
    return pl.pallas_call(
        probe_kernel,
        grid=(count, rows // tall),
        out_shape=[part, part],
        in_specs=[
            SMEM,
            pl.BlockSpec((1, tall, depth), lambda k, i: (k, i, 0)),
            pl.BlockSpec((1, probes, depth), lambda k, i: (k, 0, 0)),
        ],
        out_specs=[pl.BlockSpec((1, tall, half), lambda k, i: (k, i, 0))] * 2,
        compiler_params=params(40),
        cost_estimate=cost(4 * count * rows * depth * half, 2 * a.size + 8 * count * rows * half),
    )(at, a, b)


def pack_kernel(at_ref, a_ref, b_ref, o_ref, own_ref, sum_ref):
    total = a_ref[0] + b_ref[0]
    sum_ref[...] = total
    chips, blocks, rows, _ = o_ref.shape
    chip_here = at_ref[0] * 2 + at_ref[1]
    for block in range(blocks):
        for chip in range(chips):
            start = (block * chips + chip) * rows
            o_ref[chip, block] = total[start : start + rows].astype(BF)
        own = pl.multiple_of((block * chips + chip_here) * rows, rows)
        own_ref[block] = sum_ref[pl.ds(own, rows), :]


def pack(at, kept, received, chips):
    count, rows, half = kept.shape
    per = rows // LEAF
    blocks = LEAF // BLOCK
    slab = BLOCK // chips
    whole = count * rows // BLOCK
    return pl.pallas_call(
        pack_kernel,
        grid=(count, per),
        out_shape=[
            jax.ShapeDtypeStruct((chips, whole, slab, half), BF),
            jax.ShapeDtypeStruct((whole, slab, half), F32),
        ],
        in_specs=[
            SMEM,
            pl.BlockSpec((1, LEAF, half), lambda k, i: (k, i, 0)),
            pl.BlockSpec((1, LEAF, half), lambda k, i: (k, i, 0)),
        ],
        out_specs=[
            pl.BlockSpec((chips, blocks, slab, half), lambda k, i: (0, k * per + i, 0, 0)),
            pl.BlockSpec((blocks, slab, half), lambda k, i: (k * per + i, 0, 0)),
        ],
        scratch_shapes=[pltpu.VMEM((LEAF, half), F32)],
        compiler_params=params(24),
        cost_estimate=cost(kept.size, 10 * kept.size),
    )(at, kept, received)


def shift(value, axis, by):
    size = lax.axis_size(axis)
    return lax.ppermute(value, axis, [(i, (i + by) % size) for i in range(size)])


def ring_pieces(value, axis):
    return [value] + [shift(value, axis, by) for by in range(1, lax.axis_size(axis))]


def two_way_pieces(first, second, big, small):
    first_ring = jnp.stack(ring_pieces(first, big))
    second_pair = jnp.stack(ring_pieces(second, small))
    return ring_pieces(first_ring, small), ring_pieces(second_pair, big)


def sum_of(shares_ref, own, here, at):
    for chip in range(shares_ref.shape[0]):
        own += jnp.where(here != chip, shares_ref[(chip, *at)].astype(F32), 0.0)
    return own


def sum_kernel(at_ref, k_ref, own_ref, o_ref):
    here = at_ref[0] * 2 + at_ref[1]
    for block in range(o_ref.shape[0]):
        o_ref[block] = sum_of(k_ref, own_ref[block], here, (block,)).astype(o_ref.dtype)


def sum_shares(at, shares, own, dtype):
    chips, blocks, slab, half = shares.shape
    step = LEAF // BLOCK
    return pl.pallas_call(
        sum_kernel,
        grid=(blocks // step,),
        out_shape=jax.ShapeDtypeStruct(shares.shape[1:], dtype),
        in_specs=[
            SMEM,
            pl.BlockSpec((chips, step, slab, half), lambda i: (0, i, 0, 0)),
            pl.BlockSpec((step, slab, half), lambda i: (i, 0, 0)),
        ],
        out_specs=pl.BlockSpec((step, slab, half), lambda i: (i, 0, 0)),
        compiler_params=params(16),
        cost_estimate=cost(shares.size, 2 * shares.size),
    )(at, shares, own)


def extend_kernel(at_ref, from_ref, p_ref, own_ref, *refs):
    *kid_refs, keep_ref, send_ref, all_ref = refs
    here = at_ref[0] * 2 + at_ref[1]
    core = at_ref[2]
    step = pl.program_id(0)
    blocks = own_ref.shape[0]
    for block in range(blocks):
        total = sum_of(p_ref, own_ref[block], here, (block,))
        target = step * blocks + block
        for kid in range(2):
            ring, pair, place, there = (from_ref[kid, part, target] for part in range(4))
            for i, ref in enumerate(kid_refs):
                hit = (there > 0) & (ring == i)
                total += jnp.where(hit, ref[pair, kid, place].astype(F32), 0.0)
        all_ref[target] = total.astype(BF)

    @pl.when(step == pl.num_programs(0) - 1)
    def _():
        count = keep_ref.shape[0]
        keep_ref[...] = all_ref[pl.ds(core * count, count)]
        send_ref[...] = all_ref[pl.ds((1 - core) * count, count)]


def extend_add(at, source, parent, own, kids):
    chips, blocks, slab, half = parent.shape
    step = LEAF // BLOCK
    pair = jax.ShapeDtypeStruct((blocks // 2, slab, half), BF)
    return pl.pallas_call(
        extend_kernel,
        grid=(blocks // step,),
        out_shape=[pair, pair],
        in_specs=[
            SMEM,
            SMEM,
            pl.BlockSpec((chips, step, slab, half), lambda i: (0, i, 0, 0)),
            pl.BlockSpec((step, slab, half), lambda i: (i, 0, 0)),
        ]
        + [whole(piece) for piece in kids],
        out_specs=[whole(pair)] * 2,
        scratch_shapes=[pltpu.VMEM(parent.shape[1:], BF)],
        compiler_params=params(24),
        cost_estimate=cost(parent.size, 6 * parent.size),
    )(at, source, parent, own, *kids)


def halves(x):
    hi = x.astype(BF)
    return hi, (x - hi.astype(F32)).astype(BF)


def contract(a, b, left, right):
    return lax.dot_general(a, b, (((left,), (right,)), ((), ())), preferred_element_type=F32)


def product3(a, b):
    ah, al = halves(a)
    bh, bl = halves(b)
    return contract(ah, bh, 1, 0) + (contract(ah, bl, 1, 0) + contract(al, bh, 1, 0))


LEVEL = 14.0


def gram_kernel(at_ref, f_ref, *refs):
    a_refs, b_refs = refs[:2], refs[2:6]
    gram_ref, root_ref, cross_ref, y_ref, t_ref = refs[6:]
    x, zl, core = (at_ref[i] for i in range(3))
    step = pl.program_id(0)
    half = y_ref.shape[-1] // 2
    per = LEAF // BLOCK
    leaves, order, wide = gram_ref.shape
    row = lax.broadcasted_iota(jnp.int32, (order, wide), 0)
    col = lax.broadcasted_iota(jnp.int32, (order, wide), 1)
    lane = lax.broadcasted_iota(jnp.int32, (1, wide), 1)

    @pl.when(step == 0)
    def _():
        for side, owner in ((0, core), (1, 1 - core)):
            lanes = pl.ds(pl.multiple_of(owner * half, half), half)
            for i in range(4):
                for j in range(2):
                    chip = lax.rem(x + 4 - i, 4) * 2 + lax.rem(zl + j, 2)
                    rows = pl.ds(pl.multiple_of(chip * 16, 16), 16)
                    y_ref[:per, rows, lanes] = a_refs[j][i, side]
                    y_ref[per:, rows, lanes] = b_refs[i][j, side]
        for leaf in range(leaves):
            y = y_ref[leaf * per : (leaf + 1) * per].reshape(LEAF, wide)
            t_ref[leaf] = y.T[:order]
            gram = contract(t_ref[leaf], y, 1, 0)
            gram_ref[leaf] = gram
            square = jnp.sum(jnp.where(row == col, gram, 0.0), axis=0, keepdims=True)
            root_ref[leaf] = jnp.sqrt(jnp.where(lane < order, square, 1.0))

    here = t_ref[step]
    here = jnp.concatenate([here, here], axis=1)
    there = y_ref[pl.ds((1 - step) * per, per)].reshape(LEAF, wide)
    hi, lo = halves(jnp.dot(f_ref[...], there, preferred_element_type=F32) * (1.0 / root_ref[1 - step]))
    cross = contract(here, jnp.concatenate([hi, lo], axis=0), 1, 0)
    square = jnp.sum(jnp.where(row == col, gram_ref[step], 0.0), axis=1, keepdims=True)
    cross = cross * lax.rsqrt(square)
    most = jnp.max(jnp.max(jnp.abs(cross), axis=0, keepdims=True), axis=1, keepdims=True)
    power = jnp.ceil(jnp.log2(jnp.maximum(most, 1e-30)))
    cross = jnp.where(col < order, cross * jnp.exp2(LEVEL - power), power)
    cross = jnp.round(cross).astype(jnp.int32).astype(jnp.int16)
    cross_ref[:, 0] = cross.reshape(cross_ref.shape[0], cross_ref.shape[2], wide)


def grams(at, front, mine, order, chips):
    half = mine[0].shape[-1]
    wide = 2 * half
    return pl.pallas_call(
        gram_kernel,
        grid_spec=pltpu.PrefetchScalarGridSpec(
            num_scalar_prefetch=1,
            grid=(2,),
            in_specs=[
                pl.BlockSpec((LEAF, LEAF), lambda i, at: (at[2] * 2 + i, 1 - i)),
            ]
            + [whole(piece) for piece in mine],
            out_specs=[
                pl.BlockSpec((2, order, wide), lambda i, at: (0, 0, 0)),
                pl.BlockSpec((2, 1, wide), lambda i, at: (0, 0, 0)),
                pl.BlockSpec((chips, 1, order // chips, wide), lambda i, at: (0, i, 0, 0)),
            ],
            scratch_shapes=[
                pltpu.VMEM((2 * LEAF // BLOCK, BLOCK, wide), BF),
                pltpu.VMEM((2, order, LEAF), BF),
            ],
        ),
        out_shape=[
            jax.ShapeDtypeStruct((2, order, wide), F32),
            jax.ShapeDtypeStruct((2, 1, wide), F32),
            jax.ShapeDtypeStruct((chips, 2, order // chips, wide), jnp.int16),
        ],
        compiler_params=params(52),
        cost_estimate=cost(2 * 8 * LEAF * wide * wide, 4 * LEAF * LEAF + 2 * leaves_bytes(wide)),
    )(at, front, *mine)


def leaves_bytes(wide):
    return 2 * LEAF * wide * 2


def eliminate(s, size):
    groups = size // 8
    shape = (8, 128)
    sub = lax.broadcasted_iota(jnp.int32, shape, 0)
    for g in range(groups):
        for rows in s:
            c = {
                (i, k): jnp.broadcast_to(rows[i][:, 8 * g + k : 8 * g + k + 1], shape)
                for i in range(g, groups)
                for k in range(8)
            }
            pivot = [jnp.broadcast_to(rows[g][k : k + 1, :], shape) for k in range(8)]
            d = {
                (i, k): jnp.broadcast_to(c[g, k][i : i + 1, :], shape)
                for i in range(8)
                for k in range(i, 8)
            }
            low = {}
            scaled = []
            for k in range(8):
                inverse = pl.reciprocal(d[k, k], approx=True)
                inverse = inverse * (2.0 - d[k, k] * inverse)
                scaled.append(pivot[k] * inverse)
                for i in range(k + 1, 8):
                    low[i, k] = d[k, i] * inverse
                    pivot[i] = pivot[i] - low[i, k] * pivot[k]
                    for m in range(i, 8):
                        d[i, m] = d[i, m] - low[i, k] * d[k, m]
            for m in reversed(range(8)):
                for k in range(m + 1, 8):
                    scaled[m] = scaled[m] - low[k, m] * scaled[k]
            for i in range(g + 1, groups):
                terms = [c[i, k] * scaled[k] for k in range(8)]
                while len(terms) > 1:
                    terms = [a + b for a, b in zip(terms[::2], terms[1::2])]
                rows[i] = rows[i] - terms[0]
            new = pivot[0]
            for k in range(1, 8):
                new = jnp.where(sub == k, pivot[k], new)
            rows[g] = new


def inverse_kernel(a_ref, after_ref, w_ref, x_ref, d_ref, *, first, last):
    del after_ref
    leaves, order, wide = w_ref.shape
    blocks = order // STEP
    w_ref[...] = a_ref[...]
    lane = lax.broadcasted_iota(jnp.int32, (STEP, 128), 1)
    sub = lax.broadcasted_iota(jnp.int32, (STEP, 128), 0)
    col = lax.broadcasted_iota(jnp.int32, (STEP, wide), 1)
    row = lax.broadcasted_iota(jnp.int32, (STEP, wide), 0)
    unit = (lane - STEP == sub).astype(F32)

    def spread(k, live):
        base = pl.multiple_of(k * STEP, STEP)
        inside = (col >= base) & (col < base + STEP)
        own = (col - base == row).astype(F32)
        rest = (col >= base + STEP) & live
        for leaf in range(leaves):
            w = w_ref[leaf, pl.ds(base, STEP), :]
            r = product3(x_ref[leaf], jnp.where(inside, own, w))
            w_ref[leaf, pl.ds(base, STEP), :] = jnp.where(live, r, w)
            hi, lo = halves(r)
            none = jnp.zeros_like(hi)
            left_hi, left_lo = jnp.where(rest, hi, none), jnp.where(rest, lo, none)
            left = jnp.concatenate([left_hi, left_hi, left_lo], axis=0)
            update = contract(left, jnp.concatenate([hi, lo, hi], axis=0), 0, 0)
            for i in range(1, blocks):
                rows = slice(i * STEP, (i + 1) * STEP)
                old = jnp.where(inside & live & (i > k), 0.0, w_ref[leaf, rows, :])
                w_ref[leaf, rows, :] = old - update[rows]

    start, tile = first * STEP, first * STEP // 128 * 128
    for leaf in range(leaves):
        d = w_ref[leaf, start : start + STEP, tile : tile + 128]
        d_ref[leaf] = pltpu.roll(d, 128 - STEP, 1) if start > tile else d
        x_ref[leaf] = jnp.zeros((STEP, STEP), F32)

    @pl.loop(first, last)
    def _(k):
        s = []
        for leaf in range(leaves):
            d = jnp.where(lane < STEP, d_ref[leaf], unit)
            s.append([d[8 * i : 8 * i + 8] for i in range(STEP // 8)])
        spread(jnp.maximum(k - 1, 0), k > first)
        eliminate(s, STEP)
        base = pl.multiple_of(k * STEP, STEP)
        after = pl.multiple_of(jnp.minimum(k + 1, blocks - 1) * STEP, STEP)
        tile = pl.multiple_of(lax.div(after, 128) * 128, 128)
        odd = after - tile > 0
        for leaf in range(leaves):
            d = jnp.concatenate(s[leaf], axis=0)
            diagonal = jnp.sum(jnp.where(lane == sub, d, 0.0), axis=1, keepdims=True)
            x = (d * lax.rsqrt(diagonal))[:, STEP:]
            x_ref[leaf] = x
            hi, lo = halves(product3(x, w_ref[leaf, pl.ds(base, STEP), pl.ds(tile, 128)]))
            left = jnp.concatenate([hi, hi, lo], axis=0)
            update = contract(left, jnp.concatenate([hi, lo, hi], axis=0), 0, 0)
            update = jnp.where(odd, update[STEP:], update[:STEP])
            d = w_ref[leaf, pl.ds(after, STEP), pl.ds(tile, 128)] - update
            d_ref[leaf] = jnp.where(odd, pltpu.roll(d, 128 - STEP, 1), d)

    spread(last - 1, True)
    if last < blocks:
        return
    for leaf in range(leaves):
        for i in range(blocks):
            rows = slice(i * STEP, (i + 1) * STEP)
            w_ref[leaf, rows, :] = jnp.where(col <= row + i * STEP, w_ref[leaf, rows, :], 0.0)


def factor_inverse(work, after, first, last):
    leaves = work.shape[0]
    return pl.pallas_call(
        functools.partial(inverse_kernel, first=first, last=last),
        grid=(1,),
        out_shape=jax.ShapeDtypeStruct(work.shape, F32),
        in_specs=[whole(work), pl.BlockSpec(memory_space=pl.ANY)],
        out_specs=whole(work),
        scratch_shapes=[
            pltpu.VMEM((leaves, STEP, STEP), F32),
            pltpu.VMEM((leaves, STEP, 128), F32),
        ],
        compiler_params=params(24),
        cost_estimate=cost((last - first) * 5.5e9, 8 * work.size),
    )(work, after)


def finish_kernel(at_ref, w_ref, root_ref, own_ref, cross_ref, keep_ref, send_ref):
    leaves, order, wide = w_ref.shape
    slabs = LEAF // BLOCK
    rows = order // cross_ref.shape[0]
    base = pl.multiple_of((at_ref[0] * 2 + at_ref[1]) * rows, 8)
    first = at_ref[2] == 0
    tall = own_ref.shape[1] // 2
    for leaf in range(leaves):
        hi, lo = halves(w_ref[leaf])
        own = own_ref[leaf]
        basis = (contract(own, hi, 1, 1) + contract(own, lo, 1, 1)) * math.sqrt(LEAF)
        parts = basis.reshape(slabs, 2, tall // slabs, order)
        low, high = parts[:, 0].reshape(tall, order), parts[:, 1].reshape(tall, order)
        keep_ref[leaf, :tall] = jnp.where(first, low, high)
        send_ref[leaf, :tall] = jnp.where(first, high, low)
        left = w_ref[leaf, pl.ds(base, rows), :] * root_ref[leaf]
        cross = cross_ref[:, leaf].astype(jnp.int32).astype(F32).reshape(order, wide)
        level = jnp.exp2(cross[:1, order : order + 1] - LEVEL)
        half_way, rest = halves(product3(left[:, :order], cross))
        hi, lo = halves(w_ref[1 - leaf] * root_ref[1 - leaf])
        core = contract(half_way, hi, 1, 1) + (contract(half_way, lo, 1, 1) + contract(rest, hi, 1, 1))
        core = core * level
        low, high = core[: rows // 2], core[rows // 2 :]
        keep_ref[leaf, tall:] = jnp.where(first, low, high)
        send_ref[leaf, tall:] = jnp.where(first, high, low)


def finish(at, inverse, root, own, cross):
    leaves, order, _ = inverse.shape
    rows = (own.shape[1] + order // cross.shape[0]) // 2
    part = jax.ShapeDtypeStruct((leaves, rows, order), F32)
    return pl.pallas_call(
        finish_kernel,
        grid=(1,),
        out_shape=[part, part],
        in_specs=[SMEM, whole(inverse), whole(root), whole(own), whole(cross)],
        out_specs=[whole(part)] * 2,
        compiler_params=params(24),
        cost_estimate=cost(2e9, 4 * (inverse.size + cross.size)),
    )(at, inverse, root, own, cross)


def local(parent_front, child_update, parent_test, child_test, child_map):
    y, zh = lax.axis_index("y"), lax.axis_index("zh")
    x, zl, core = lax.axis_index("x"), lax.axis_index("zl"), lax.axis_index("core")
    row_index = lax.axis_index(ROW)
    probes = parent_test.shape[1]
    half = 256
    chips = lax.axis_size(CHIP)
    own_blocks = parent_front.shape[0] // BLOCK
    kid_blocks = child_update.shape[1] // BLOCK
    swap = [(0, 1), (1, 0)]

    at = jnp.stack([x, zl, core]).astype(jnp.int32)
    kid_sent, kid_kept = probe(at, child_update, jnp.swapaxes(child_test, 1, 2), half, 2 * LEAF)
    kid_sent = lax.ppermute(kid_sent, "core", swap)
    own_sent, own_kept = probe(at, parent_front[None], parent_test.T[None], half, LEAF)
    own_sent = lax.ppermute(own_sent, "core", swap)
    kid_part, kid_rest = pack(at, kid_kept, kid_sent, chips)
    kid_share = lax.all_to_all(kid_part, CHIP, 0, 0, tiled=True)
    own_part, own_rest = pack(at, own_kept, own_sent, chips)

    kids = sum_shares(at, kid_share, kid_rest, BF).reshape(2, kid_blocks, -1, half)
    pair = ring_pieces(kids, "zh")
    pair[1], own_part = lax.optimization_barrier((pair[1], own_part))
    pair = jnp.stack(pair)
    own_share = lax.all_to_all(own_part, CHIP, 0, 0, tiled=True)
    reach = [(0, 1), (0, 2), (1, 0), (1, 2), (2, 1), (2, 3), (3, 1), (3, 2)]
    kid_pieces = [pair] + [
        lax.ppermute(pair, "y", [(i, j) for i, j in reach if (j - i) % 4 == by])
        for by in range(1, 4)
    ]

    targets = row_index * own_blocks + jnp.arange(own_blocks, dtype=jnp.int32)
    hit = child_map[:, None, :] == targets[None, :, None]
    there = jnp.any(hit, axis=2).astype(jnp.int32)
    source = jnp.sum(jnp.where(hit, jnp.arange(child_map.shape[1], dtype=jnp.int32), 0), axis=2)
    owner, place = source // kid_blocks, source % kid_blocks
    ring = (y - owner // 2) % 4
    pair_of = (zh - owner % 2) % 2
    origin = jnp.stack([ring, pair_of, place, there], axis=1).astype(jnp.int32)
    keep, send = extend_add(at, origin, own_share, own_rest, kid_pieces)
    came = lax.ppermute(send, "core", swap)

    per = LEAF // BLOCK
    first = jnp.stack([keep[:per], came[:per]])
    second = jnp.stack([keep[per:], came[per:]])
    firsts, seconds = two_way_pieces(first, second, "x", "zl")
    gram, root, cross = grams(at, parent_front, firsts + seconds, probes, chips)

    own_rows = jnp.where(
        core == 0,
        jnp.concatenate([keep, came], axis=2),
        jnp.concatenate([came, keep], axis=2),
    ).reshape(2, -1, 2 * half)

    cross = lax.all_to_all(cross, CHIP, 0, 0, tiled=True)
    ready = lax.dynamic_slice_in_dim(cross, row_index, 1, 0)
    work = factor_inverse(gram, own_rows, 0, 3)
    cross = lax.all_to_all(jnp.broadcast_to(ready, (chips, *ready.shape[1:])), CHIP, 0, 0, tiled=True)
    inverse = factor_inverse(work, ready[0, 0, :8, :128].astype(F32), 3, probes // STEP)
    keep, send = finish(at, inverse, root, own_rows, cross)
    came = lax.ppermute(send, "core", swap)
    both = jnp.where(core == 0, jnp.concatenate([keep, came]), jnp.concatenate([came, keep]))
    tall = own_rows.shape[1] // 2
    leaf_basis = both[:, :tall].astype(BF).reshape(own_blocks, -1, probes)
    return (leaf_basis, both[:, tall:])


def solution(mesh):
    split = Mesh(mesh.devices.reshape(4, 2, 4, 2, 2), ("y", "zh", "x", "zl", "core"))
    placed = (P(ROW, COL), P(None, ROW, COL), P(COL, None), P(None, COL, None), P())
    return jax.shard_map(
        local,
        mesh=split,
        in_specs=placed,
        out_specs=(P(ROW, COL, None), P(ROW, COL, None)),
        check_vma=False,
    )
```

```python
import functools
import math

import jax
import jax.numpy as jnp
from jax import lax
from jax.experimental import pallas as pl
from jax.experimental.pallas import tpu as pltpu
from jax.sharding import Mesh
from jax.sharding import PartitionSpec as P

LEAF = 896
BLOCK = 128
ROW = ("y", "zh")
CHIP = ("x", "zl")
COL = ("x", "zl", "core")
F32 = jnp.float32
BF = jnp.bfloat16
SMEM = pl.BlockSpec(memory_space=pltpu.SMEM)
STEP = 64


def whole(array):
    return pl.BlockSpec(array.shape, lambda *_: (0,) * len(array.shape))


def params(mib):
    return pltpu.CompilerParams(vmem_limit_bytes=mib << 20)


def cost(flops, nbytes):
    return pl.CostEstimate(flops=int(flops), bytes_accessed=int(nbytes), transcendentals=0)


def probe_kernel(at_ref, a_ref, b_ref, sent_ref, kept_ref):
    total = contract(a_ref[0], b_ref[0], 1, 1)
    half = sent_ref.shape[2]
    low = total[:, :half]
    pad = jnp.zeros((total.shape[0], 2 * half - total.shape[1]), F32)
    high = jnp.concatenate([total[:, half:], pad], axis=1)
    first = at_ref[2] == 0
    kept_ref[0] = jnp.where(first, low, high)
    sent_ref[0] = jnp.where(first, high, low)


def probe(at, a, b, half):
    count, rows, depth = a.shape
    probes = b.shape[1]
    part = jax.ShapeDtypeStruct((count, rows, half), F32)
    return pl.pallas_call(
        probe_kernel,
        grid=(count, rows // LEAF),
        out_shape=[part, part],
        in_specs=[
            SMEM,
            pl.BlockSpec((1, LEAF, depth), lambda k, i: (k, i, 0)),
            pl.BlockSpec((1, probes, depth), lambda k, i: (k, 0, 0)),
        ],
        out_specs=[pl.BlockSpec((1, LEAF, half), lambda k, i: (k, i, 0))] * 2,
        compiler_params=params(40),
        cost_estimate=cost(4 * count * rows * depth * half, 2 * a.size + 8 * count * rows * half),
    )(at, a, b)


def pack_kernel(at_ref, a_ref, b_ref, o_ref, own_ref, sum_ref):
    total = a_ref[0] + b_ref[0]
    sum_ref[...] = total
    chips, blocks, rows, _ = o_ref.shape
    chip_here = at_ref[0] * 2 + at_ref[1]
    for block in range(blocks):
        for chip in range(chips):
            start = (block * chips + chip) * rows
            o_ref[chip, block] = total[start : start + rows].astype(BF)
        own = pl.multiple_of((block * chips + chip_here) * rows, rows)
        own_ref[block] = sum_ref[pl.ds(own, rows), :]


def pack(at, kept, received, chips):
    count, rows, half = kept.shape
    per = rows // LEAF
    blocks = LEAF // BLOCK
    slab = BLOCK // chips
    whole = count * rows // BLOCK
    return pl.pallas_call(
        pack_kernel,
        grid=(count, per),
        out_shape=[
            jax.ShapeDtypeStruct((chips, whole, slab, half), BF),
            jax.ShapeDtypeStruct((whole, slab, half), F32),
        ],
        in_specs=[
            SMEM,
            pl.BlockSpec((1, LEAF, half), lambda k, i: (k, i, 0)),
            pl.BlockSpec((1, LEAF, half), lambda k, i: (k, i, 0)),
        ],
        out_specs=[
            pl.BlockSpec((chips, blocks, slab, half), lambda k, i: (0, k * per + i, 0, 0)),
            pl.BlockSpec((blocks, slab, half), lambda k, i: (k * per + i, 0, 0)),
        ],
        scratch_shapes=[pltpu.VMEM((LEAF, half), F32)],
        compiler_params=params(24),
        cost_estimate=cost(kept.size, 10 * kept.size),
    )(at, kept, received)


def shift(value, axis, by):
    size = lax.axis_size(axis)
    return lax.ppermute(value, axis, [(i, (i + by) % size) for i in range(size)])


def ring_pieces(value, axis):
    return [value] + [shift(value, axis, by) for by in range(1, lax.axis_size(axis))]


def two_way_pieces(first, second, big, small):
    first_ring = jnp.stack(ring_pieces(first, big))
    second_pair = jnp.stack(ring_pieces(second, small))
    return ring_pieces(first_ring, small), ring_pieces(second_pair, big)


def sum_of(shares_ref, own, here, at):
    for chip in range(shares_ref.shape[0]):
        own += jnp.where(here != chip, shares_ref[(chip, *at)].astype(F32), 0.0)
    return own


def sum_kernel(at_ref, k_ref, own_ref, o_ref):
    here = at_ref[0] * 2 + at_ref[1]
    for block in range(o_ref.shape[0]):
        o_ref[block] = sum_of(k_ref, own_ref[block], here, (block,)).astype(o_ref.dtype)


def sum_shares(at, shares, own, dtype):
    chips, blocks, slab, half = shares.shape
    step = LEAF // BLOCK
    return pl.pallas_call(
        sum_kernel,
        grid=(blocks // step,),
        out_shape=jax.ShapeDtypeStruct(shares.shape[1:], dtype),
        in_specs=[
            SMEM,
            pl.BlockSpec((chips, step, slab, half), lambda i: (0, i, 0, 0)),
            pl.BlockSpec((step, slab, half), lambda i: (i, 0, 0)),
        ],
        out_specs=pl.BlockSpec((step, slab, half), lambda i: (i, 0, 0)),
        compiler_params=params(16),
        cost_estimate=cost(shares.size, 2 * shares.size),
    )(at, shares, own)


def extend_kernel(at_ref, from_ref, p_ref, own_ref, *refs):
    *kid_refs, keep_ref, send_ref, all_ref = refs
    here = at_ref[0] * 2 + at_ref[1]
    core = at_ref[2]
    step = pl.program_id(0)
    blocks = own_ref.shape[0]
    for block in range(blocks):
        total = sum_of(p_ref, own_ref[block], here, (block,))
        target = step * blocks + block
        for kid in range(2):
            ring, pair, place, there = (from_ref[kid, part, target] for part in range(4))
            for i, ref in enumerate(kid_refs):
                hit = (there > 0) & (ring == i)
                total += jnp.where(hit, ref[pair, kid, place].astype(F32), 0.0)
        all_ref[target] = total.astype(BF)

    @pl.when(step == pl.num_programs(0) - 1)
    def _():
        count = keep_ref.shape[0]
        keep_ref[...] = all_ref[pl.ds(core * count, count)]
        send_ref[...] = all_ref[pl.ds((1 - core) * count, count)]


def extend_add(at, source, parent, own, kids):
    chips, blocks, slab, half = parent.shape
    step = LEAF // BLOCK
    pair = jax.ShapeDtypeStruct((blocks // 2, slab, half), BF)
    return pl.pallas_call(
        extend_kernel,
        grid=(blocks // step,),
        out_shape=[pair, pair],
        in_specs=[
            SMEM,
            SMEM,
            pl.BlockSpec((chips, step, slab, half), lambda i: (0, i, 0, 0)),
            pl.BlockSpec((step, slab, half), lambda i: (i, 0, 0)),
        ]
        + [whole(piece) for piece in kids],
        out_specs=[whole(pair)] * 2,
        scratch_shapes=[pltpu.VMEM(parent.shape[1:], BF)],
        compiler_params=params(24),
        cost_estimate=cost(parent.size, 6 * parent.size),
    )(at, source, parent, own, *kids)


def halves(x):
    hi = x.astype(BF)
    return hi, (x - hi.astype(F32)).astype(BF)


def contract(a, b, left, right):
    return lax.dot_general(a, b, (((left,), (right,)), ((), ())), preferred_element_type=F32)


def product3(a, b):
    ah, al = halves(a)
    bh, bl = halves(b)
    return contract(ah, bh, 1, 0) + (contract(ah, bl, 1, 0) + contract(al, bh, 1, 0))


LEVEL = 14.0


def gram_kernel(at_ref, f_ref, *refs):
    a_refs, b_refs = refs[:2], refs[2:6]
    gram_ref, root_ref, cross_ref, y_ref, t_ref = refs[6:]
    x, zl, core = (at_ref[i] for i in range(3))
    step = pl.program_id(0)
    half = y_ref.shape[-1] // 2
    per = LEAF // BLOCK
    leaves, order, wide = gram_ref.shape
    row = lax.broadcasted_iota(jnp.int32, (order, wide), 0)
    col = lax.broadcasted_iota(jnp.int32, (order, wide), 1)
    lane = lax.broadcasted_iota(jnp.int32, (1, wide), 1)

    @pl.when(step == 0)
    def _():
        for side, owner in ((0, core), (1, 1 - core)):
            lanes = pl.ds(pl.multiple_of(owner * half, half), half)
            for i in range(4):
                for j in range(2):
                    chip = lax.rem(x + 4 - i, 4) * 2 + lax.rem(zl + j, 2)
                    rows = pl.ds(pl.multiple_of(chip * 16, 16), 16)
                    y_ref[:per, rows, lanes] = a_refs[j][i, side]
                    y_ref[per:, rows, lanes] = b_refs[i][j, side]
        for leaf in range(leaves):
            y = y_ref[leaf * per : (leaf + 1) * per].reshape(LEAF, wide)
            t_ref[leaf] = y.T[:order]
            gram = contract(t_ref[leaf], y, 1, 0)
            gram_ref[leaf] = gram
            square = jnp.sum(jnp.where(row == col, gram, 0.0), axis=0, keepdims=True)
            root_ref[leaf] = jnp.sqrt(jnp.where(lane < order, square, 1.0))

    here = t_ref[step]
    there = y_ref[pl.ds((1 - step) * per, per)].reshape(LEAF, wide)
    hi, lo = halves(jnp.dot(f_ref[...], there, preferred_element_type=F32) * (1.0 / root_ref[1 - step]))
    cross = contract(here, hi, 1, 0) + contract(here, lo, 1, 0)
    square = jnp.sum(jnp.where(row == col, gram_ref[step], 0.0), axis=1, keepdims=True)
    cross = cross * lax.rsqrt(square)
    most = jnp.max(jnp.max(jnp.abs(cross), axis=0, keepdims=True), axis=1, keepdims=True)
    power = jnp.ceil(jnp.log2(jnp.maximum(most, 1e-30)))
    cross = jnp.where(col < order, cross * jnp.exp2(LEVEL - power), power)
    cross = jnp.round(cross).astype(jnp.int32).astype(jnp.int16)
    cross_ref[:, 0] = cross.reshape(cross_ref.shape[0], cross_ref.shape[2], wide)


def grams(at, front, mine, order, chips):
    half = mine[0].shape[-1]
    wide = 2 * half
    return pl.pallas_call(
        gram_kernel,
        grid_spec=pltpu.PrefetchScalarGridSpec(
            num_scalar_prefetch=1,
            grid=(2,),
            in_specs=[
                pl.BlockSpec((LEAF, LEAF), lambda i, at: (at[2] * 2 + i, 1 - i)),
            ]
            + [whole(piece) for piece in mine],
            out_specs=[
                pl.BlockSpec((2, order, wide), lambda i, at: (0, 0, 0)),
                pl.BlockSpec((2, 1, wide), lambda i, at: (0, 0, 0)),
                pl.BlockSpec((chips, 1, order // chips, wide), lambda i, at: (0, i, 0, 0)),
            ],
            scratch_shapes=[
                pltpu.VMEM((2 * LEAF // BLOCK, BLOCK, wide), BF),
                pltpu.VMEM((2, order, LEAF), BF),
            ],
        ),
        out_shape=[
            jax.ShapeDtypeStruct((2, order, wide), F32),
            jax.ShapeDtypeStruct((2, 1, wide), F32),
            jax.ShapeDtypeStruct((chips, 2, order // chips, wide), jnp.int16),
        ],
        compiler_params=params(52),
        cost_estimate=cost(2 * 8 * LEAF * wide * wide, 4 * LEAF * LEAF + 2 * leaves_bytes(wide)),
    )(at, front, *mine)


def leaves_bytes(wide):
    return 2 * LEAF * wide * 2


def eliminate(s, size):
    groups = size // 8
    shape = (8, 128)
    sub = lax.broadcasted_iota(jnp.int32, shape, 0)
    for g in range(groups):
        for rows in s:
            c = {
                (i, k): jnp.broadcast_to(rows[i][:, 8 * g + k : 8 * g + k + 1], shape)
                for i in range(g, groups)
                for k in range(8)
            }
            pivot = [jnp.broadcast_to(rows[g][k : k + 1, :], shape) for k in range(8)]
            d = {
                (i, k): jnp.broadcast_to(c[g, k][i : i + 1, :], shape)
                for i in range(8)
                for k in range(i, 8)
            }
            low = {}
            scaled = []
            for k in range(8):
                inverse = pl.reciprocal(d[k, k], approx=True)
                inverse = inverse * (2.0 - d[k, k] * inverse)
                scaled.append(pivot[k] * inverse)
                for i in range(k + 1, 8):
                    low[i, k] = d[k, i] * inverse
                    pivot[i] = pivot[i] - low[i, k] * pivot[k]
                    for m in range(i, 8):
                        d[i, m] = d[i, m] - low[i, k] * d[k, m]
            for m in reversed(range(8)):
                for k in range(m + 1, 8):
                    scaled[m] = scaled[m] - low[k, m] * scaled[k]
            for i in range(g + 1, groups):
                terms = [c[i, k] * scaled[k] for k in range(8)]
                while len(terms) > 1:
                    terms = [a + b for a, b in zip(terms[::2], terms[1::2])]
                rows[i] = rows[i] - terms[0]
            new = pivot[0]
            for k in range(1, 8):
                new = jnp.where(sub == k, pivot[k], new)
            rows[g] = new


def inverse_kernel(a_ref, after_ref, w_ref, x_ref, d_ref, *, first, last):
    del after_ref
    leaves, order, wide = w_ref.shape
    blocks = order // STEP
    w_ref[...] = a_ref[...]
    lane = lax.broadcasted_iota(jnp.int32, (STEP, 128), 1)
    sub = lax.broadcasted_iota(jnp.int32, (STEP, 128), 0)
    col = lax.broadcasted_iota(jnp.int32, (STEP, wide), 1)
    row = lax.broadcasted_iota(jnp.int32, (STEP, wide), 0)
    unit = (lane - STEP == sub).astype(F32)

    def spread(k, live):
        base = pl.multiple_of(k * STEP, STEP)
        inside = (col >= base) & (col < base + STEP)
        own = (col - base == row).astype(F32)
        rest = (col >= base + STEP) & live
        for leaf in range(leaves):
            w = w_ref[leaf, pl.ds(base, STEP), :]
            r = product3(x_ref[leaf], jnp.where(inside, own, w))
            w_ref[leaf, pl.ds(base, STEP), :] = jnp.where(live, r, w)
            hi, lo = halves(r)
            none = jnp.zeros_like(hi)
            left_hi, left_lo = jnp.where(rest, hi, none), jnp.where(rest, lo, none)
            left = jnp.concatenate([left_hi, left_hi, left_lo], axis=0)
            update = contract(left, jnp.concatenate([hi, lo, hi], axis=0), 0, 0)
            for i in range(1, blocks):
                rows = slice(i * STEP, (i + 1) * STEP)
                old = jnp.where(inside & live & (i > k), 0.0, w_ref[leaf, rows, :])
                w_ref[leaf, rows, :] = old - update[rows]

    start, tile = first * STEP, first * STEP // 128 * 128
    for leaf in range(leaves):
        d = w_ref[leaf, start : start + STEP, tile : tile + 128]
        d_ref[leaf] = pltpu.roll(d, 128 - STEP, 1) if start > tile else d
        x_ref[leaf] = jnp.zeros((STEP, STEP), F32)

    @pl.loop(first, last)
    def _(k):
        s = []
        for leaf in range(leaves):
            d = jnp.where(lane < STEP, d_ref[leaf], unit)
            s.append([d[8 * i : 8 * i + 8] for i in range(STEP // 8)])
        spread(jnp.maximum(k - 1, 0), k > first)
        eliminate(s, STEP)
        base = pl.multiple_of(k * STEP, STEP)
        after = pl.multiple_of(jnp.minimum(k + 1, blocks - 1) * STEP, STEP)
        tile = pl.multiple_of(lax.div(after, 128) * 128, 128)
        odd = after - tile > 0
        for leaf in range(leaves):
            d = jnp.concatenate(s[leaf], axis=0)
            diagonal = jnp.sum(jnp.where(lane == sub, d, 0.0), axis=1, keepdims=True)
            x = (d * lax.rsqrt(diagonal))[:, STEP:]
            x_ref[leaf] = x
            hi, lo = halves(product3(x, w_ref[leaf, pl.ds(base, STEP), pl.ds(tile, 128)]))
            left = jnp.concatenate([hi, hi, lo], axis=0)
            update = contract(left, jnp.concatenate([hi, lo, hi], axis=0), 0, 0)
            update = jnp.where(odd, update[STEP:], update[:STEP])
            d = w_ref[leaf, pl.ds(after, STEP), pl.ds(tile, 128)] - update
            d_ref[leaf] = jnp.where(odd, pltpu.roll(d, 128 - STEP, 1), d)

    spread(last - 1, True)
    if last < blocks:
        return
    for leaf in range(leaves):
        for i in range(blocks):
            rows = slice(i * STEP, (i + 1) * STEP)
            w_ref[leaf, rows, :] = jnp.where(col <= row + i * STEP, w_ref[leaf, rows, :], 0.0)


def factor_inverse(work, after, first, last):
    leaves = work.shape[0]
    return pl.pallas_call(
        functools.partial(inverse_kernel, first=first, last=last),
        grid=(1,),
        out_shape=jax.ShapeDtypeStruct(work.shape, F32),
        in_specs=[whole(work), pl.BlockSpec(memory_space=pl.ANY)],
        out_specs=whole(work),
        scratch_shapes=[
            pltpu.VMEM((leaves, STEP, STEP), F32),
            pltpu.VMEM((leaves, STEP, 128), F32),
        ],
        compiler_params=params(24),
        cost_estimate=cost((last - first) * 5.5e9, 8 * work.size),
    )(work, after)


def finish_kernel(at_ref, w_ref, root_ref, own_ref, cross_ref, keep_ref, send_ref):
    leaves, order, wide = w_ref.shape
    slabs = LEAF // BLOCK
    rows = order // cross_ref.shape[0]
    base = pl.multiple_of((at_ref[0] * 2 + at_ref[1]) * rows, 8)
    first = at_ref[2] == 0
    tall = own_ref.shape[1] // 2
    for leaf in range(leaves):
        hi, lo = halves(w_ref[leaf])
        own = own_ref[leaf]
        basis = (contract(own, hi, 1, 1) + contract(own, lo, 1, 1)) * math.sqrt(LEAF)
        parts = basis.reshape(slabs, 2, tall // slabs, order)
        low, high = parts[:, 0].reshape(tall, order), parts[:, 1].reshape(tall, order)
        keep_ref[leaf, :tall] = jnp.where(first, low, high)
        send_ref[leaf, :tall] = jnp.where(first, high, low)
        left = w_ref[leaf, pl.ds(base, rows), :] * root_ref[leaf]
        cross = cross_ref[:, leaf].astype(jnp.int32).astype(F32).reshape(order, wide)
        level = jnp.exp2(cross[:1, order : order + 1] - LEVEL)
        half_way, rest = halves(product3(left[:, :order], cross))
        hi, lo = halves(w_ref[1 - leaf] * root_ref[1 - leaf])
        core = contract(half_way, hi, 1, 1) + (contract(half_way, lo, 1, 1) + contract(rest, hi, 1, 1))
        core = core * level
        low, high = core[: rows // 2], core[rows // 2 :]
        keep_ref[leaf, tall:] = jnp.where(first, low, high)
        send_ref[leaf, tall:] = jnp.where(first, high, low)


def finish(at, inverse, root, own, cross):
    leaves, order, _ = inverse.shape
    rows = (own.shape[1] + order // cross.shape[0]) // 2
    part = jax.ShapeDtypeStruct((leaves, rows, order), F32)
    return pl.pallas_call(
        finish_kernel,
        grid=(1,),
        out_shape=[part, part],
        in_specs=[SMEM, whole(inverse), whole(root), whole(own), whole(cross)],
        out_specs=[whole(part)] * 2,
        compiler_params=params(24),
        cost_estimate=cost(2e9, 4 * (inverse.size + cross.size)),
    )(at, inverse, root, own, cross)


def local(parent_front, child_update, parent_test, child_test, child_map):
    y, zh = lax.axis_index("y"), lax.axis_index("zh")
    x, zl, core = lax.axis_index("x"), lax.axis_index("zl"), lax.axis_index("core")
    row_index = lax.axis_index(ROW)
    probes = parent_test.shape[1]
    half = 256
    chips = lax.axis_size(CHIP)
    own_blocks = parent_front.shape[0] // BLOCK
    kid_blocks = child_update.shape[1] // BLOCK
    swap = [(0, 1), (1, 0)]

    at = jnp.stack([x, zl, core]).astype(jnp.int32)
    kid_sent, kid_kept = probe(at, child_update, jnp.swapaxes(child_test, 1, 2), half)
    kid_sent = lax.ppermute(kid_sent, "core", swap)
    own_sent, own_kept = probe(at, parent_front[None], parent_test.T[None], half)
    own_sent = lax.ppermute(own_sent, "core", swap)
    kid_part, kid_rest = pack(at, kid_kept, kid_sent, chips)
    kid_share = lax.all_to_all(kid_part, CHIP, 0, 0, tiled=True)
    own_part, own_rest = pack(at, own_kept, own_sent, chips)

    kid_share, own_part = lax.optimization_barrier((kid_share, own_part))
    kids = sum_shares(at, kid_share, kid_rest, BF).reshape(2, kid_blocks, -1, half)
    pair = ring_pieces(kids, "zh")
    pair[1], own_part = lax.optimization_barrier((pair[1], own_part))
    pair = jnp.stack(pair)
    own_share = lax.all_to_all(own_part, CHIP, 0, 0, tiled=True)
    reach = [(0, 1), (0, 2), (1, 0), (1, 2), (2, 1), (2, 3), (3, 1), (3, 2)]
    kid_pieces = [pair] + [
        lax.ppermute(pair, "y", [(i, j) for i, j in reach if (j - i) % 4 == by])
        for by in range(1, 4)
    ]

    targets = row_index * own_blocks + jnp.arange(own_blocks, dtype=jnp.int32)
    hit = child_map[:, None, :] == targets[None, :, None]
    there = jnp.any(hit, axis=2).astype(jnp.int32)
    source = jnp.sum(jnp.where(hit, jnp.arange(child_map.shape[1], dtype=jnp.int32), 0), axis=2)
    owner, place = source // kid_blocks, source % kid_blocks
    ring = (y - owner // 2) % 4
    pair_of = (zh - owner % 2) % 2
    origin = jnp.stack([ring, pair_of, place, there], axis=1).astype(jnp.int32)
    keep, send = extend_add(at, origin, own_share, own_rest, kid_pieces)
    came = lax.ppermute(send, "core", swap)

    per = LEAF // BLOCK
    first = jnp.stack([keep[:per], came[:per]])
    second = jnp.stack([keep[per:], came[per:]])
    firsts, seconds = two_way_pieces(first, second, "x", "zl")
    gram, root, cross = grams(at, parent_front, firsts + seconds, probes, chips)

    own_rows = jnp.where(
        core == 0,
        jnp.concatenate([keep, came], axis=2),
        jnp.concatenate([came, keep], axis=2),
    ).reshape(2, -1, 2 * half)

    cross = lax.all_to_all(cross, CHIP, 0, 0, tiled=True)
    ready = lax.dynamic_slice_in_dim(cross, row_index, 1, 0)
    work = factor_inverse(gram, own_rows, 0, 3)
    cross = lax.all_to_all(jnp.broadcast_to(ready, (chips, *ready.shape[1:])), CHIP, 0, 0, tiled=True)
    inverse = factor_inverse(work, ready[0, 0, :8, :128].astype(F32), 3, probes // STEP)
    keep, send = finish(at, inverse, root, own_rows, cross)
    came = lax.ppermute(send, "core", swap)
    both = jnp.where(core == 0, jnp.concatenate([keep, came]), jnp.concatenate([came, keep]))
    tall = own_rows.shape[1] // 2
    leaf_basis = both[:, :tall].astype(BF).reshape(own_blocks, -1, probes)
    return (leaf_basis, both[:, tall:])


def solution(mesh):
    split = Mesh(mesh.devices.reshape(4, 2, 4, 2, 2), ("y", "zh", "x", "zl", "core"))
    placed = (P(ROW, COL), P(None, ROW, COL), P(COL, None), P(None, COL, None), P())
    return jax.shard_map(
        local,
        mesh=split,
        in_specs=placed,
        out_specs=(P(ROW, COL, None), P(ROW, COL, None)),
        check_vma=False,
    )
```

```python
import functools
import math

import jax
import jax.numpy as jnp
from jax import lax
from jax.experimental import pallas as pl
from jax.experimental.pallas import tpu as pltpu
from jax.sharding import Mesh
from jax.sharding import PartitionSpec as P

LEAF = 896
BLOCK = 128
ROW = ("y", "zh")
CHIP = ("x", "zl")
COL = ("x", "zl", "core")
F32 = jnp.float32
BF = jnp.bfloat16
SMEM = pl.BlockSpec(memory_space=pltpu.SMEM)
STEP = 64


def whole(array):
    return pl.BlockSpec(array.shape, lambda *_: (0,) * len(array.shape))


def params(mib):
    return pltpu.CompilerParams(vmem_limit_bytes=mib << 20)


def cost(flops, nbytes):
    return pl.CostEstimate(flops=int(flops), bytes_accessed=int(nbytes), transcendentals=0)


def probe_kernel(at_ref, a_ref, b_ref, sent_ref, kept_ref):
    total = contract(a_ref[0], b_ref[0], 1, 1)
    half = sent_ref.shape[2]
    low = total[:, :half]
    pad = jnp.zeros((total.shape[0], 2 * half - total.shape[1]), F32)
    high = jnp.concatenate([total[:, half:], pad], axis=1)
    first = at_ref[2] == 0
    kept_ref[0] = jnp.where(first, low, high)
    sent_ref[0] = jnp.where(first, high, low)


def probe(at, a, b, half):
    count, rows, depth = a.shape
    probes = b.shape[1]
    part = jax.ShapeDtypeStruct((count, rows, half), F32)
    return pl.pallas_call(
        probe_kernel,
        grid=(count, rows // LEAF),
        out_shape=[part, part],
        in_specs=[
            SMEM,
            pl.BlockSpec((1, LEAF, depth), lambda k, i: (k, i, 0)),
            pl.BlockSpec((1, probes, depth), lambda k, i: (k, 0, 0)),
        ],
        out_specs=[pl.BlockSpec((1, LEAF, half), lambda k, i: (k, i, 0))] * 2,
        compiler_params=params(40),
        cost_estimate=cost(4 * count * rows * depth * half, 2 * a.size + 8 * count * rows * half),
    )(at, a, b)


def pack_kernel(at_ref, a_ref, b_ref, o_ref, own_ref, sum_ref):
    total = a_ref[0] + b_ref[0]
    sum_ref[...] = total
    chips, blocks, rows, _ = o_ref.shape
    chip_here = at_ref[0] * 2 + at_ref[1]
    for block in range(blocks):
        for chip in range(chips):
            start = (block * chips + chip) * rows
            o_ref[chip, block] = total[start : start + rows].astype(BF)
        own = pl.multiple_of((block * chips + chip_here) * rows, rows)
        own_ref[block] = sum_ref[pl.ds(own, rows), :]


def pack(at, kept, received, chips):
    count, rows, half = kept.shape
    per = rows // LEAF
    blocks = LEAF // BLOCK
    slab = BLOCK // chips
    whole = count * rows // BLOCK
    return pl.pallas_call(
        pack_kernel,
        grid=(count, per),
        out_shape=[
            jax.ShapeDtypeStruct((chips, whole, slab, half), BF),
            jax.ShapeDtypeStruct((whole, slab, half), F32),
        ],
        in_specs=[
            SMEM,
            pl.BlockSpec((1, LEAF, half), lambda k, i: (k, i, 0)),
            pl.BlockSpec((1, LEAF, half), lambda k, i: (k, i, 0)),
        ],
        out_specs=[
            pl.BlockSpec((chips, blocks, slab, half), lambda k, i: (0, k * per + i, 0, 0)),
            pl.BlockSpec((blocks, slab, half), lambda k, i: (k * per + i, 0, 0)),
        ],
        scratch_shapes=[pltpu.VMEM((LEAF, half), F32)],
        compiler_params=params(24),
        cost_estimate=cost(kept.size, 10 * kept.size),
    )(at, kept, received)


def shift(value, axis, by):
    size = lax.axis_size(axis)
    return lax.ppermute(value, axis, [(i, (i + by) % size) for i in range(size)])


def ring_pieces(value, axis):
    return [value] + [shift(value, axis, by) for by in range(1, lax.axis_size(axis))]


def two_way_pieces(first, second, big, small):
    first_ring = jnp.stack(ring_pieces(first, big))
    second_pair = jnp.stack(ring_pieces(second, small))
    return ring_pieces(first_ring, small), ring_pieces(second_pair, big)


def sum_of(shares_ref, own, here, at):
    for chip in range(shares_ref.shape[0]):
        own += jnp.where(here != chip, shares_ref[(chip, *at)].astype(F32), 0.0)
    return own


def sum_kernel(at_ref, k_ref, own_ref, o_ref):
    here = at_ref[0] * 2 + at_ref[1]
    for block in range(o_ref.shape[0]):
        o_ref[block] = sum_of(k_ref, own_ref[block], here, (block,)).astype(o_ref.dtype)


def sum_shares(at, shares, own, dtype):
    chips, blocks, slab, half = shares.shape
    step = LEAF // BLOCK
    return pl.pallas_call(
        sum_kernel,
        grid=(blocks // step,),
        out_shape=jax.ShapeDtypeStruct(shares.shape[1:], dtype),
        in_specs=[
            SMEM,
            pl.BlockSpec((chips, step, slab, half), lambda i: (0, i, 0, 0)),
            pl.BlockSpec((step, slab, half), lambda i: (i, 0, 0)),
        ],
        out_specs=pl.BlockSpec((step, slab, half), lambda i: (i, 0, 0)),
        compiler_params=params(16),
        cost_estimate=cost(shares.size, 2 * shares.size),
    )(at, shares, own)


def extend_kernel(at_ref, from_ref, p_ref, own_ref, *refs):
    *kid_refs, keep_ref, send_ref, all_ref = refs
    here = at_ref[0] * 2 + at_ref[1]
    core = at_ref[2]
    step = pl.program_id(0)
    blocks = own_ref.shape[0]
    for block in range(blocks):
        total = sum_of(p_ref, own_ref[block], here, (block,))
        target = step * blocks + block
        for kid in range(2):
            ring, pair, place, there = (from_ref[kid, part, target] for part in range(4))
            for i, ref in enumerate(kid_refs):
                hit = (there > 0) & (ring == i)
                total += jnp.where(hit, ref[pair, kid, place].astype(F32), 0.0)
        all_ref[target] = total.astype(BF)

    @pl.when(step == pl.num_programs(0) - 1)
    def _():
        count = keep_ref.shape[0]
        keep_ref[...] = all_ref[pl.ds(core * count, count)]
        send_ref[...] = all_ref[pl.ds((1 - core) * count, count)]


def extend_add(at, source, parent, own, kids):
    chips, blocks, slab, half = parent.shape
    step = LEAF // BLOCK
    pair = jax.ShapeDtypeStruct((blocks // 2, slab, half), BF)
    return pl.pallas_call(
        extend_kernel,
        grid=(blocks // step,),
        out_shape=[pair, pair],
        in_specs=[
            SMEM,
            SMEM,
            pl.BlockSpec((chips, step, slab, half), lambda i: (0, i, 0, 0)),
            pl.BlockSpec((step, slab, half), lambda i: (i, 0, 0)),
        ]
        + [whole(piece) for piece in kids],
        out_specs=[whole(pair)] * 2,
        scratch_shapes=[pltpu.VMEM(parent.shape[1:], BF)],
        compiler_params=params(24),
        cost_estimate=cost(parent.size, 6 * parent.size),
    )(at, source, parent, own, *kids)


def halves(x):
    hi = x.astype(BF)
    return hi, (x - hi.astype(F32)).astype(BF)


def contract(a, b, left, right):
    return lax.dot_general(a, b, (((left,), (right,)), ((), ())), preferred_element_type=F32)


def product3(a, b):
    ah, al = halves(a)
    bh, bl = halves(b)
    return contract(ah, bh, 1, 0) + (contract(ah, bl, 1, 0) + contract(al, bh, 1, 0))


LEVEL = 14.0


def gram_kernel(at_ref, f_ref, *refs):
    a_refs, b_refs = refs[:2], refs[2:6]
    gram_ref, root_ref, cross_ref, y_ref, t_ref = refs[6:]
    x, zl, core = (at_ref[i] for i in range(3))
    step = pl.program_id(0)
    half = y_ref.shape[-1] // 2
    per = LEAF // BLOCK
    leaves, order, wide = gram_ref.shape
    row = lax.broadcasted_iota(jnp.int32, (order, wide), 0)
    col = lax.broadcasted_iota(jnp.int32, (order, wide), 1)
    lane = lax.broadcasted_iota(jnp.int32, (1, wide), 1)

    @pl.when(step == 0)
    def _():
        for side, owner in ((0, core), (1, 1 - core)):
            lanes = pl.ds(pl.multiple_of(owner * half, half), half)
            for i in range(4):
                for j in range(2):
                    chip = lax.rem(x + 4 - i, 4) * 2 + lax.rem(zl + j, 2)
                    rows = pl.ds(pl.multiple_of(chip * 16, 16), 16)
                    y_ref[:per, rows, lanes] = a_refs[j][i, side]
                    y_ref[per:, rows, lanes] = b_refs[i][j, side]
        for leaf in range(leaves):
            y = y_ref[leaf * per : (leaf + 1) * per].reshape(LEAF, wide)
            t_ref[leaf] = y.T[:order]
            gram = contract(t_ref[leaf], y, 1, 0)
            gram_ref[leaf] = gram
            square = jnp.sum(jnp.where(row == col, gram, 0.0), axis=0, keepdims=True)
            root_ref[leaf] = jnp.sqrt(jnp.where(lane < order, square, 1.0))

    here = t_ref[step]
    there = y_ref[pl.ds((1 - step) * per, per)].reshape(LEAF, wide)
    hi, lo = halves(jnp.dot(f_ref[...], there, preferred_element_type=F32) * (1.0 / root_ref[1 - step]))
    cross = contract(here, hi, 1, 0) + contract(here, lo, 1, 0)
    square = jnp.sum(jnp.where(row == col, gram_ref[step], 0.0), axis=1, keepdims=True)
    cross = cross * lax.rsqrt(square)
    most = jnp.max(jnp.max(jnp.abs(cross), axis=0, keepdims=True), axis=1, keepdims=True)
    power = jnp.ceil(jnp.log2(jnp.maximum(most, 1e-30)))
    cross = jnp.where(col < order, cross * jnp.exp2(LEVEL - power), power)
    cross = jnp.round(cross).astype(jnp.int32).astype(jnp.int16)
    cross_ref[:, 0] = cross.reshape(cross_ref.shape[0], cross_ref.shape[2], wide)


def grams(at, front, mine, order, chips):
    half = mine[0].shape[-1]
    wide = 2 * half
    return pl.pallas_call(
        gram_kernel,
        grid_spec=pltpu.PrefetchScalarGridSpec(
            num_scalar_prefetch=1,
            grid=(2,),
            in_specs=[
                pl.BlockSpec((LEAF, LEAF), lambda i, at: (at[2] * 2 + i, 1 - i)),
            ]
            + [whole(piece) for piece in mine],
            out_specs=[
                pl.BlockSpec((2, order, wide), lambda i, at: (0, 0, 0)),
                pl.BlockSpec((2, 1, wide), lambda i, at: (0, 0, 0)),
                pl.BlockSpec((chips, 1, order // chips, wide), lambda i, at: (0, i, 0, 0)),
            ],
            scratch_shapes=[
                pltpu.VMEM((2 * LEAF // BLOCK, BLOCK, wide), BF),
                pltpu.VMEM((2, order, LEAF), BF),
            ],
        ),
        out_shape=[
            jax.ShapeDtypeStruct((2, order, wide), F32),
            jax.ShapeDtypeStruct((2, 1, wide), F32),
            jax.ShapeDtypeStruct((chips, 2, order // chips, wide), jnp.int16),
        ],
        compiler_params=params(52),
        cost_estimate=cost(2 * 8 * LEAF * wide * wide, 4 * LEAF * LEAF + 2 * leaves_bytes(wide)),
    )(at, front, *mine)


def leaves_bytes(wide):
    return 2 * LEAF * wide * 2


def eliminate(s, size):
    groups = size // 8
    shape = (8, 128)
    sub = lax.broadcasted_iota(jnp.int32, shape, 0)
    for g in range(groups):
        for rows in s:
            c = {
                (i, k): jnp.broadcast_to(rows[i][:, 8 * g + k : 8 * g + k + 1], shape)
                for i in range(g, groups)
                for k in range(8)
            }
            pivot = [jnp.broadcast_to(rows[g][k : k + 1, :], shape) for k in range(8)]
            d = {
                (i, k): jnp.broadcast_to(c[g, k][i : i + 1, :], shape)
                for i in range(8)
                for k in range(i, 8)
            }
            low = {}
            scaled = []
            for k in range(8):
                inverse = pl.reciprocal(d[k, k], approx=True)
                inverse = inverse * (2.0 - d[k, k] * inverse)
                scaled.append(pivot[k] * inverse)
                for i in range(k + 1, 8):
                    low[i, k] = d[k, i] * inverse
                    pivot[i] = pivot[i] - low[i, k] * pivot[k]
                    for m in range(i, 8):
                        d[i, m] = d[i, m] - low[i, k] * d[k, m]
            for m in reversed(range(8)):
                for k in range(m + 1, 8):
                    scaled[m] = scaled[m] - low[k, m] * scaled[k]
            for i in range(g + 1, groups):
                terms = [c[i, k] * scaled[k] for k in range(8)]
                while len(terms) > 1:
                    terms = [a + b for a, b in zip(terms[::2], terms[1::2])]
                rows[i] = rows[i] - terms[0]
            new = pivot[0]
            for k in range(1, 8):
                new = jnp.where(sub == k, pivot[k], new)
            rows[g] = new


def inverse_kernel(a_ref, after_ref, w_ref, x_ref, d_ref, *, first, last):
    del after_ref
    leaves, order, wide = w_ref.shape
    blocks = order // STEP
    w_ref[...] = a_ref[...]
    lane = lax.broadcasted_iota(jnp.int32, (STEP, 128), 1)
    sub = lax.broadcasted_iota(jnp.int32, (STEP, 128), 0)
    col = lax.broadcasted_iota(jnp.int32, (STEP, wide), 1)
    row = lax.broadcasted_iota(jnp.int32, (STEP, wide), 0)
    unit = (lane - STEP == sub).astype(F32)

    def spread(k, live):
        base = pl.multiple_of(k * STEP, STEP)
        inside = (col >= base) & (col < base + STEP)
        own = (col - base == row).astype(F32)
        rest = (col >= base + STEP) & live
        for leaf in range(leaves):
            w = w_ref[leaf, pl.ds(base, STEP), :]
            r = product3(x_ref[leaf], jnp.where(inside, own, w))
            w_ref[leaf, pl.ds(base, STEP), :] = jnp.where(live, r, w)
            hi, lo = halves(r)
            none = jnp.zeros_like(hi)
            left_hi, left_lo = jnp.where(rest, hi, none), jnp.where(rest, lo, none)
            left = jnp.concatenate([left_hi, left_hi, left_lo], axis=0)
            update = contract(left, jnp.concatenate([hi, lo, hi], axis=0), 0, 0)
            for i in range(1, blocks):
                rows = slice(i * STEP, (i + 1) * STEP)
                old = jnp.where(inside & live & (i > k), 0.0, w_ref[leaf, rows, :])
                w_ref[leaf, rows, :] = old - update[rows]

    start, tile = first * STEP, first * STEP // 128 * 128
    for leaf in range(leaves):
        d = w_ref[leaf, start : start + STEP, tile : tile + 128]
        d_ref[leaf] = pltpu.roll(d, 128 - STEP, 1) if start > tile else d
        x_ref[leaf] = jnp.zeros((STEP, STEP), F32)

    @pl.loop(first, last)
    def _(k):
        s = []
        for leaf in range(leaves):
            d = jnp.where(lane < STEP, d_ref[leaf], unit)
            s.append([d[8 * i : 8 * i + 8] for i in range(STEP // 8)])
        spread(jnp.maximum(k - 1, 0), k > first)
        eliminate(s, STEP)
        base = pl.multiple_of(k * STEP, STEP)
        after = pl.multiple_of(jnp.minimum(k + 1, blocks - 1) * STEP, STEP)
        tile = pl.multiple_of(lax.div(after, 128) * 128, 128)
        odd = after - tile > 0
        for leaf in range(leaves):
            d = jnp.concatenate(s[leaf], axis=0)
            diagonal = jnp.sum(jnp.where(lane == sub, d, 0.0), axis=1, keepdims=True)
            x = (d * lax.rsqrt(diagonal))[:, STEP:]
            x_ref[leaf] = x
            hi, lo = halves(product3(x, w_ref[leaf, pl.ds(base, STEP), pl.ds(tile, 128)]))
            left = jnp.concatenate([hi, hi, lo], axis=0)
            update = contract(left, jnp.concatenate([hi, lo, hi], axis=0), 0, 0)
            update = jnp.where(odd, update[STEP:], update[:STEP])
            d = w_ref[leaf, pl.ds(after, STEP), pl.ds(tile, 128)] - update
            d_ref[leaf] = jnp.where(odd, pltpu.roll(d, 128 - STEP, 1), d)

    spread(last - 1, True)
    if last < blocks:
        return
    for leaf in range(leaves):
        for i in range(blocks):
            rows = slice(i * STEP, (i + 1) * STEP)
            w_ref[leaf, rows, :] = jnp.where(col <= row + i * STEP, w_ref[leaf, rows, :], 0.0)


def factor_inverse(work, after, first, last):
    leaves = work.shape[0]
    return pl.pallas_call(
        functools.partial(inverse_kernel, first=first, last=last),
        grid=(1,),
        out_shape=jax.ShapeDtypeStruct(work.shape, F32),
        in_specs=[whole(work), pl.BlockSpec(memory_space=pl.ANY)],
        out_specs=whole(work),
        scratch_shapes=[
            pltpu.VMEM((leaves, STEP, STEP), F32),
            pltpu.VMEM((leaves, STEP, 128), F32),
        ],
        compiler_params=params(24),
        cost_estimate=cost((last - first) * 5.5e9, 8 * work.size),
    )(work, after)


def finish_kernel(at_ref, w_ref, root_ref, own_ref, cross_ref, keep_ref, send_ref):
    leaves, order, wide = w_ref.shape
    slabs = LEAF // BLOCK
    rows = order // cross_ref.shape[0]
    base = pl.multiple_of((at_ref[0] * 2 + at_ref[1]) * rows, 8)
    first = at_ref[2] == 0
    tall = own_ref.shape[1] // 2
    for leaf in range(leaves):
        hi, lo = halves(w_ref[leaf])
        own = own_ref[leaf]
        basis = (contract(own, hi, 1, 1) + contract(own, lo, 1, 1)) * math.sqrt(LEAF)
        parts = basis.reshape(slabs, 2, tall // slabs, order)
        low, high = parts[:, 0].reshape(tall, order), parts[:, 1].reshape(tall, order)
        keep_ref[leaf, :tall] = jnp.where(first, low, high)
        send_ref[leaf, :tall] = jnp.where(first, high, low)
        left = w_ref[leaf, pl.ds(base, rows), :] * root_ref[leaf]
        cross = cross_ref[:, leaf].astype(jnp.int32).astype(F32).reshape(order, wide)
        level = jnp.exp2(cross[:1, order : order + 1] - LEVEL)
        half_way, rest = halves(product3(left[:, :order], cross))
        hi, lo = halves(w_ref[1 - leaf] * root_ref[1 - leaf])
        core = contract(half_way, hi, 1, 1) + (contract(half_way, lo, 1, 1) + contract(rest, hi, 1, 1))
        core = core * level
        low, high = core[: rows // 2], core[rows // 2 :]
        keep_ref[leaf, tall:] = jnp.where(first, low, high)
        send_ref[leaf, tall:] = jnp.where(first, high, low)


def finish(at, inverse, root, own, cross):
    leaves, order, _ = inverse.shape
    rows = (own.shape[1] + order // cross.shape[0]) // 2
    part = jax.ShapeDtypeStruct((leaves, rows, order), F32)
    return pl.pallas_call(
        finish_kernel,
        grid=(1,),
        out_shape=[part, part],
        in_specs=[SMEM, whole(inverse), whole(root), whole(own), whole(cross)],
        out_specs=[whole(part)] * 2,
        compiler_params=params(56),
        cost_estimate=cost(2e9, 4 * (inverse.size + cross.size)),
    )(at, inverse, root, own, cross)


def local(parent_front, child_update, parent_test, child_test, child_map):
    y, zh = lax.axis_index("y"), lax.axis_index("zh")
    x, zl, core = lax.axis_index("x"), lax.axis_index("zl"), lax.axis_index("core")
    row_index = lax.axis_index(ROW)
    probes = parent_test.shape[1]
    half = 256
    chips = lax.axis_size(CHIP)
    own_blocks = parent_front.shape[0] // BLOCK
    kid_blocks = child_update.shape[1] // BLOCK
    swap = [(0, 1), (1, 0)]

    at = jnp.stack([x, zl, core]).astype(jnp.int32)
    kid_sent, kid_kept = probe(at, child_update, jnp.swapaxes(child_test, 1, 2), half)
    kid_sent = lax.ppermute(kid_sent, "core", swap)
    own_sent, own_kept = probe(at, parent_front[None], parent_test.T[None], half)
    own_sent = lax.ppermute(own_sent, "core", swap)
    kid_part, kid_rest = pack(at, kid_kept, kid_sent, chips)
    kid_share = lax.all_to_all(kid_part, CHIP, 0, 0, tiled=True)
    own_part, own_rest = pack(at, own_kept, own_sent, chips)

    kids = sum_shares(at, kid_share, kid_rest, BF).reshape(2, kid_blocks, -1, half)
    pair = ring_pieces(kids, "zh")
    pair[1], own_part = lax.optimization_barrier((pair[1], own_part))
    pair = jnp.stack(pair)
    own_share = lax.all_to_all(own_part, CHIP, 0, 0, tiled=True)
    reach = [(0, 1), (0, 2), (1, 0), (1, 2), (2, 1), (2, 3), (3, 1), (3, 2)]
    kid_pieces = [pair] + [
        lax.ppermute(pair, "y", [(i, j) for i, j in reach if (j - i) % 4 == by])
        for by in range(1, 4)
    ]

    targets = row_index * own_blocks + jnp.arange(own_blocks, dtype=jnp.int32)
    hit = child_map[:, None, :] == targets[None, :, None]
    there = jnp.any(hit, axis=2).astype(jnp.int32)
    source = jnp.sum(jnp.where(hit, jnp.arange(child_map.shape[1], dtype=jnp.int32), 0), axis=2)
    owner, place = source // kid_blocks, source % kid_blocks
    ring = (y - owner // 2) % 4
    pair_of = (zh - owner % 2) % 2
    origin = jnp.stack([ring, pair_of, place, there], axis=1).astype(jnp.int32)
    keep, send = extend_add(at, origin, own_share, own_rest, kid_pieces)
    came = lax.ppermute(send, "core", swap)

    per = LEAF // BLOCK
    first = jnp.stack([keep[:per], came[:per]])
    second = jnp.stack([keep[per:], came[per:]])
    firsts, seconds = two_way_pieces(first, second, "x", "zl")
    gram, root, cross = grams(at, parent_front, firsts + seconds, probes, chips)

    own_rows = jnp.where(
        core == 0,
        jnp.concatenate([keep, came], axis=2),
        jnp.concatenate([came, keep], axis=2),
    ).reshape(2, -1, 2 * half)

    cross = lax.all_to_all(cross, CHIP, 0, 0, tiled=True)
    ready = lax.dynamic_slice_in_dim(cross, row_index, 1, 0)
    work = factor_inverse(gram, own_rows, 0, 3)
    cross = lax.all_to_all(jnp.broadcast_to(ready, (chips, *ready.shape[1:])), CHIP, 0, 0, tiled=True)
    inverse = factor_inverse(work, ready[0, 0, :8, :128].astype(F32), 3, probes // STEP)
    keep, send = finish(at, inverse, root, own_rows, cross)
    came = lax.ppermute(send, "core", swap)
    both = jnp.where(core == 0, jnp.concatenate([keep, came]), jnp.concatenate([came, keep]))
    tall = own_rows.shape[1] // 2
    leaf_basis = both[:, :tall].astype(BF).reshape(own_blocks, -1, probes)
    return (leaf_basis, both[:, tall:])


def solution(mesh):
    split = Mesh(mesh.devices.reshape(4, 2, 4, 2, 2), ("y", "zh", "x", "zl", "core"))
    placed = (P(ROW, COL), P(None, ROW, COL), P(COL, None), P(None, COL, None), P())
    return jax.shard_map(
        local,
        mesh=split,
        in_specs=placed,
        out_specs=(P(ROW, COL, None), P(ROW, COL, None)),
        check_vma=False,
    )
```
